1024 devices in a mesh: gx: 64 (over z, y), gy: 16 (over x, core).
Axes of the slice: x: 8, y: 8, z: 8, core: 2. Of those that a mesh axis runs over, the one named last changes fastest.
Arguments:
- coarse_state: float32 [5, 2, 4096, 2048], P(None, None, 'gx', 'gy'), as said below
- fine_state: float32 [64, 16, 8, 5, 4, 256], P('gx', 'gy'), as said below
- source_rows: int32 [64, 16, 8], P(None, 'gy'), may hold values from 0 to 63, as said below
- tile_ids: int32 [64, 16, 8], P(None, 'gy'), may hold values from 17 to 110, as said below
Outputs:
- coarse_out: float32 [5, 2, 4096, 2048], P(None, None, 'gx', 'gy')
- fine_out: float32 [64, 16, 8, 5, 4, 256], P('gx', 'gy')
The draws below stay inside these ranges and needn't reach their ends.
Inputs may be any that keep to these rules, and one draw needn't show every extreme that they name: `coarse_state`: fields are density, the three momenta and energy of a gas of adiabatic index 1.4; density and pressure lie between 0.5 and 2 and each velocity component between -0.5 and 0.5. `fine_state`: as for coarse_state. `source_rows`: entry [o, j, r] is the gx index of the device in grid column j whose block the fine box r of device (o, j) refines. Among the 8 entries of one device no value appears more than 1 times, and some value appears exactly 1 times. `tile_ids`: tile t covers the 8 x 8 coarse cells from row (t // 16) * 8 and column (t % 16) * 8 of the source device's block. No tile lies in the outermost cycle of tiles of a block (1 <= t // 16 <= 6 and 1 <= t % 16 <= 14), and no pair of source and tile occurs twice in one grid column.
All inputs are finite; a program needn't handle non-finite values.
Results may differ from the reference program's by a relative error of at most 0.0003.
Values sent between devices are 32-bit elements; how exact they have to be, the bound alone decides.
A program may use at most 64 MiB of HBM per device.

```python
import jax
import jax.numpy as jnp
from jax import lax

NF = 5
TB = 8
CZ = 2
CX = 64
CY = 128
R = 8
NX = 4096
NY = 2048
TX = 8
TY = 16
FZ = 4
FB = 16
N_GX = 64
N_GY = 16


HEAT_RATIO = 1.4


def gas_cells(key, out_shape, field_axis, log_share, common_share):
    subkeys = jax.random.split(key, 6)

    def positive(subkey):
        uniform_draw = jax.random.uniform(subkey, out_shape, jnp.float32)
        return log_share * (0.5 * 4.0 ** uniform_draw) + (1.0 - log_share) * (0.5 + 1.5 * uniform_draw)
    density = positive(subkeys[0])
    pressure = positive(subkeys[1])
    common = jax.random.uniform(subkeys[5], (3,), jnp.float32, -1.0, 1.0)
    velocity = [0.5 * ((1.0 - common_share) * jax.random.uniform(subkeys[2 + axis_id], out_shape, jnp.float32, -1.0, 1.0) + common_share * common[axis_id]) for axis_id in range(3)]
    energy = pressure / (HEAT_RATIO - 1.0) + 0.5 * density * (velocity[0] ** 2 + velocity[1] ** 2 + velocity[2] ** 2)
    fields = [density, density * velocity[0], density * velocity[1], density * velocity[2], energy]
    return jnp.stack(fields, axis=field_axis)


def knapsack(key):
    subkeys = jax.random.split(key, 3)
    centers = jax.random.randint(subkeys[0], (N_GY,), 0, N_GX)
    orders = jax.vmap(lambda subkey: jax.random.permutation(subkey, N_GX))(jax.random.split(subkeys[1], N_GY))
    starts = centers[:, None] + orders // 4
    offsets = jnp.arange(R, dtype=jnp.int32) % N_GX
    rows_all = (starts[:, :, None] + offsets[None, None, :]) % N_GX
    inner_count = (TX - 2) * (TY - 2)
    shuffles = jax.vmap(lambda subkey: jax.random.permutation(subkey, inner_count))(jax.random.split(subkeys[2], N_GY * N_GX)).reshape(N_GY, N_GX, inner_count)

    def assign(column_rows, column_shuffles):
        flat_rows = column_rows.reshape(-1)
        onehot = (flat_rows[:, None] == jnp.arange(N_GX, dtype=jnp.int32)[None, :]).astype(jnp.int32)
        before = jnp.cumsum(onehot, axis=0) - onehot
        rank_in = jnp.sum(before * onehot, axis=1)
        chosen = column_shuffles[flat_rows, rank_in]
        return (1 + chosen // (TY - 2)) * TY + 1 + chosen % (TY - 2)
    tile_all = jax.vmap(assign)(rows_all, shuffles).reshape(N_GY, N_GX, R)
    return (jnp.transpose(rows_all, (1, 0, 2)).astype(jnp.int32), jnp.transpose(tile_all, (1, 0, 2)).astype(jnp.int32))


def draw_coarse_state(key, part):
    key = jax.random.fold_in(key, 5)
    return gas_cells(key, (CZ, NX, NY), 0, 0.0, 0.0)


def draw_fine_state(key, part):
    key = jax.random.fold_in(key, 6)
    return gas_cells(key, (N_GX, N_GY, R, FZ, FB * FB), 3, 0.0, 0.0)


def draw_source_rows(key, part):
    shared = knapsack(key)
    key = jax.random.fold_in(key, 7)
    return shared[0]


def draw_tile_ids(key, part):
    shared = knapsack(key)
    key = jax.random.fold_in(key, 8)
    return shared[1]


def setup_inputs(seed: int = 0) -> dict:
    splits = jax.random.split(jax.random.key(seed), 5)
    return {
        "coarse_state": draw_coarse_state(jax.random.fold_in(splits[4], 71), 0),
        "fine_state": draw_fine_state(jax.random.fold_in(splits[4], 71), 0),
        "source_rows": draw_source_rows(jax.random.fold_in(splits[4], 71), 0),
        "tile_ids": draw_tile_ids(jax.random.fold_in(splits[4], 71), 0),
    }


HEAT_RATIO = 1.4
STEP_RATIO = 0.05

def primitives(conserved):
    density = conserved[0]
    velocity = conserved[1:4] / density
    kinetic = 0.5 * lax.optimization_barrier(jnp.sum(conserved[1:4] * velocity, axis=0))
    pressure = (HEAT_RATIO - 1.0) * (conserved[4] - kinetic)
    sound_speed = jnp.sqrt(HEAT_RATIO * pressure / density)
    return (velocity, pressure, sound_speed)

def directed(conserved, velocity, pressure, sound_speed, axis_id):
    normal_vel = velocity[axis_id]
    cell_flux = conserved * normal_vel[None]
    cell_flux = cell_flux.at[1 + axis_id].add(pressure)
    cell_flux = cell_flux.at[4].add(pressure * normal_vel)
    return (cell_flux, jnp.abs(normal_vel) + sound_speed)

def edge_terms(edge_cells, axis_id):
    velocity, pressure, sound_speed = primitives(edge_cells)
    return directed(edge_cells, velocity, pressure, sound_speed, axis_id)

def rusanov(left_flux, left_speed, left_cells, right_flux, right_speed, right_cells):
    return 0.5 * (left_flux + right_flux) - 0.5 * jnp.maximum(left_speed, right_speed)[None] * (right_cells - left_cells)

def advance(conserved, x_lower, x_upper, y_lower, y_upper):
    velocity, pressure, sound_speed = primitives(conserved)
    flux_z, speed_z = directed(conserved, velocity, pressure, sound_speed, 0)
    flux_x, speed_x = directed(conserved, velocity, pressure, sound_speed, 1)
    flux_y, speed_y = directed(conserved, velocity, pressure, sound_speed, 2)
    low_flux, low_speed = edge_terms(x_lower, 1)
    high_flux, high_speed = edge_terms(x_upper, 1)
    all_flux = jnp.concatenate([low_flux, flux_x, high_flux], axis=2)
    all_speed = jnp.concatenate([low_speed, speed_x, high_speed], axis=1)
    all_cells = jnp.concatenate([x_lower, conserved, x_upper], axis=2)
    faces_x = rusanov(all_flux[:, :, :-1], all_speed[:, :-1], all_cells[:, :, :-1], all_flux[:, :, 1:], all_speed[:, 1:], all_cells[:, :, 1:])
    low_flux, low_speed = edge_terms(y_lower, 2)
    high_flux, high_speed = edge_terms(y_upper, 2)
    all_flux = jnp.concatenate([low_flux, flux_y, high_flux], axis=3)
    all_speed = jnp.concatenate([low_speed, speed_y, high_speed], axis=2)
    all_cells = jnp.concatenate([y_lower, conserved, y_upper], axis=3)
    faces_y = rusanov(all_flux[..., :-1], all_speed[..., :-1], all_cells[..., :-1], all_flux[..., 1:], all_speed[..., 1:], all_cells[..., 1:])
    faces_z = rusanov(flux_z, speed_z, conserved, jnp.roll(flux_z, -1, 1), jnp.roll(speed_z, -1, 0), jnp.roll(conserved, -1, 1))
    change = faces_x[:, :, 1:] - faces_x[:, :, :-1] + (faces_y[..., 1:] - faces_y[..., :-1])
    change = change + (faces_z - jnp.roll(faces_z, 1, 1))
    return (conserved - STEP_RATIO * change, faces_x, faces_y)

def fine_strips(rim_cells):
    widened = jnp.repeat(jnp.repeat(rim_cells, 2, axis=2), 2, axis=3)
    return (widened[0][:, :, None, :], widened[1][:, :, None, :], widened[2][:, :, :, None], widened[3][:, :, :, None])

def coarsen_edges(faces_x, faces_y):
    edge_flux = jnp.stack([faces_x[:, :, 0], faces_x[:, :, -1], faces_y[:, :, :, 0], faces_y[:, :, :, -1]])
    half_depth = edge_flux.shape[2] // 2
    half_span = edge_flux.shape[3] // 2
    return edge_flux.reshape(4, edge_flux.shape[1], half_depth, 2, half_span, 2).sum(axis=(3, 5))

def fine_substep(box_cells, rim_cells):
    x_lower, x_upper, y_lower, y_upper = fine_strips(rim_cells)
    stepped, faces_x, faces_y = advance(box_cells, x_lower, x_upper, y_lower, y_upper)
    return (stepped, coarsen_edges(faces_x, faces_y))

def average_down(box_cells):
    box_shape = box_cells.shape
    grouped = box_cells.reshape(box_shape[0], box_shape[1] // 2, 2, box_shape[2] // 2, 2, box_shape[3] // 2, 2)
    return 0.125 * grouped.sum(axis=(2, 4, 6))

def fine_level(box_cells, old_rims, new_rims):
    first_step, first_sum = fine_substep(box_cells, old_rims)
    second, second_sum = fine_substep(first_step, 0.5 * (old_rims + new_rims))
    return (second, average_down(second), 0.125 * (first_sum + second_sum))

def reference(coarse_state, fine_state, source_rows, tile_ids):
    padded_y = jnp.concatenate([coarse_state[..., -1:], coarse_state, coarse_state[..., :1]], axis=3)
    offsets = jnp.arange(TB, dtype=jnp.int32)
    anchor = jnp.zeros((), jnp.int32)

    def one_column(column_id):
        stripe = lax.dynamic_slice(padded_y, (anchor, anchor, anchor, column_id * CY), (NF, CZ, NX, CY + 2))
        interior = stripe[..., 1:-1]
        coarse_new, faces_x, faces_y = advance(interior, interior[:, :, -1:], interior[:, :, :1], stripe[..., 0:1], stripe[..., -1:])
        sources = lax.dynamic_index_in_dim(source_rows, column_id, 1, keepdims=False).reshape(-1).astype(jnp.int32)
        tile_list = lax.dynamic_index_in_dim(tile_ids, column_id, 1, keepdims=False).reshape(-1).astype(jnp.int32)
        fine_boxes = lax.dynamic_index_in_dim(fine_state, column_id, 1, keepdims=False).reshape(N_GX * R, NF, FZ, FB, FB)
        x_start = (sources * CX + tile_list // TY * TB).astype(jnp.int32)
        y_start = (tile_list % TY * TB).astype(jnp.int32)

        def rim_cells(field_cells, x_first, y_first):
            return jnp.stack([lax.dynamic_slice(field_cells, (anchor, anchor, x_first - 1, y_first), (NF, CZ, 1, TB))[:, :, 0], lax.dynamic_slice(field_cells, (anchor, anchor, x_first + TB, y_first), (NF, CZ, 1, TB))[:, :, 0], lax.dynamic_slice(field_cells, (anchor, anchor, x_first, y_first - 1), (NF, CZ, TB, 1))[..., 0], lax.dynamic_slice(field_cells, (anchor, anchor, x_first, y_first + TB), (NF, CZ, TB, 1))[..., 0]])

        def interface(x_first, y_first):
            return jnp.stack([lax.dynamic_slice(faces_x, (anchor, anchor, x_first, y_first), (NF, CZ, 1, TB))[:, :, 0], lax.dynamic_slice(faces_x, (anchor, anchor, x_first + TB, y_first), (NF, CZ, 1, TB))[:, :, 0], lax.dynamic_slice(faces_y, (anchor, anchor, x_first, y_first), (NF, CZ, TB, 1))[..., 0], lax.dynamic_slice(faces_y, (anchor, anchor, x_first, y_first + TB), (NF, CZ, TB, 1))[..., 0]])
        old_rims = jax.vmap(rim_cells, (None, 0, 0))(interior, x_start, y_start)
        new_rims = jax.vmap(rim_cells, (None, 0, 0))(coarse_new, x_start, y_start)
        fine_new, averaged, flux_mean = jax.vmap(fine_level)(fine_boxes, old_rims, new_rims)
        coarse_flux = jax.vmap(interface)(x_start, y_start)
        by_field = jnp.moveaxis(STEP_RATIO * (flux_mean - coarse_flux), 0, 3)
        span_x = x_start[:, None] + offsets[None, :]
        span_y = y_start[:, None] + offsets[None, :]
        correction = jnp.zeros((NF, CZ, NX, CY), jnp.float32)
        correction = correction.at[:, :, (x_start - 1)[:, None], span_y].add(-by_field[0])
        correction = correction.at[:, :, (x_start + TB)[:, None], span_y].add(by_field[1])
        correction = correction.at[:, :, span_x, (y_start - 1)[:, None]].add(-by_field[2])
        correction = correction.at[:, :, span_x, (y_start + TB)[:, None]].add(by_field[3])
        x_index = x_start[:, None, None] + offsets[None, :, None]
        y_index = y_start[:, None, None] + offsets[None, None, :]
        average_field = jnp.zeros((NF, CZ, NX, CY), jnp.float32).at[:, :, x_index, y_index].set(jnp.moveaxis(averaged, 0, 2))
        covered = jnp.zeros((NX, CY), jnp.float32).at[x_index, y_index].set(1.0)
        coarse_out = jnp.where(covered > 0.5, average_field, coarse_new + correction)
        return (coarse_out, fine_new.reshape(N_GX, R, NF, FZ, FB * FB))
    coarse_cols, fine_cols = lax.map(one_column, jnp.arange(N_GY, dtype=jnp.int32))
    coarse_out = jnp.transpose(coarse_cols, (1, 2, 3, 0, 4)).reshape(NF, CZ, NX, NY)
    fine_out = jnp.swapaxes(fine_cols, 0, 1)
    return (coarse_out, fine_out)
```

```python
import functools

import jax
import jax.numpy as jnp
from jax import lax
from jax.experimental import pallas as pl
from jax.experimental.pallas import tpu as pltpu
from jax.sharding import PartitionSpec as P

MESH = pl.DeviceIdType.MESH
HEAT_RATIO = 1.4
HALF_STEP = 0.025
BOXES = 8
IMAGES = 10
ROWS = 64
LANES = 128


def iota(shape, dim):
    return lax.broadcasted_iota(jnp.int32, shape, dim)


def roll(x, shift, axis):
    if isinstance(shift, int):
        shift = shift % x.shape[axis]
        if shift == 0:
            return x
    return pltpu.roll(x, shift, axis)


def primitives(u):
    inverse = 1.0 / u[0]
    velocity = [u[1] * inverse, u[2] * inverse, u[3] * inverse]
    kinetic = 0.5 * (u[1] * velocity[0] + u[2] * velocity[1] + u[3] * velocity[2])
    pressure = (HEAT_RATIO - 1.0) * (u[4] - kinetic)
    sound = jnp.sqrt(HEAT_RATIO * pressure * inverse)
    return velocity, pressure, sound


def scaled_state(u, velocity, pressure, sound, k):
    drift = HALF_STEP * velocity[k]
    speed = HALF_STEP * (jnp.abs(velocity[k]) + sound)
    return list(u) + [pressure, drift, speed]


def scaled_flux(state, k):
    u, pressure, drift = state[:5], state[5], state[6]
    flux = [u[f] * drift for f in range(5)]
    flux[1 + k] = flux[1 + k] + HALF_STEP * pressure
    flux[4] = (u[4] + pressure) * drift
    return flux


def face_flux(left, right, k):
    a, b = scaled_flux(left, k), scaled_flux(right, k)
    top = jnp.maximum(left[7], right[7])
    return [(a[f] + b[f]) - top * (right[f] - left[f]) for f in range(5)]


def coarse_step(img, flux_x, flux_y):
    first_row = iota((ROWS, LANES), 0) == 0
    first_col = iota((ROWS, LANES), 1) == 0
    cells, prims = [], []
    for z in range(2):
        u = [img[pl.ds((2 * f + z) * ROWS, ROWS), :] for f in range(5)]
        cells.append(u)
        prims.append(primitives(u))
    depth = [HALF_STEP * (jnp.abs(prims[z][0][0]) + prims[z][2]) for z in range(2)]
    depth = 2.0 * jnp.maximum(depth[0], depth[1])
    for z in range(2):
        u = cells[z]
        new = [u[f] - depth * (u[f] - cells[1 - z][f]) for f in range(5)]
        for k, axis, first, saved in ((1, 0, first_row, flux_x), (2, 1, first_col, flux_y)):
            state = scaled_state(u, *prims[z], k)
            before = [roll(s, 1, axis) for s in state]
            faces = face_flux(before, state, k)
            for f in range(5):
                face = jnp.where(first, 0.0, faces[f])
                saved[pl.ds((2 * f + z) * ROWS, ROWS), :] = face
                new[f] = new[f] - (roll(face, -1, axis) - face)
        for f in range(5):
            img[pl.ds((IMAGES + 2 * f + z) * ROWS, ROWS), :] = new[f]


def build_tables(img, turned, table_x, table_y):
    for tx in range(1, 7):
        for k, row in ((0, 8 * tx - 1), (1, 8 * tx + 8)):
            table_x[tx, pl.ds(16 * k, 8), :] = img[pl.ds(row, 8, stride=ROWS), :]
            table_x[tx, pl.ds(16 * k + 8, 8), :] = img[pl.ds(8 * ROWS + row, 8, stride=ROWS), :]
            table_x[tx, pl.ds(32 + 4 * k, 4), :] = img[pl.ds(16 * ROWS + row, 4, stride=ROWS), :]
    for p in range(IMAGES):
        turned[pl.ds(p * LANES, LANES), :] = jnp.transpose(img[pl.ds(p * LANES, LANES), :])
    for ty in range(1, 15):
        for k, col in ((0, 8 * ty - 1), (1, 8 * ty + 8)):
            table_y[ty, pl.ds(8 * k, 8), :] = turned[pl.ds(col, 8, stride=LANES), :]
            table_y[ty, pl.ds(16 + 2 * k, 2), :] = turned[pl.ds(8 * LANES + col, 2, stride=LANES), :]


def wanted_tile(sources, tiles, o, me):
    tile = jnp.int32(0)
    for r in range(BOXES):
        tile = jnp.where(sources[o, r] == me, tiles[o, r], tile)
    return tile


def pack_rims(n, me, sources, tiles, table_x, table_y, by_tile, rims):
    group = iota((8, LANES), 1) // 8
    for tx in range(1, 7):
        for ty in range(1, 15):
            message = jnp.zeros((8, LANES), jnp.float32)
            for g in range(5):
                part = roll(table_x[tx, pl.ds(8 * g, 8), :], 8 * g - 8 * ty, 1)
                message = jnp.where(group == g, part, message)
            for u in range(3):
                columns = table_y[ty, pl.ds(8 * u, 8), :]
                for j in range(2):
                    part = roll(columns, 64 + 16 * u + 8 * j - 64 * j - 8 * tx, 1)
                    message = jnp.where(group == 8 + 2 * u + j, part, message)
            by_tile[16 * tx + ty] = message

    def one(o, carry):
        rims[o] = by_tile[jnp.maximum(wanted_tile(sources, tiles, o, me), 17)]
        return carry

    lax.fori_loop(0, n, one, 0)


def pack_halo(img, halo_rows, halo_cols):
    halo_rows[...] = jnp.zeros_like(halo_rows)
    halo_rows[pl.ds(0, 8), :] = img[pl.ds(0, 8, stride=ROWS), :]
    halo_rows[pl.ds(8, 2), :] = img[pl.ds(8 * ROWS, 2, stride=ROWS), :]
    halo_rows[pl.ds(16, 8), :] = img[pl.ds(ROWS - 1, 8, stride=ROWS), :]
    halo_rows[pl.ds(24, 2), :] = img[pl.ds(9 * ROWS - 1, 2, stride=ROWS), :]
    lane = iota((ROWS, LANES), 1)
    packed = jnp.ones((ROWS, LANES), jnp.float32)
    for image in range(IMAGES):
        cells = img[pl.ds(image * ROWS, ROWS), :]
        packed = jnp.where(lane == image, roll(cells, image, 1), packed)
        packed = jnp.where(lane == 16 + image, roll(cells, 17 + image, 1), packed)
    halo_cols[...] = packed


def finish_edges(img, halo_rows, halo_cols, from_rows, from_cols):
    def by_row(source, start):
        u = [source[pl.ds(start + 2 * f, 2), :] for f in range(5)]
        return scaled_state(u, *primitives(u), 1)

    own_low, own_high = by_row(halo_rows, 0), by_row(halo_rows, 16)
    low = face_flux(by_row(from_rows.at[0], 16), own_low, 1)
    high = face_flux(own_high, by_row(from_rows.at[1], 0), 1)
    for f in range(5):
        for z in range(2):
            base = (IMAGES + 2 * f + z) * ROWS
            first, last = pl.ds(base, 1), pl.ds(base + ROWS - 1, 1)
            img[first, :] = img[first, :] + low[f][z : z + 1]
            img[last, :] = img[last, :] - high[f][z : z + 1]

    lane = iota((ROWS, LANES), 1)
    own = halo_cols[...]
    left = jnp.where(lane < 16, roll(from_cols[0], -16, 1), own)
    right = jnp.where(lane < 16, own, roll(from_cols[1], 16, 1))

    def by_lane(packed):
        u = [roll(packed, -2 * f, 1) for f in range(5)]
        return scaled_state(u, *primitives(u), 2)

    faces = face_flux(by_lane(left), by_lane(right), 2)
    for f in range(5):
        for z in range(2):
            rows = pl.ds((IMAGES + 2 * f + z) * ROWS, ROWS)
            cells = img[rows, :]
            cells = jnp.where(lane == 0, cells + roll(faces[f], -z, 1), cells)
            cells = jnp.where(lane == LANES - 1, cells - roll(faces[f], 111 - z, 1), cells)
            img[rows, :] = cells


def own_rims(me, sources, rims, held):
    for r in range(BOXES):
        held[pl.ds(8 * r, 8), :] = rims[sources[me, r]]
    by_row = [held[pl.ds(s, BOXES, stride=8), :] for s in range(8)]
    lane = iota((BOXES, LANES), 1)

    def pair(low, low_lane, high, high_lane):
        first = roll(low, -low_lane, 1)
        second = roll(high, 8 - high_lane, 1)
        return jnp.where(lane < 8, first, jnp.where(lane < 16, second, 0.0))

    sides = [[], []]
    for image in range(2 * IMAGES):
        s, g = image % 8, image // 8
        if g < 2:
            sides[0].append(pair(by_row[s], 8 * g, by_row[s], 8 * (g + 2)))
        else:
            sides[0].append(pair(by_row[s], 32, by_row[s + 4], 32))
        p, j = image // 2, image % 2
        if p < 8:
            sides[1].append(pair(by_row[p], 64 + 8 * j, by_row[p], 80 + 8 * j))
        else:
            sides[1].append(pair(by_row[p - 8], 96 + 8 * j, by_row[p - 6], 96 + 8 * j))

    source, cell = iota((LANES, 256), 0), iota((LANES, 256), 1)
    a, b = cell // 16, cell % 16
    spread = []
    for side, (along, across) in enumerate(((b, a), (a, b))):
        chosen = (source < 16) & (source % 8 == along // 2) & (source // 8 == across // 8)
        weights = jnp.where(chosen, 1.0, 0.0)
        old = sides[side][:IMAGES]
        mid = [0.5 * (x + y) for x, y in zip(old, sides[side][IMAGES:])]
        ghosts = jnp.dot(
            jnp.concatenate(old + mid, axis=0),
            weights,
            precision=lax.Precision.HIGHEST,
            preferred_element_type=jnp.float32,
        )
        spread.append(
            [
                [ghosts[(IMAGES * t + i) * 8 : (IMAGES * t + i) * 8 + 8] for i in range(IMAGES)]
                for t in range(2)
            ]
        )
    return spread


def fine_step(u, ghosts_x, ghosts_y, edges):
    cell = iota((BOXES, 256), 1)
    a, b = cell // 16, cell % 16
    prims = [primitives([u[f][z] for f in range(5)]) for z in range(4)]
    states = [scaled_state([u[f][z] for f in range(5)], *prims[z], 0) for z in range(4)]
    deep = [face_flux(states[z], states[(z + 1) % 4], 0) for z in range(4)]
    new = [[u[f][z] - (deep[z][f] - deep[z - 1][f]) for z in range(4)] for f in range(5)]
    sides = (
        (1, ghosts_x, 16, a == 0, a == 15, a < 8),
        (2, ghosts_y, 1, b == 0, b == 15, b < 8),
    )
    for side, (k, ghosts, stride, first, last, lower) in enumerate(sides):
        for half in range(2):
            cells = [ghosts[2 * f + half] for f in range(5)]
            ghost = scaled_state(cells, *primitives(cells), k)
            for z in (2 * half, 2 * half + 1):
                state = scaled_state([u[f][z] for f in range(5)], *prims[z], k)
                before = [
                    jnp.where(first, ghost[i], roll(state[i], stride, 1)) for i in range(8)
                ]
                low = face_flux(before, state, k)
                outer = face_flux(state, ghost, k)
                for f in range(5):
                    high = jnp.where(last, outer[f], roll(low[f], -stride, 1))
                    new[f][z] = new[f][z] - (high - low[f])
                    edge = jnp.where(lower, low[f], high)
                    held = edges[side][2 * f + half]
                    edges[side][2 * f + half] = edge if held is None else held + edge
    return new


def pack_results(n, me, sources, u, edges, held, packed, results):
    cell, target = iota((256, LANES), 0), iota((256, LANES), 1)
    a, b = cell // 16, cell % 16
    flipped, along = 7 - a // 2, b // 2
    average = (target < 64) & (target // 8 == flipped) & (target % 8 == along)
    rows = ((target // 8 == 8) & (a == 0) | (target // 8 == 9) & (a == 15)) & (target % 8 == along)
    cols = ((target // 8 == 10) & (b == 0) | (target // 8 == 11) & (b == 15)) & (
        target % 8 == flipped
    )
    thick = [u[i // 2][2 * (i % 2)] + u[i // 2][2 * (i % 2) + 1] for i in range(IMAGES)]
    total = None
    for values, weights in ((thick, average), (edges[0], rows), (edges[1], cols)):
        part = jnp.dot(
            jnp.concatenate(values, axis=0),
            jnp.where(weights, 0.125, 0.0),
            precision=lax.Precision.HIGHEST,
            preferred_element_type=jnp.float32,
        )
        total = part if total is None else total + part
    sums = [total[8 * i : 8 * i + 8] for i in range(IMAGES)]
    lane = iota((BOXES, LANES), 1)
    for q in range(5):
        row = jnp.where(lane < 64, sums[2 * q], roll(sums[2 * q + 1], 64, 1))
        held[pl.ds(q, BOXES, stride=8), :] = row
    for w in range(3):
        row = jnp.zeros((BOXES, LANES), jnp.float32)
        for h in range(4):
            if 4 * w + h < IMAGES:
                row = jnp.where(lane // 32 == h, roll(sums[4 * w + h], 32 * h - 64, 1), row)
        held[pl.ds(5 + w, BOXES, stride=8), :] = row

    for r in range(BOXES):
        packed[r] = held[pl.ds(8 * r, 8), :]

    def one(s, carry):
        box = jnp.int32(0)
        for r in range(BOXES):
            box = jnp.where(sources[me, r] == s, r, box)
        results[s] = packed[box]
        return carry

    lax.fori_loop(0, n, one, 0)


def exchange(n, me, source, target, sems):
    def send(step, carry):
        other = lax.rem(me + step, n)
        pltpu.make_async_remote_copy(
            src_ref=source.at[other],
            dst_ref=target.at[me],
            send_sem=sems.at[0],
            recv_sem=sems.at[1],
            device_id={"gx": other},
            device_id_type=MESH,
        ).start()
        return carry

    lax.fori_loop(1, n, send, 0)
    return pltpu.make_async_remote_copy(
        src_ref=source.at[pl.ds(0, n - 1)],
        dst_ref=target.at[pl.ds(0, n - 1)],
        send_sem=sems.at[0],
        recv_sem=sems.at[1],
        device_id={"gx": me},
        device_id_type=MESH,
    )


def level_kernel(
    n,
    m,
    coarse,
    fine,
    sources,
    tiles,
    coarse_new,
    rows_x,
    flux_y,
    returned,
    fine_out,
    img,
    flux_x,
    turned,
    table_x,
    table_y,
    by_tile,
    rims,
    rims_in,
    held,
    packed,
    results,
    cells,
    halo_rows,
    halo_cols,
    from_rows,
    from_cols,
    rim_sems,
    result_sems,
    halo_sems,
):
    me, column = lax.axis_index("gx"), lax.axis_index("gy")
    up, down = lax.rem(me + 1, n), lax.rem(me + n - 1, n)
    right, left = lax.rem(column + 1, m), lax.rem(column + m - 1, m)
    barrier = pltpu.get_barrier_semaphore()

    def greet(step, carry):
        other = lax.rem(me + step, n)
        pl.semaphore_signal(barrier, 1, device_id={"gx": other}, device_id_type=MESH)
        return carry

    lax.fori_loop(1, n, greet, 0)
    pl.semaphore_signal(barrier, 1, device_id={"gy": right}, device_id_type=MESH)
    pl.semaphore_signal(barrier, 1, device_id={"gy": left}, device_id_type=MESH)

    img[pl.ds(0, IMAGES * ROWS), :] = coarse[...]
    coarse_step(img, flux_x, flux_y)
    table_x[...] = jnp.zeros_like(table_x)
    table_y[...] = jnp.zeros_like(table_y)
    build_tables(img, turned, table_x, table_y)
    pack_rims(n, me, sources, tiles, table_x, table_y, by_tile, rims)
    pack_halo(img, halo_rows, halo_cols)
    pl.semaphore_wait(barrier, n + 1)

    rim_copies = exchange(n, me, rims, rims_in, rim_sems)
    halos = []
    for i, (source, target, where) in enumerate(
        (
            (halo_rows, from_rows.at[0], {"gx": up}),
            (halo_rows, from_rows.at[1], {"gx": down}),
            (halo_cols, from_cols.at[0], {"gy": right}),
            (halo_cols, from_cols.at[1], {"gy": left}),
        )
    ):
        copy = pltpu.make_async_remote_copy(
            src_ref=source,
            dst_ref=target,
            send_sem=halo_sems.at[0, i],
            recv_sem=halo_sems.at[1, i],
            device_id=where,
            device_id_type=MESH,
        )
        copy.start()
        halos.append(copy)
    for r in range(BOXES):
        for f in range(5):
            for z in range(4):
                cells[4 * f + z, pl.ds(r, 1), :] = fine[r, f, pl.ds(z, 1), :]
    for i in range(8):
        for image in range(IMAGES):
            rows_x[i, pl.ds(image, 1), :] = flux_x[pl.ds(image * ROWS + 8 * i, 1), :]
    rows_x[:, pl.ds(IMAGES, 6), :] = jnp.zeros((8, 6, LANES), jnp.float32)
    for copy in halos:
        copy.wait_recv()
    finish_edges(img, halo_rows, halo_cols, from_rows, from_cols)
    coarse_new[...] = img[pl.ds(IMAGES * ROWS, IMAGES * ROWS), :]

    rim_copies.wait_recv()
    rims_in[me] = rims[me]
    ghosts = own_rims(me, sources, rims_in, held)
    u = [[cells[4 * f + z] for z in range(4)] for f in range(5)]
    edges = [[None] * IMAGES, [None] * IMAGES]
    u = fine_step(u, ghosts[0][0], ghosts[1][0], edges)
    u = fine_step(u, ghosts[0][1], ghosts[1][1], edges)
    pack_results(n, me, sources, u, edges, held, packed, results)
    result_copies = exchange(n, me, results, returned, result_sems)
    for f in range(5):
        for z in range(4):
            for r in range(BOXES):
                fine_out[r, f, pl.ds(z, 1), :] = u[f][z][r : r + 1]
    rim_copies.wait_send()
    for copy in halos:
        copy.wait_send()
    result_copies.wait_recv()
    returned[me] = results[me]
    result_copies.wait_send()


def merge_kernel(n, new, rows_x, flux_y, returned, sources, tiles, fine, out, fine_out):
    me = lax.axis_index("gx")
    out[...] = new[...]
    fine_out[...] = fine[...]
    lane, sub = iota((8, LANES), 1), iota((8, LANES), 0)

    def spread(o, row):
        return jnp.broadcast_to(returned[o, pl.ds(row, 1), :], (8, LANES))

    def turned(x, shift, stride):
        x = pltpu.roll(x, 0, 1, stride=stride, stride_axis=0)
        return pltpu.roll(x, lax.rem(shift + 2 * LANES, LANES), 1)

    def correct(o, carry):
        tile = wanted_tile(sources, tiles, o, me)

        @pl.when(tile > 0)
        def _():
            tx, ty = tile // 16, tile % 16
            inside = lane // 8 == ty
            low_face = rows_x[tx]
            high_face = rows_x[tx + 1]
            for image in range(IMAGES):
                base = 32 * (image % 4)
                values = spread(o, 5 + image // 4)
                here = image * ROWS + 8 * tx
                rows = pl.ds(pl.multiple_of(here - 8, 8), 8)
                low = pltpu.roll(values, lax.rem(8 * ty - base + LANES, LANES), 1)
                change = low - low_face[image : image + 1]
                out[rows, :] = out[rows, :] - jnp.where(inside & (sub == 7), change, 0.0)
                rows = pl.ds(pl.multiple_of(here + 8, 8), 8)
                high = pltpu.roll(values, lax.rem(8 * ty - base - 8 + 2 * LANES, LANES), 1)
                change = high - high_face[image : image + 1]
                out[rows, :] = out[rows, :] + jnp.where(inside & (sub == 0), change, 0.0)
                rows = pl.ds(pl.multiple_of(here, 8), 8)
                faces = flux_y[rows, :]
                low = turned(values, 8 * ty - 1 - base - 23, 1) - pltpu.roll(faces, LANES - 1, 1)
                high = turned(values, 8 * ty + 8 - base - 31, 1) - faces
                change = jnp.where(lane == 8 * ty + 8, high, 0.0)
                change = jnp.where(lane == 8 * ty - 1, -low, change)
                out[rows, :] = out[rows, :] + change

        return carry

    def average(o, carry):
        tile = wanted_tile(sources, tiles, o, me)

        @pl.when(tile > 0)
        def _():
            tx, ty = tile // 16, tile % 16
            inside = lane // 8 == ty
            for image in range(IMAGES):
                rows = pl.ds(pl.multiple_of(image * ROWS + 8 * tx, 8), 8)
                values = turned(spread(o, image // 2), 8 * ty - 64 * (image % 2) - 56, 8)
                out[rows, :] = jnp.where(inside, values, out[rows, :])

        return carry

    lax.fori_loop(0, n, correct, 0)
    lax.fori_loop(0, n, average, 0)


def body(n, m, coarse_state, fine_state, source_rows, tile_ids):
    vmem = pl.BlockSpec(memory_space=pltpu.VMEM)
    smem = pl.BlockSpec(memory_space=pltpu.SMEM)
    f32 = jnp.float32
    coarse = coarse_state.reshape(IMAGES * ROWS, LANES)
    fine = fine_state.reshape(BOXES, 5, 4, 256)
    sources = source_rows.reshape(n, BOXES)
    tiles = tile_ids.reshape(n, BOXES)
    shape = jax.ShapeDtypeStruct
    new, rows_x, flux_y, returned, fine_out = pl.pallas_call(
        functools.partial(level_kernel, n, m),
        out_shape=(
            shape((IMAGES * ROWS, LANES), f32),
            shape((8, 16, LANES), f32),
            shape((IMAGES * ROWS, LANES), f32),
            shape((n, 8, LANES), f32),
            shape((BOXES, 5, 4, 256), f32),
        ),
        in_specs=[vmem, vmem, smem, smem],
        out_specs=(vmem,) * 5,
        scratch_shapes=[
            pltpu.VMEM((2 * IMAGES * ROWS, LANES), f32),
            pltpu.VMEM((IMAGES * ROWS, LANES), f32),
            pltpu.VMEM((IMAGES * LANES, LANES), f32),
            pltpu.VMEM((8, 40, LANES), f32),
            pltpu.VMEM((16, 24, LANES), f32),
            pltpu.VMEM((128, 8, LANES), f32),
            pltpu.VMEM((n, 8, LANES), f32),
            pltpu.VMEM((n, 8, LANES), f32),
            pltpu.VMEM((8 * BOXES, LANES), f32),
            pltpu.VMEM((BOXES, 8, LANES), f32),
            pltpu.VMEM((n, 8, LANES), f32),
            pltpu.VMEM((20, BOXES, 256), f32),
            pltpu.VMEM((32, LANES), f32),
            pltpu.VMEM((ROWS, LANES), f32),
            pltpu.VMEM((2, 32, LANES), f32),
            pltpu.VMEM((2, ROWS, LANES), f32),
            pltpu.SemaphoreType.DMA((2,)),
            pltpu.SemaphoreType.DMA((2,)),
            pltpu.SemaphoreType.DMA((2, 4)),
        ],
        compiler_params=pltpu.CompilerParams(
            collective_id=0, has_side_effects=True, vmem_limit_bytes=40 * 1024 * 1024
        ),
        name="levels",
    )(coarse, fine, sources, tiles)
    out, fine_out = pl.pallas_call(
        functools.partial(merge_kernel, n),
        out_shape=(
            shape((IMAGES * ROWS, LANES), f32),
            shape((BOXES, 5, 4, 256), f32),
        ),
        in_specs=[vmem, vmem, vmem, vmem, smem, smem, vmem],
        out_specs=(vmem,) * 2,
        compiler_params=pltpu.CompilerParams(vmem_limit_bytes=40 * 1024 * 1024),
        name="merge",
    )(new, rows_x, flux_y, returned, sources, tiles, fine_out)
    return out.reshape(coarse_state.shape), fine_out.reshape(fine_state.shape)


def solution(mesh):
    return jax.shard_map(
        functools.partial(body, mesh.shape["gx"], mesh.shape["gy"]),
        mesh=mesh,
        in_specs=(
            P(None, None, "gx", "gy"),
            P("gx", "gy", None, None, None, None),
            P(None, "gy", None),
            P(None, "gy", None),
        ),
        out_specs=(P(None, None, "gx", "gy"), P("gx", "gy", None, None, None, None)),
        check_vma=False,
    )
```

```python
import functools

import jax
import jax.numpy as jnp
from jax import lax
from jax.experimental import pallas as pl
from jax.experimental.pallas import tpu as pltpu
from jax.sharding import PartitionSpec as P

MESH = pl.DeviceIdType.MESH
HEAT_RATIO = 1.4
HALF_STEP = 0.025
BOXES = 8
IMAGES = 10
ROWS = 64
LANES = 128
VMEM_LIMIT = 65280 * 1024


def iota(shape, dim):
    return lax.broadcasted_iota(jnp.int32, shape, dim)


def roll(x, shift, axis):
    if isinstance(shift, int):
        shift = shift % x.shape[axis]
        if shift == 0:
            return x
    return pltpu.roll(x, shift, axis)


def select_dot(values, weights):
    x = jnp.concatenate(values, axis=0)
    high = x.astype(jnp.bfloat16)
    x = x - high.astype(jnp.float32)
    middle = x.astype(jnp.bfloat16)
    low = (x - middle.astype(jnp.float32)).astype(jnp.bfloat16)
    weights = weights.astype(jnp.bfloat16)
    parts = [
        jnp.dot(part, weights, preferred_element_type=jnp.float32) for part in (low, middle, high)
    ]
    return parts[0] + parts[1] + parts[2]


def primitives(u):
    inverse = 1.0 / u[0]
    velocity = [u[1] * inverse, u[2] * inverse, u[3] * inverse]
    kinetic = 0.5 * (u[1] * velocity[0] + u[2] * velocity[1] + u[3] * velocity[2])
    pressure = (HEAT_RATIO - 1.0) * (u[4] - kinetic)
    sound = jnp.sqrt(HEAT_RATIO * pressure * inverse)
    return velocity, pressure, sound


def scaled_state(u, velocity, pressure, sound, k):
    drift = HALF_STEP * velocity[k]
    speed = HALF_STEP * (jnp.abs(velocity[k]) + sound)
    return list(u) + [pressure, drift, speed]


def scaled_flux(state, k):
    u, pressure, drift = state[:5], state[5], state[6]
    flux = [u[f] * drift for f in range(5)]
    flux[1 + k] = flux[1 + k] + HALF_STEP * pressure
    flux[4] = (u[4] + pressure) * drift
    return flux


def face_flux(left, right, k):
    a, b = scaled_flux(left, k), scaled_flux(right, k)
    top = jnp.maximum(left[7], right[7])
    return [(a[f] + b[f]) - top * (right[f] - left[f]) for f in range(5)]


def coarse_step(img, flux_x, flux_y):
    row, col = iota((ROWS, LANES), 0), iota((ROWS, LANES), 1)
    cells, prims = [], []
    for z in range(2):
        u = [img[pl.ds((2 * f + z) * ROWS, ROWS), :] for f in range(5)]
        cells.append(u)
        prims.append(primitives(u))
    depth = [HALF_STEP * (jnp.abs(prims[z][0][0]) + prims[z][2]) for z in range(2)]
    depth = 2.0 * jnp.maximum(depth[0], depth[1])
    for z in range(2):
        u = cells[z]
        new = [u[f] - depth * (u[f] - cells[1 - z][f]) for f in range(5)]
        for k, axis, place, saved in ((1, 0, row, flux_x), (2, 1, col, flux_y)):
            state = scaled_state(u, *prims[z], k)
            before = [roll(s, 1, axis) for s in state]
            faces = face_flux(before, state, k)
            for f in range(5):
                face = jnp.where(place == 0, 0.0, faces[f])
                upper = roll(face, -1, axis)
                signed = jnp.where(place % 8 == 7, -upper, face)
                saved[pl.ds((2 * f + z) * ROWS, ROWS), :] = signed
                new[f] = new[f] - (upper - face)
        for f in range(5):
            img[pl.ds((IMAGES + 2 * f + z) * ROWS, ROWS), :] = new[f]


def build_tables(img, turned, table_x, table_y):
    for tx in range(1, 7):
        for k, row in ((0, 8 * tx - 1), (1, 8 * tx + 8)):
            table_x[tx, pl.ds(16 * k, 8), :] = img[pl.ds(row, 8, stride=ROWS), :]
            table_x[tx, pl.ds(16 * k + 8, 8), :] = img[pl.ds(8 * ROWS + row, 8, stride=ROWS), :]
            table_x[tx, pl.ds(32 + 4 * k, 4), :] = img[pl.ds(16 * ROWS + row, 4, stride=ROWS), :]
    for p in range(IMAGES):
        turned[pl.ds(p * LANES, LANES), :] = jnp.transpose(img[pl.ds(p * LANES, LANES), :])
    for ty in range(1, 15):
        for k, col in ((0, 8 * ty - 1), (1, 8 * ty + 8)):
            table_y[ty, pl.ds(8 * k, 8), :] = turned[pl.ds(col, 8, stride=LANES), :]
            table_y[ty, pl.ds(16 + 2 * k, 2), :] = turned[pl.ds(8 * LANES + col, 2, stride=LANES), :]


def wanted_tile(sources, tiles, o, me):
    tile = jnp.int32(0)
    for r in range(BOXES):
        tile = jnp.where(sources[r, o] == me, tiles[r, o], tile)
    return tile


def pack_rims(n, me, sources, tiles, table_x, table_y, by_tile, rims, wanted):
    group = iota((8, LANES), 1) // 8
    for tx in range(1, 7):
        for ty in range(1, 15):
            message = jnp.zeros((8, LANES), jnp.float32)
            for g in range(5):
                part = roll(table_x[tx, pl.ds(8 * g, 8), :], 8 * g - 8 * ty, 1)
                message = jnp.where(group == g, part, message)
            for u in range(3):
                columns = table_y[ty, pl.ds(8 * u, 8), :]
                for j in range(2):
                    part = roll(columns, 64 + 16 * u + 8 * j - 64 * j - 8 * tx, 1)
                    message = jnp.where(group == 8 + 2 * u + j, part, message)
            by_tile[16 * tx + ty] = message

    def one(o, carry):
        tile = wanted_tile(sources, tiles, o, me)
        wanted[o] = tile
        rims[o] = by_tile[jnp.maximum(tile, 17)]
        return carry

    lax.fori_loop(0, n, one, 0)


def pack_halo(img, halo_rows, halo_cols):
    halo_rows[...] = jnp.zeros_like(halo_rows)
    halo_rows[pl.ds(0, 8), :] = img[pl.ds(0, 8, stride=ROWS), :]
    halo_rows[pl.ds(8, 2), :] = img[pl.ds(8 * ROWS, 2, stride=ROWS), :]
    halo_rows[pl.ds(16, 8), :] = img[pl.ds(ROWS - 1, 8, stride=ROWS), :]
    halo_rows[pl.ds(24, 2), :] = img[pl.ds(9 * ROWS - 1, 2, stride=ROWS), :]
    lane = iota((ROWS, LANES), 1)
    packed = jnp.ones((ROWS, LANES), jnp.float32)
    for image in range(IMAGES):
        cells = img[pl.ds(image * ROWS, ROWS), :]
        packed = jnp.where(lane == image, roll(cells, image, 1), packed)
        packed = jnp.where(lane == 16 + image, roll(cells, 17 + image, 1), packed)
    halo_cols[...] = packed


def finish_edges(img, halo_rows, halo_cols, from_rows, from_cols):
    def by_row(source, start):
        u = [source[pl.ds(start + 2 * f, 2), :] for f in range(5)]
        return scaled_state(u, *primitives(u), 1)

    own_low, own_high = by_row(halo_rows, 0), by_row(halo_rows, 16)
    low = face_flux(by_row(from_rows.at[0], 16), own_low, 1)
    high = face_flux(own_high, by_row(from_rows.at[1], 0), 1)
    for f in range(5):
        for z in range(2):
            base = (IMAGES + 2 * f + z) * ROWS
            first, last = pl.ds(base, 1), pl.ds(base + ROWS - 1, 1)
            img[first, :] = img[first, :] + low[f][z : z + 1]
            img[last, :] = img[last, :] - high[f][z : z + 1]

    lane = iota((ROWS, LANES), 1)
    own = halo_cols[...]
    left = jnp.where(lane < 16, roll(from_cols[0], -16, 1), own)
    right = jnp.where(lane < 16, own, roll(from_cols[1], 16, 1))

    def by_lane(packed):
        u = [roll(packed, -2 * f, 1) for f in range(5)]
        return scaled_state(u, *primitives(u), 2)

    faces = face_flux(by_lane(left), by_lane(right), 2)
    for f in range(5):
        for z in range(2):
            rows = pl.ds((IMAGES + 2 * f + z) * ROWS, ROWS)
            cells = img[rows, :]
            cells = jnp.where(lane == 0, cells + roll(faces[f], -z, 1), cells)
            cells = jnp.where(lane == LANES - 1, cells - roll(faces[f], 111 - z, 1), cells)
            img[rows, :] = cells


def own_rims(me, sources, rims, held):
    for r in range(BOXES):
        held[pl.ds(8 * r, 8), :] = rims[sources[r, me]]
    by_row = [held[pl.ds(s, BOXES, stride=8), :] for s in range(8)]
    lane = iota((BOXES, LANES), 1)

    def pair(low, low_lane, high, high_lane):
        first = roll(low, -low_lane, 1)
        second = roll(high, 8 - high_lane, 1)
        return jnp.where(lane < 8, first, jnp.where(lane < 16, second, 0.0))

    sides = [[], []]
    for image in range(2 * IMAGES):
        s, g = image % 8, image // 8
        if g < 2:
            sides[0].append(pair(by_row[s], 8 * g, by_row[s], 8 * (g + 2)))
        else:
            sides[0].append(pair(by_row[s], 32, by_row[s + 4], 32))
        p, j = image // 2, image % 2
        if p < 8:
            sides[1].append(pair(by_row[p], 64 + 8 * j, by_row[p], 80 + 8 * j))
        else:
            sides[1].append(pair(by_row[p - 8], 96 + 8 * j, by_row[p - 6], 96 + 8 * j))

    source, cell = iota((LANES, 256), 0), iota((LANES, 256), 1)
    a, b = cell // 16, cell % 16
    spread = []
    for side, (along, across) in enumerate(((b, a), (a, b))):
        chosen = (source < 16) & (source % 8 == along // 2) & (source // 8 == across // 8)
        weights = jnp.where(chosen, 1.0, 0.0)
        old = sides[side][:IMAGES]
        mid = [0.5 * (x + y) for x, y in zip(old, sides[side][IMAGES:])]
        ghosts = select_dot(old + mid, weights)
        spread.append(
            [
                [ghosts[(IMAGES * t + i) * 8 : (IMAGES * t + i) * 8 + 8] for i in range(IMAGES)]
                for t in range(2)
            ]
        )
    return spread


def fine_step(u, ghosts_x, ghosts_y, edges):
    cell = iota((BOXES, 256), 1)
    a, b = cell // 16, cell % 16
    prims = [primitives([u[f][z] for f in range(5)]) for z in range(4)]
    states = [scaled_state([u[f][z] for f in range(5)], *prims[z], 0) for z in range(4)]
    deep = [face_flux(states[z], states[(z + 1) % 4], 0) for z in range(4)]
    new = [[u[f][z] - (deep[z][f] - deep[z - 1][f]) for z in range(4)] for f in range(5)]
    sides = (
        (1, ghosts_x, 16, a == 0, a == 15, a < 8),
        (2, ghosts_y, 1, b == 0, b == 15, b < 8),
    )
    for side, (k, ghosts, stride, first, last, lower) in enumerate(sides):
        for half in range(2):
            cells = [ghosts[2 * f + half] for f in range(5)]
            ghost = scaled_state(cells, *primitives(cells), k)
            for z in (2 * half, 2 * half + 1):
                state = scaled_state([u[f][z] for f in range(5)], *prims[z], k)
                before = [
                    jnp.where(first, ghost[i], roll(state[i], stride, 1)) for i in range(8)
                ]
                low = face_flux(before, state, k)
                outer = face_flux(state, ghost, k)
                for f in range(5):
                    high = jnp.where(last, outer[f], roll(low[f], -stride, 1))
                    new[f][z] = new[f][z] - (high - low[f])
                    edge = jnp.where(lower, low[f], high)
                    held = edges[side][2 * f + half]
                    edges[side][2 * f + half] = edge if held is None else held + edge
    return new


def pack_results(n, me, sources, u, edges, held, packed, results):
    cell, target = iota((256, LANES), 0), iota((256, LANES), 1)
    a, b = cell // 16, cell % 16
    row, lane = target // 16, target % 16
    average = (row == a // 2) & (lane - 1 == b // 2)
    low_col = (row == a // 2) & (lane == 0) & (b == 0)
    high_col = (row == a // 2) & (lane == 9) & (b == 15)
    low_row = (target == b // 2) & (a == 0)
    high_row = (target == 8 + b // 2) & (a == 15)

    def weights(low, high):
        return jnp.where(low, -0.125, jnp.where(high, 0.125, 0.0))

    thick = [u[i // 2][2 * (i % 2)] + u[i // 2][2 * (i % 2) + 1] for i in range(IMAGES)]
    inner = select_dot(thick, jnp.where(average, 0.125, 0.0))
    inner = inner + select_dot(edges[1], weights(low_col, high_col))
    outer = select_dot(edges[0], weights(low_row, high_row))
    inner = [inner[8 * i : 8 * i + 8] for i in range(IMAGES)]
    outer = [outer[8 * i : 8 * i + 8] for i in range(IMAGES)]
    lane = iota((BOXES, LANES), 1)
    for i in range(8):
        message = roll(outer[i], 100, 1)
        if i < 4:
            last = roll(outer[8 + i % 2], 116 if i < 2 else 108, 1)
            message = jnp.where(lane < 116, message, last)
        for image in range(IMAGES - 1, -1, -1):
            part = roll(inner[image], 10 * image - 16 * i, 1)
            message = jnp.where(lane < 10 * image + 10, part, message)
        held[pl.ds(i, BOXES, stride=8), :] = message
    for r in range(BOXES):
        packed[r] = held[pl.ds(8 * r, 8), :]

    def one(s, carry):
        box = jnp.int32(0)
        for r in range(BOXES):
            box = jnp.where(sources[r, me] == s, r, box)
        results[s] = packed[box]
        return carry

    lax.fori_loop(0, n, one, 0)


def exchange(n, me, source, target, sems):
    def send(step, carry):
        other = lax.rem(me + step, n)
        pltpu.make_async_remote_copy(
            src_ref=source.at[other],
            dst_ref=target.at[me],
            send_sem=sems.at[0],
            recv_sem=sems.at[1],
            device_id={"gx": other},
            device_id_type=MESH,
        ).start()
        return carry

    lax.fori_loop(1, n, send, 0)
    return pltpu.make_async_remote_copy(
        src_ref=source.at[pl.ds(0, n - 1)],
        dst_ref=target.at[pl.ds(0, n - 1)],
        send_sem=sems.at[0],
        recv_sem=sems.at[1],
        device_id={"gx": me},
        device_id_type=MESH,
    )


def level_kernel(
    n,
    m,
    coarse,
    fine_in,
    sources_in,
    tiles_in,
    coarse_new,
    flux_x,
    flux_y,
    returned,
    fine_out,
    wanted,
    sources,
    tiles,
    img,
    fine,
    turned,
    table_x,
    table_y,
    by_tile,
    rims,
    rims_in,
    held,
    packed,
    results,
    cells,
    halo_rows,
    halo_cols,
    from_rows,
    from_cols,
    load_sems,
    rim_sems,
    result_sems,
    halo_sems,
):
    me, column = lax.axis_index("gx"), lax.axis_index("gy")
    up, down = lax.rem(me + 1, n), lax.rem(me + n - 1, n)
    right, left = lax.rem(column + 1, m), lax.rem(column + m - 1, m)
    barrier = pltpu.get_barrier_semaphore()

    def greet(step, carry):
        other = lax.rem(me + step, n)
        pl.semaphore_signal(barrier, 1, device_id={"gx": other}, device_id_type=MESH)
        return carry

    lax.fori_loop(1, n, greet, 0)
    pl.semaphore_signal(barrier, 1, device_id={"gy": right}, device_id_type=MESH)
    pl.semaphore_signal(barrier, 1, device_id={"gy": left}, device_id_type=MESH)

    load = pltpu.make_async_copy(coarse, img.at[pl.ds(0, IMAGES * ROWS)], load_sems.at[0])
    load_fine = pltpu.make_async_copy(fine_in, fine, load_sems.at[1])
    load_sources = pltpu.make_async_copy(sources_in, sources, load_sems.at[2])
    load_tiles = pltpu.make_async_copy(tiles_in, tiles, load_sems.at[3])
    load.start()
    load_sources.start()
    load_tiles.start()
    load_fine.start()
    load.wait()
    coarse_step(img, flux_x, flux_y)
    table_x[...] = jnp.zeros_like(table_x)
    table_y[...] = jnp.zeros_like(table_y)
    build_tables(img, turned, table_x, table_y)
    load_sources.wait()
    load_tiles.wait()
    pack_rims(n, me, sources, tiles, table_x, table_y, by_tile, rims, wanted)
    pack_halo(img, halo_rows, halo_cols)
    pl.semaphore_wait(barrier, n + 1)

    rim_copies = exchange(n, me, rims, rims_in, rim_sems)
    halos = []
    for i, (source, target, where) in enumerate(
        (
            (halo_rows, from_rows.at[0], {"gx": up}),
            (halo_rows, from_rows.at[1], {"gx": down}),
            (halo_cols, from_cols.at[0], {"gy": right}),
            (halo_cols, from_cols.at[1], {"gy": left}),
        )
    ):
        copy = pltpu.make_async_remote_copy(
            src_ref=source,
            dst_ref=target,
            send_sem=halo_sems.at[0, i],
            recv_sem=halo_sems.at[1, i],
            device_id=where,
            device_id_type=MESH,
        )
        copy.start()
        halos.append(copy)
    load_fine.wait()
    for r in range(BOXES):
        for f in range(5):
            for z in range(4):
                cells[4 * f + z, pl.ds(r, 1), :] = fine[r, f, pl.ds(z, 1), :]
    for copy in halos:
        copy.wait_recv()
    finish_edges(img, halo_rows, halo_cols, from_rows, from_cols)
    coarse_new[...] = img[pl.ds(IMAGES * ROWS, IMAGES * ROWS), :]

    rim_copies.wait_recv()
    rims_in[me] = rims[me]
    ghosts = own_rims(me, sources, rims_in, held)
    u = [[cells[4 * f + z] for z in range(4)] for f in range(5)]
    edges = [[None] * IMAGES, [None] * IMAGES]
    u = fine_step(u, ghosts[0][0], ghosts[1][0], edges)
    u = fine_step(u, ghosts[0][1], ghosts[1][1], edges)
    pack_results(n, me, sources, u, edges, held, packed, results)
    result_copies = exchange(n, me, results, returned, result_sems)
    for f in range(5):
        for z in range(4):
            for r in range(BOXES):
                fine_out[r, f, pl.ds(z, 1), :] = u[f][z][r : r + 1]
    rim_copies.wait_send()
    for copy in halos:
        copy.wait_send()
    result_copies.wait_recv()
    returned[me] = results[me]
    result_copies.wait_send()


def merge_kernel(
    n, new, flux_x, flux_y, returned, wanted, fine, out, fine_out, slots, marks, outer, inner
):
    fine_out[...] = fine[...]
    lane, sub = iota((8, LANES), 1), iota((8, LANES), 0)

    def clear(t, carry):
        slots[t] = -1
        return carry

    def place(o, carry):
        slots[wanted[o]] = o
        return carry

    lax.fori_loop(0, 128, clear, 0, unroll=8)
    lax.fori_loop(0, n, place, 0, unroll=8)
    blank = jnp.zeros((8, LANES), jnp.float32)
    for tx in (0, 7):
        for i in range(2):
            marks[tx, i] = blank
        for image in range(IMAGES):
            inner[tx, image] = blank
        for g in range(3):
            outer[tx, g] = blank

    def row_of_tiles(tx, carry):
        parts = [blank] * IMAGES
        sides = [blank] * 3
        covered, touched = blank, blank
        before = jnp.int32(0)
        for ty in range(1, 15):
            slot = slots[16 * tx + ty]
            live = (slot >= 0).astype(jnp.int32)
            message = returned[jnp.maximum(slot, 0)]
            here = (lane // 8 == ty) & (lane < 1024 * live)
            first = jnp.where(live > 0, 8 * ty - 1 + before, 1024)
            wide = (lane >= first) & (lane < 8 * ty + 9)
            covered = jnp.where(here, 1.0, covered)
            touched = jnp.where(wide, 1.0, touched)
            for image in range(IMAGES):
                turned = roll(message, 8 * ty - 1 - 10 * image, 1)
                parts[image] = jnp.where(wide, turned, parts[image])
            for g in range(3):
                sides[g] = jnp.where(here, roll(message, 8 * ty - 100 - 8 * g, 1), sides[g])
            before = live
        marks[tx, 0] = covered
        marks[tx, 1] = touched
        for image in range(IMAGES):
            inner[tx, image] = parts[image]
        for g in range(3):
            outer[tx, g] = sides[g]
        return carry

    lax.fori_loop(1, 7, row_of_tiles, 0)

    def finish(tx, carry):
        above, below = jnp.minimum(tx + 1, 7), jnp.maximum(tx - 1, 0)
        covered = marks[tx, 0] > 0.5
        touched = marks[tx, 1] > 0.5
        beside = (sub == 7) & (marks[above, 0] > 0.5) | (sub == 0) & (marks[below, 0] > 0.5)
        low, high = [outer[above, g] for g in range(3)], [outer[below, g] for g in range(3)]
        for image in range(IMAGES):
            if image < 8:
                lows, highs = low[0][image : image + 1], high[1][image : image + 1]
            else:
                lows, highs = low[2][image - 8 : image - 7], high[2][image - 6 : image - 5]
            rows = pl.ds(pl.multiple_of(image * ROWS + 8 * tx, 8), 8)
            value = inner[tx, image]
            cells = new[rows, :] + jnp.where(touched, value - flux_y[rows, :], 0.0)
            faces = jnp.where(sub == 7, lows, highs)
            cells = cells + jnp.where(beside, faces - flux_x[rows, :], 0.0)
            out[rows, :] = jnp.where(covered, value, cells)
        return carry

    lax.fori_loop(0, 8, finish, 0)


def body(n, m, coarse_state, fine_state, source_rows, tile_ids):
    vmem = pl.BlockSpec(memory_space=pltpu.VMEM)
    smem = pl.BlockSpec(memory_space=pltpu.SMEM)
    hbm = pl.BlockSpec(memory_space=pltpu.HBM)
    f32 = jnp.float32
    coarse = coarse_state.reshape(IMAGES * ROWS, LANES)
    fine = fine_state.reshape(BOXES, 5, 4, 256)
    sources = source_rows.reshape(n, BOXES).T
    tiles = tile_ids.reshape(n, BOXES).T
    shape = jax.ShapeDtypeStruct
    image = shape((IMAGES * ROWS, LANES), f32)
    boxes = shape((BOXES, 5, 4, 256), f32)
    new, flux_x, flux_y, returned, fine_out, wanted = pl.pallas_call(
        functools.partial(level_kernel, n, m),
        out_shape=(
            image,
            image,
            image,
            shape((n, 8, LANES), f32),
            boxes,
            shape((n,), jnp.int32),
        ),
        in_specs=[hbm] * 4,
        out_specs=(vmem,) * 5 + (smem,),
        scratch_shapes=[
            pltpu.SMEM((BOXES, n), jnp.int32),
            pltpu.SMEM((BOXES, n), jnp.int32),
            pltpu.VMEM((2 * IMAGES * ROWS, LANES), f32),
            pltpu.VMEM((BOXES, 5, 4, 256), f32),
            pltpu.VMEM((IMAGES * LANES, LANES), f32),
            pltpu.VMEM((8, 40, LANES), f32),
            pltpu.VMEM((16, 24, LANES), f32),
            pltpu.VMEM((128, 8, LANES), f32),
            pltpu.VMEM((n, 8, LANES), f32),
            pltpu.VMEM((n, 8, LANES), f32),
            pltpu.VMEM((8 * BOXES, LANES), f32),
            pltpu.VMEM((BOXES, 8, LANES), f32),
            pltpu.VMEM((n, 8, LANES), f32),
            pltpu.VMEM((20, BOXES, 256), f32),
            pltpu.VMEM((32, LANES), f32),
            pltpu.VMEM((ROWS, LANES), f32),
            pltpu.VMEM((2, 32, LANES), f32),
            pltpu.VMEM((2, ROWS, LANES), f32),
            pltpu.SemaphoreType.DMA((4,)),
            pltpu.SemaphoreType.DMA((2,)),
            pltpu.SemaphoreType.DMA((2,)),
            pltpu.SemaphoreType.DMA((2, 4)),
        ],
        compiler_params=pltpu.CompilerParams(
            collective_id=0, has_side_effects=True, vmem_limit_bytes=VMEM_LIMIT
        ),
        name="levels",
    )(coarse, fine, sources, tiles)
    out, fine_out = pl.pallas_call(
        functools.partial(merge_kernel, n),
        out_shape=(image, boxes),
        in_specs=[vmem, vmem, vmem, vmem, smem, vmem],
        out_specs=(vmem,) * 2,
        scratch_shapes=[
            pltpu.SMEM((128,), jnp.int32),
            pltpu.VMEM((8, 2, 8, LANES), f32),
            pltpu.VMEM((8, 3, 8, LANES), f32),
            pltpu.VMEM((8, IMAGES, 8, LANES), f32),
        ],
        compiler_params=pltpu.CompilerParams(vmem_limit_bytes=VMEM_LIMIT),
        name="merge",
    )(new, flux_x, flux_y, returned, wanted, fine_out)
    return out.reshape(coarse_state.shape), fine_out.reshape(fine_state.shape)


def solution(mesh):
    return jax.shard_map(
        functools.partial(body, mesh.shape["gx"], mesh.shape["gy"]),
        mesh=mesh,
        in_specs=(
            P(None, None, "gx", "gy"),
            P("gx", "gy", None, None, None, None),
            P(None, "gy", None),
            P(None, "gy", None),
        ),
        out_specs=(P(None, None, "gx", "gy"), P("gx", "gy", None, None, None, None)),
        check_vma=False,
    )
```

```python
import functools

import jax
import jax.numpy as jnp
from jax import lax
from jax.experimental import pallas as pl
from jax.experimental.pallas import tpu as pltpu
from jax.sharding import PartitionSpec as P

MESH = pl.DeviceIdType.MESH
HEAT_RATIO = 1.4
HALF_STEP = 0.025
BOXES = 8
IMAGES = 10
ROWS = 64
LANES = 128
VMEM_LIMIT = 65280 * 1024


def iota(shape, dim):
    return lax.broadcasted_iota(jnp.int32, shape, dim)


def roll(x, shift, axis):
    if isinstance(shift, int):
        shift = shift % x.shape[axis]
        if shift == 0:
            return x
    return pltpu.roll(x, shift, axis)


def select_dot(values, weights):
    x = jnp.concatenate(values, axis=0)
    high = x.astype(jnp.bfloat16)
    x = x - high.astype(jnp.float32)
    middle = x.astype(jnp.bfloat16)
    low = (x - middle.astype(jnp.float32)).astype(jnp.bfloat16)
    parts = [
        jnp.dot(part, weights, preferred_element_type=jnp.float32) for part in (low, middle, high)
    ]
    return parts[0] + parts[1] + parts[2]


def primitives(u):
    inverse = 1.0 / u[0]
    velocity = [u[1] * inverse, u[2] * inverse, u[3] * inverse]
    kinetic = 0.5 * (u[1] * velocity[0] + u[2] * velocity[1] + u[3] * velocity[2])
    pressure = (HEAT_RATIO - 1.0) * (u[4] - kinetic)
    sound = jnp.sqrt(HEAT_RATIO * pressure * inverse)
    return velocity, pressure, sound


def scaled_state(u, velocity, pressure, sound, k):
    drift = HALF_STEP * velocity[k]
    speed = HALF_STEP * (jnp.abs(velocity[k]) + sound)
    return list(u) + [pressure, drift, speed]


def scaled_flux(state, k):
    u, pressure, drift = state[:5], state[5], state[6]
    flux = [u[f] * drift for f in range(5)]
    flux[1 + k] = flux[1 + k] + HALF_STEP * pressure
    flux[4] = (u[4] + pressure) * drift
    return flux


def face_flux(left, right, k):
    a, b = scaled_flux(left, k), scaled_flux(right, k)
    top = jnp.maximum(left[7], right[7])
    return [(a[f] + b[f]) - top * (right[f] - left[f]) for f in range(5)]


def coarse_step(img, flux_x, flux_y):
    row, col = iota((ROWS, LANES), 0), iota((ROWS, LANES), 1)
    cells, prims = [], []
    for z in range(2):
        u = [img[pl.ds((2 * f + z) * ROWS, ROWS), :] for f in range(5)]
        cells.append(u)
        prims.append(primitives(u))
    depth = [HALF_STEP * (jnp.abs(prims[z][0][0]) + prims[z][2]) for z in range(2)]
    depth = 2.0 * jnp.maximum(depth[0], depth[1])
    for z in range(2):
        u = cells[z]
        new = [u[f] - depth * (u[f] - cells[1 - z][f]) for f in range(5)]
        for k, axis, place, saved in ((1, 0, row, flux_x), (2, 1, col, flux_y)):
            state = scaled_state(u, *prims[z], k)
            before = [roll(s, 1, axis) for s in state]
            faces = face_flux(before, state, k)
            for f in range(5):
                face = jnp.where(place == 0, 0.0, faces[f])
                upper = roll(face, -1, axis)
                signed = jnp.where(place % 8 == 7, -upper, face)
                saved[pl.ds((2 * f + z) * ROWS, ROWS), :] = signed
                new[f] = new[f] - (upper - face)
        for f in range(5):
            img[pl.ds((IMAGES + 2 * f + z) * ROWS, ROWS), :] = new[f]


def build_tables(img, turned, table_x, table_y):
    for tx in range(1, 7):
        for k, row in ((0, 8 * tx - 1), (1, 8 * tx + 8)):
            table_x[tx, pl.ds(16 * k, 8), :] = img[pl.ds(row, 8, stride=ROWS), :]
            table_x[tx, pl.ds(16 * k + 8, 8), :] = img[pl.ds(8 * ROWS + row, 8, stride=ROWS), :]
            table_x[tx, pl.ds(32 + 4 * k, 4), :] = img[pl.ds(16 * ROWS + row, 4, stride=ROWS), :]
    for p in range(IMAGES):
        turned[pl.ds(p * LANES, LANES), :] = jnp.transpose(img[pl.ds(p * LANES, LANES), :])
    for ty in range(1, 15):
        for k, col in ((0, 8 * ty - 1), (1, 8 * ty + 8)):
            table_y[ty, pl.ds(8 * k, 8), :] = turned[pl.ds(col, 8, stride=LANES), :]
            table_y[ty, pl.ds(16 + 2 * k, 2), :] = turned[pl.ds(8 * LANES + col, 2, stride=LANES), :]


def wanted_tile(sources, tiles, o, me):
    tile = jnp.int32(0)
    for r in range(BOXES):
        tile = jnp.where(sources[r, o] == me, tiles[r, o], tile)
    return tile


def pack_rims(n, me, sources, tiles, table_x, table_y, by_tile, rims, wanted, box_of):
    group = iota((8, LANES), 1) // 8
    for tx in range(1, 7):
        for ty in range(1, 15):
            message = jnp.zeros((8, LANES), jnp.float32)
            for g in range(5):
                part = roll(table_x[tx, pl.ds(8 * g, 8), :], 8 * g - 8 * ty, 1)
                message = jnp.where(group == g, part, message)
            for u in range(3):
                columns = table_y[ty, pl.ds(8 * u, 8), :]
                for j in range(2):
                    part = roll(columns, 64 + 16 * u + 8 * j - 64 * j - 8 * tx, 1)
                    message = jnp.where(group == 8 + 2 * u + j, part, message)
            by_tile[16 * tx + ty] = message

    def one(o, carry):
        tile = wanted_tile(sources, tiles, o, me)
        wanted[o] = tile
        rims[o] = by_tile[jnp.maximum(tile, 17)]
        box = jnp.int32(0)
        for r in range(BOXES):
            box = jnp.where(sources[r, me] == o, r, box)
        box_of[o] = box
        return carry

    lax.fori_loop(0, n, one, 0)


def pack_halo(img, halo_rows, halo_cols):
    halo_rows[...] = jnp.zeros_like(halo_rows)
    halo_rows[pl.ds(0, 8), :] = img[pl.ds(0, 8, stride=ROWS), :]
    halo_rows[pl.ds(8, 2), :] = img[pl.ds(8 * ROWS, 2, stride=ROWS), :]
    halo_rows[pl.ds(16, 8), :] = img[pl.ds(ROWS - 1, 8, stride=ROWS), :]
    halo_rows[pl.ds(24, 2), :] = img[pl.ds(9 * ROWS - 1, 2, stride=ROWS), :]
    lane = iota((ROWS, LANES), 1)
    packed = jnp.ones((ROWS, LANES), jnp.float32)
    for image in range(IMAGES):
        cells = img[pl.ds(image * ROWS, ROWS), :]
        packed = jnp.where(lane == image, roll(cells, image, 1), packed)
        packed = jnp.where(lane == 16 + image, roll(cells, 17 + image, 1), packed)
    halo_cols[...] = packed


def finish_edges(img, halo_rows, halo_cols, from_rows, from_cols):
    def by_row(source, start):
        u = [source[pl.ds(start + 2 * f, 2), :] for f in range(5)]
        return scaled_state(u, *primitives(u), 1)

    own_low, own_high = by_row(halo_rows, 0), by_row(halo_rows, 16)
    low = face_flux(by_row(from_rows.at[0], 16), own_low, 1)
    high = face_flux(own_high, by_row(from_rows.at[1], 0), 1)
    for f in range(5):
        for z in range(2):
            base = (IMAGES + 2 * f + z) * ROWS
            first, last = pl.ds(base, 1), pl.ds(base + ROWS - 1, 1)
            img[first, :] = img[first, :] + low[f][z : z + 1]
            img[last, :] = img[last, :] - high[f][z : z + 1]

    lane = iota((ROWS, LANES), 1)
    own = halo_cols[...]
    left = jnp.where(lane < 16, roll(from_cols[0], -16, 1), own)
    right = jnp.where(lane < 16, own, roll(from_cols[1], 16, 1))

    def by_lane(packed):
        u = [roll(packed, -2 * f, 1) for f in range(5)]
        return scaled_state(u, *primitives(u), 2)

    faces = face_flux(by_lane(left), by_lane(right), 2)
    for f in range(5):
        for z in range(2):
            rows = pl.ds((IMAGES + 2 * f + z) * ROWS, ROWS)
            cells = img[rows, :]
            cells = jnp.where(lane == 0, cells + roll(faces[f], -z, 1), cells)
            cells = jnp.where(lane == LANES - 1, cells - roll(faces[f], 111 - z, 1), cells)
            img[rows, :] = cells


def spread_weights(weights):
    source, cell = iota((LANES, 256), 0), iota((LANES, 256), 1)
    a, b = cell // 16, cell % 16
    for side, (along, across) in enumerate(((b, a), (a, b))):
        chosen = (source < 16) & (source % 8 == along // 2) & (source // 8 == across // 8)
        weights[side] = jnp.where(chosen, 1.0, 0.0).astype(jnp.bfloat16)


def gather_weights(weights):
    cell, target = iota((256, LANES), 0), iota((256, LANES), 1)
    a, b = cell // 16, cell % 16
    row, lane = target // 16, target % 16
    average = (row == a // 2) & (lane - 1 == b // 2)
    low_col = (row == a // 2) & (lane == 0) & (b == 0)
    high_col = (row == a // 2) & (lane == 9) & (b == 15)
    low_row = (target == b // 2) & (a == 0)
    high_row = (target == 8 + b // 2) & (a == 15)
    for i, (low, high) in enumerate(((None, average), (low_col, high_col), (low_row, high_row))):
        values = jnp.where(high, 0.125, 0.0)
        if low is not None:
            values = jnp.where(low, -0.125, values)
        weights[i] = values.astype(jnp.bfloat16)


def own_rims(me, sources, rims, held, weights):
    for r in range(BOXES):
        held[pl.ds(8 * r, 8), :] = rims[sources[r, me]]
    by_row = [held[pl.ds(s, BOXES, stride=8), :] for s in range(8)]
    lane = iota((BOXES, LANES), 1)

    def pair(low, low_lane, high, high_lane):
        first = roll(low, -low_lane, 1)
        second = roll(high, 8 - high_lane, 1)
        return jnp.where(lane < 8, first, jnp.where(lane < 16, second, 0.0))

    sides = [[], []]
    for image in range(2 * IMAGES):
        s, g = image % 8, image // 8
        if g < 2:
            sides[0].append(pair(by_row[s], 8 * g, by_row[s], 8 * (g + 2)))
        else:
            sides[0].append(pair(by_row[s], 32, by_row[s + 4], 32))
        p, j = image // 2, image % 2
        if p < 8:
            sides[1].append(pair(by_row[p], 64 + 8 * j, by_row[p], 80 + 8 * j))
        else:
            sides[1].append(pair(by_row[p - 8], 96 + 8 * j, by_row[p - 6], 96 + 8 * j))

    spread = []
    for side in range(2):
        old = sides[side][:IMAGES]
        mid = [0.5 * (x + y) for x, y in zip(old, sides[side][IMAGES:])]
        ghosts = select_dot(old + mid, weights[side])
        spread.append(
            [
                [ghosts[(IMAGES * t + i) * 8 : (IMAGES * t + i) * 8 + 8] for i in range(IMAGES)]
                for t in range(2)
            ]
        )
    return spread


def fine_step(u, ghosts_x, ghosts_y, edges):
    cell = iota((BOXES, 256), 1)
    a, b = cell // 16, cell % 16
    prims = [primitives([u[f][z] for f in range(5)]) for z in range(4)]
    states = [scaled_state([u[f][z] for f in range(5)], *prims[z], 0) for z in range(4)]
    deep = [face_flux(states[z], states[(z + 1) % 4], 0) for z in range(4)]
    new = [[u[f][z] - (deep[z][f] - deep[z - 1][f]) for z in range(4)] for f in range(5)]
    sides = (
        (1, ghosts_x, 16, a == 0, a == 15, a < 8),
        (2, ghosts_y, 1, b == 0, b == 15, b < 8),
    )
    for side, (k, ghosts, stride, first, last, lower) in enumerate(sides):
        for half in range(2):
            cells = [ghosts[2 * f + half] for f in range(5)]
            ghost = scaled_state(cells, *primitives(cells), k)
            for z in (2 * half, 2 * half + 1):
                state = scaled_state([u[f][z] for f in range(5)], *prims[z], k)
                before = [
                    jnp.where(first, ghost[i], roll(state[i], stride, 1)) for i in range(8)
                ]
                low = face_flux(before, state, k)
                outer = face_flux(state, ghost, k)
                for f in range(5):
                    high = jnp.where(last, outer[f], roll(low[f], -stride, 1))
                    new[f][z] = new[f][z] - (high - low[f])
                    edge = jnp.where(lower, low[f], high)
                    held = edges[side][2 * f + half]
                    edges[side][2 * f + half] = edge if held is None else held + edge
    return new


def pack_results(u, edges, weights, held, packed):
    thick = [u[i // 2][2 * (i % 2)] + u[i // 2][2 * (i % 2) + 1] for i in range(IMAGES)]
    inner = select_dot(thick, weights[0])
    inner = inner + select_dot(edges[1], weights[1])
    outer = select_dot(edges[0], weights[2])
    inner = [inner[8 * i : 8 * i + 8] for i in range(IMAGES)]
    outer = [outer[8 * i : 8 * i + 8] for i in range(IMAGES)]
    lane = iota((BOXES, LANES), 1)
    for i in range(8):
        message = roll(outer[i], 100, 1)
        if i < 4:
            last = roll(outer[8 + i % 2], 116 if i < 2 else 108, 1)
            message = jnp.where(lane < 116, message, last)
        for image in range(IMAGES - 1, -1, -1):
            part = roll(inner[image], 10 * image - 16 * i, 1)
            message = jnp.where(lane < 10 * image + 10, part, message)
        held[pl.ds(i, BOXES, stride=8), :] = message
    for r in range(BOXES):
        packed[r] = held[pl.ds(8 * r, 8), :]


def far_first(n):
    side = round(n**0.5)
    steps = [(a, b) for a in range(side) for b in range(side) if a or b]
    return side, sorted(steps, key=lambda s: -sum(min(x, side - x) for x in s))


def partners(n, me):
    side, steps = far_first(n)
    high, low = me // side, lax.rem(me, side)
    for a, b in steps:
        yield lax.rem(high + a, side) * side + lax.rem(low + b, side)


def send(me, other, source, target, sems):
    pltpu.make_async_remote_copy(
        src_ref=source.at[other],
        dst_ref=target.at[me],
        send_sem=sems.at[0],
        recv_sem=sems.at[1],
        device_id={"gx": other},
        device_id_type=MESH,
    ).start()


def all_slots(n, me, source, target, sems):
    return pltpu.make_async_remote_copy(
        src_ref=source.at[pl.ds(0, n - 1)],
        dst_ref=target.at[pl.ds(0, n - 1)],
        send_sem=sems.at[0],
        recv_sem=sems.at[1],
        device_id={"gx": me},
        device_id_type=MESH,
    )


def level_kernel(
    n,
    m,
    coarse,
    fine_in,
    sources_in,
    tiles_in,
    coarse_new,
    flux_x_out,
    flux_y_out,
    returned,
    fine_out,
    wanted_out,
    sources,
    tiles,
    wanted,
    box_of,
    img,
    flux_x,
    flux_y,
    fine,
    turned,
    table_x,
    table_y,
    by_tile,
    rims,
    rims_in,
    held,
    packed,
    results,
    cells,
    halo_rows,
    halo_cols,
    from_rows,
    from_cols,
    spread,
    gather,
    load_sems,
    store_sems,
    rim_sems,
    result_sems,
    halo_sems,
):
    me, column = lax.axis_index("gx"), lax.axis_index("gy")
    up, down = lax.rem(me + 1, n), lax.rem(me + n - 1, n)
    right, left = lax.rem(column + 1, m), lax.rem(column + m - 1, m)
    barrier = pltpu.get_barrier_semaphore()

    for other in partners(n, me):
        pl.semaphore_signal(barrier, 1, device_id={"gx": other}, device_id_type=MESH)
    pl.semaphore_signal(barrier, 1, device_id={"gy": right}, device_id_type=MESH)
    pl.semaphore_signal(barrier, 1, device_id={"gy": left}, device_id_type=MESH)

    old, new = pl.ds(0, IMAGES * ROWS), pl.ds(IMAGES * ROWS, IMAGES * ROWS)
    load = pltpu.make_async_copy(coarse, img.at[old], load_sems.at[0])
    load_fine = pltpu.make_async_copy(fine_in, fine, load_sems.at[1])
    load_sources = pltpu.make_async_copy(sources_in, sources, load_sems.at[2])
    load_tiles = pltpu.make_async_copy(tiles_in, tiles, load_sems.at[3])
    load.start()
    load_sources.start()
    load_tiles.start()
    load_fine.start()
    load.wait()
    coarse_step(img, flux_x, flux_y)
    stores = [
        pltpu.make_async_copy(flux_x, flux_x_out, store_sems.at[0]),
        pltpu.make_async_copy(flux_y, flux_y_out, store_sems.at[1]),
    ]
    stores[0].start()
    stores[1].start()
    table_x[...] = jnp.zeros_like(table_x)
    table_y[...] = jnp.zeros_like(table_y)
    build_tables(img, turned, table_x, table_y)
    load_sources.wait()
    load_tiles.wait()
    pack_rims(n, me, sources, tiles, table_x, table_y, by_tile, rims, wanted, box_of)
    rims_in[me] = rims[me]
    stores.append(pltpu.make_async_copy(wanted, wanted_out, store_sems.at[2]))
    stores[2].start()
    pack_halo(img, halo_rows, halo_cols)
    load_fine.wait()
    for r in range(BOXES):
        for f in range(5):
            for z in range(4):
                cells[4 * f + z, pl.ds(r, 1), :] = fine[r, f, pl.ds(z, 1), :]
    spread_weights(spread)
    gather_weights(gather)
    pl.semaphore_wait(barrier, n + 1)

    for other in partners(n, me):
        send(me, other, rims, rims_in, rim_sems)
    halos = []
    for i, (source, target, where) in enumerate(
        (
            (halo_rows, from_rows.at[0], {"gx": up}),
            (halo_rows, from_rows.at[1], {"gx": down}),
            (halo_cols, from_cols.at[0], {"gy": right}),
            (halo_cols, from_cols.at[1], {"gy": left}),
        )
    ):
        copy = pltpu.make_async_remote_copy(
            src_ref=source,
            dst_ref=target,
            send_sem=halo_sems.at[0, i],
            recv_sem=halo_sems.at[1, i],
            device_id=where,
            device_id_type=MESH,
        )
        copy.start()
        halos.append(copy)

    rim_copies = all_slots(n, me, rims, rims_in, rim_sems)
    rim_copies.wait_recv()
    ghosts = own_rims(me, sources, rims_in, held, spread)
    u = [[cells[4 * f + z] for z in range(4)] for f in range(5)]
    edges = [[None] * IMAGES, [None] * IMAGES]
    u = fine_step(u, ghosts[0][0], ghosts[1][0], edges)
    u = fine_step(u, ghosts[0][1], ghosts[1][1], edges)
    pack_results(u, edges, gather, held, packed)
    for other in partners(n, me):
        results[other] = packed[box_of[other]]
        send(me, other, results, returned, result_sems)
    results[me] = packed[box_of[me]]
    stores.append(pltpu.make_async_copy(results.at[me], returned.at[me], store_sems.at[3]))
    stores[3].start()
    for f in range(5):
        for z in range(4):
            for r in range(BOXES):
                fine[r, f, pl.ds(z, 1), :] = u[f][z][r : r + 1]
    stores.append(pltpu.make_async_copy(fine, fine_out, store_sems.at[4]))
    stores[4].start()
    for copy in halos:
        copy.wait_recv()
    finish_edges(img, halo_rows, halo_cols, from_rows, from_cols)
    stores.append(pltpu.make_async_copy(img.at[new], coarse_new, store_sems.at[5]))
    stores[5].start()
    rim_copies.wait_send()
    for copy in halos:
        copy.wait_send()
    for copy in stores:
        copy.wait()
    result_copies = all_slots(n, me, results, returned, result_sems)
    result_copies.wait_send()
    result_copies.wait_recv()


def merge_kernel(
    n,
    new_in,
    flux_x_in,
    flux_y_in,
    returned_in,
    wanted_in,
    fine_in,
    out_to,
    fine_out,
    new,
    flux_x,
    flux_y,
    returned,
    wanted,
    out,
    slots,
    marks,
    outer,
    inner,
    sems,
    out_sem,
):
    pairs = (
        (wanted_in, wanted),
        (returned_in, returned),
        (new_in, new),
        (flux_x_in, flux_x),
        (flux_y_in, flux_y),
        (fine_in, fine_out),
    )
    loads = [pltpu.make_async_copy(a, b, sems.at[i]) for i, (a, b) in enumerate(pairs)]
    for copy in loads:
        copy.start()
    lane, sub = iota((8, LANES), 1), iota((8, LANES), 0)

    def clear(t, carry):
        slots[t] = -1
        return carry

    def place(o, carry):
        slots[wanted[o]] = o
        return carry

    lax.fori_loop(0, 128, clear, 0, unroll=8)
    loads[0].wait()
    lax.fori_loop(0, n, place, 0, unroll=8)
    blank = jnp.zeros((8, LANES), jnp.float32)
    for tx in (0, 7):
        for i in range(2):
            marks[tx, i] = blank
        for image in range(IMAGES):
            inner[tx, image] = blank
        for g in range(3):
            outer[tx, g] = blank

    def row_of_tiles(tx, carry):
        parts = [blank] * IMAGES
        sides = [blank] * 3
        covered, touched = blank, blank
        before = jnp.int32(0)
        for ty in range(1, 15):
            slot = slots[16 * tx + ty]
            live = (slot >= 0).astype(jnp.int32)
            message = returned[jnp.maximum(slot, 0)]
            here = (lane // 8 == ty) & (lane < 1024 * live)
            first = jnp.where(live > 0, 8 * ty - 1 + before, 1024)
            wide = (lane >= first) & (lane < 8 * ty + 9)
            covered = jnp.where(here, 1.0, covered)
            touched = jnp.where(wide, 1.0, touched)
            for image in range(IMAGES):
                turned = roll(message, 8 * ty - 1 - 10 * image, 1)
                parts[image] = jnp.where(wide, turned, parts[image])
            for g in range(3):
                sides[g] = jnp.where(here, roll(message, 8 * ty - 100 - 8 * g, 1), sides[g])
            before = live
        marks[tx, 0] = covered
        marks[tx, 1] = touched
        for image in range(IMAGES):
            inner[tx, image] = parts[image]
        for g in range(3):
            outer[tx, g] = sides[g]
        return carry

    loads[1].wait()
    lax.fori_loop(1, 7, row_of_tiles, 0)
    for copy in loads[2:5]:
        copy.wait()

    def finish(tx, carry):
        above, below = jnp.minimum(tx + 1, 7), jnp.maximum(tx - 1, 0)
        covered = marks[tx, 0] > 0.5
        touched = marks[tx, 1] > 0.5
        beside = (sub == 7) & (marks[above, 0] > 0.5) | (sub == 0) & (marks[below, 0] > 0.5)
        rows = pl.ds(pl.multiple_of(8 * tx, 8), 8)
        low, high = [outer[above, g] for g in range(3)], [outer[below, g] for g in range(3)]
        for image in range(IMAGES):
            if image < 8:
                lows, highs = low[0][image : image + 1], high[1][image : image + 1]
            else:
                lows, highs = low[2][image - 8 : image - 7], high[2][image - 6 : image - 5]
            value = inner[tx, image]
            cells = new[image, rows, :] + jnp.where(touched, value - flux_y[image, rows, :], 0.0)
            faces = jnp.where(sub == 7, lows, highs)
            cells = cells + jnp.where(beside, faces - flux_x[image, rows, :], 0.0)
            out[image, rows, :] = jnp.where(covered, value, cells)
        pltpu.make_async_copy(out.at[:, rows], out_to.at[:, rows], out_sem).start()
        return carry

    lax.fori_loop(0, 8, finish, 0)
    pltpu.make_async_copy(out, out_to, out_sem).wait()
    loads[5].wait()


def body(n, m, coarse_state, fine_state, source_rows, tile_ids):
    hbm = pl.BlockSpec(memory_space=pltpu.HBM)
    f32 = jnp.float32
    coarse = coarse_state.reshape(IMAGES * ROWS, LANES)
    fine = fine_state.reshape(BOXES, 5, 4, 256)
    sources = source_rows.reshape(n, BOXES).T
    tiles = tile_ids.reshape(n, BOXES).T
    shape = jax.ShapeDtypeStruct
    image = shape((IMAGES * ROWS, LANES), f32)
    boxes = shape((BOXES, 5, 4, 256), f32)
    new, flux_x, flux_y, returned, fine_out, wanted = pl.pallas_call(
        functools.partial(level_kernel, n, m),
        out_shape=(
            image,
            image,
            image,
            shape((n, 8, LANES), f32),
            boxes,
            shape((n,), jnp.int32),
        ),
        in_specs=[hbm] * 4,
        out_specs=(hbm,) * 6,
        scratch_shapes=[
            pltpu.SMEM((BOXES, n), jnp.int32),
            pltpu.SMEM((BOXES, n), jnp.int32),
            pltpu.SMEM((n,), jnp.int32),
            pltpu.SMEM((n,), jnp.int32),
            pltpu.VMEM((2 * IMAGES * ROWS, LANES), f32),
            pltpu.VMEM((IMAGES * ROWS, LANES), f32),
            pltpu.VMEM((IMAGES * ROWS, LANES), f32),
            pltpu.VMEM((BOXES, 5, 4, 256), f32),
            pltpu.VMEM((IMAGES * LANES, LANES), f32),
            pltpu.VMEM((8, 40, LANES), f32),
            pltpu.VMEM((16, 24, LANES), f32),
            pltpu.VMEM((128, 8, LANES), f32),
            pltpu.VMEM((n, 8, LANES), f32),
            pltpu.VMEM((n, 8, LANES), f32),
            pltpu.VMEM((8 * BOXES, LANES), f32),
            pltpu.VMEM((BOXES, 8, LANES), f32),
            pltpu.VMEM((n, 8, LANES), f32),
            pltpu.VMEM((20, BOXES, 256), f32),
            pltpu.VMEM((32, LANES), f32),
            pltpu.VMEM((ROWS, LANES), f32),
            pltpu.VMEM((2, 32, LANES), f32),
            pltpu.VMEM((2, ROWS, LANES), f32),
            pltpu.VMEM((2, LANES, 256), jnp.bfloat16),
            pltpu.VMEM((3, 256, LANES), jnp.bfloat16),
            pltpu.SemaphoreType.DMA((4,)),
            pltpu.SemaphoreType.DMA((6,)),
            pltpu.SemaphoreType.DMA((2,)),
            pltpu.SemaphoreType.DMA((2,)),
            pltpu.SemaphoreType.DMA((2, 4)),
        ],
        compiler_params=pltpu.CompilerParams(
            collective_id=0, has_side_effects=True, vmem_limit_bytes=VMEM_LIMIT
        ),
        name="levels",
    )(coarse, fine, sources, tiles)
    stack = shape((IMAGES, ROWS, LANES), f32)
    field = pltpu.VMEM((IMAGES, ROWS, LANES), f32)
    out, fine_out = pl.pallas_call(
        functools.partial(merge_kernel, n),
        out_shape=(stack, boxes),
        in_specs=[hbm] * 6,
        out_specs=(hbm,) * 2,
        scratch_shapes=[
            field,
            field,
            field,
            pltpu.VMEM((n, 8, LANES), f32),
            pltpu.SMEM((n,), jnp.int32),
            field,
            pltpu.SMEM((128,), jnp.int32),
            pltpu.VMEM((8, 2, 8, LANES), f32),
            pltpu.VMEM((8, 3, 8, LANES), f32),
            pltpu.VMEM((8, IMAGES, 8, LANES), f32),
            pltpu.SemaphoreType.DMA((6,)),
            pltpu.SemaphoreType.DMA,
        ],
        compiler_params=pltpu.CompilerParams(vmem_limit_bytes=VMEM_LIMIT),
        name="merge",
    )(
        new.reshape(stack.shape),
        flux_x.reshape(stack.shape),
        flux_y.reshape(stack.shape),
        returned,
        wanted,
        fine_out,
    )
    return out.reshape(coarse_state.shape), fine_out.reshape(fine_state.shape)


def solution(mesh):
    return jax.shard_map(
        functools.partial(body, mesh.shape["gx"], mesh.shape["gy"]),
        mesh=mesh,
        in_specs=(
            P(None, None, "gx", "gy"),
            P("gx", "gy", None, None, None, None),
            P(None, "gy", None),
            P(None, "gy", None),
        ),
        out_specs=(P(None, None, "gx", "gy"), P("gx", "gy", None, None, None, None)),
        check_vma=False,
    )
```

```python
import functools

import jax
import jax.numpy as jnp
from jax import lax
from jax.experimental import pallas as pl
from jax.experimental.pallas import tpu as pltpu
from jax.sharding import PartitionSpec as P

MESH = pl.DeviceIdType.MESH
HEAT_RATIO = 1.4
HALF_STEP = 0.025
BOXES = 8
IMAGES = 10
ROWS = 64
LANES = 128
VMEM_LIMIT = 65280 * 1024


def iota(shape, dim):
    return lax.broadcasted_iota(jnp.int32, shape, dim)


def roll(x, shift, axis):
    if isinstance(shift, int):
        shift = shift % x.shape[axis]
        if shift == 0:
            return x
    return pltpu.roll(x, shift, axis)


def select_dot(values, weights):
    x = jnp.concatenate(values, axis=0)
    high = x.astype(jnp.bfloat16)
    x = x - high.astype(jnp.float32)
    middle = x.astype(jnp.bfloat16)
    low = (x - middle.astype(jnp.float32)).astype(jnp.bfloat16)
    parts = [
        jnp.dot(part, weights, preferred_element_type=jnp.float32) for part in (low, middle, high)
    ]
    return parts[0] + parts[1] + parts[2]


def primitives(u):
    inverse = 1.0 / u[0]
    velocity = [u[1] * inverse, u[2] * inverse, u[3] * inverse]
    kinetic = 0.5 * (u[1] * velocity[0] + u[2] * velocity[1] + u[3] * velocity[2])
    pressure = (HEAT_RATIO - 1.0) * (u[4] - kinetic)
    sound = jnp.sqrt(HEAT_RATIO * pressure * inverse)
    return velocity, pressure, sound


def scaled_state(u, velocity, pressure, sound, k):
    drift = HALF_STEP * velocity[k]
    speed = HALF_STEP * (jnp.abs(velocity[k]) + sound)
    return list(u) + [pressure, drift, speed]


def scaled_flux(state, k):
    u, pressure, drift = state[:5], state[5], state[6]
    flux = [u[f] * drift for f in range(5)]
    flux[1 + k] = flux[1 + k] + HALF_STEP * pressure
    flux[4] = (u[4] + pressure) * drift
    return flux


def face_flux(left, right, k):
    a, b = scaled_flux(left, k), scaled_flux(right, k)
    top = jnp.maximum(left[7], right[7])
    return [(a[f] + b[f]) - top * (right[f] - left[f]) for f in range(5)]


def coarse_step(img, flux_x, flux_y):
    row, col = iota((ROWS, LANES), 0), iota((ROWS, LANES), 1)
    cells, prims = [], []
    for z in range(2):
        u = [img[pl.ds((2 * f + z) * ROWS, ROWS), :] for f in range(5)]
        cells.append(u)
        prims.append(primitives(u))
    depth = [HALF_STEP * (jnp.abs(prims[z][0][0]) + prims[z][2]) for z in range(2)]
    depth = 2.0 * jnp.maximum(depth[0], depth[1])
    for z in range(2):
        u = cells[z]
        new = [u[f] - depth * (u[f] - cells[1 - z][f]) for f in range(5)]
        for k, axis, place, saved in ((1, 0, row, flux_x), (2, 1, col, flux_y)):
            state = scaled_state(u, *prims[z], k)
            before = [roll(s, 1, axis) for s in state]
            faces = face_flux(before, state, k)
            for f in range(5):
                face = jnp.where(place == 0, 0.0, faces[f])
                upper = roll(face, -1, axis)
                signed = jnp.where(place % 8 == 7, -upper, face)
                saved[pl.ds((2 * f + z) * ROWS, ROWS), :] = signed
                new[f] = new[f] - (upper - face)
        for f in range(5):
            img[pl.ds((IMAGES + 2 * f + z) * ROWS, ROWS), :] = new[f]


def build_tables(img, turned, table_x, table_y):
    for tx in range(1, 7):
        for k, row in ((0, 8 * tx - 1), (1, 8 * tx + 8)):
            table_x[tx, pl.ds(16 * k, 8), :] = img[pl.ds(row, 8, stride=ROWS), :]
            table_x[tx, pl.ds(16 * k + 8, 8), :] = img[pl.ds(8 * ROWS + row, 8, stride=ROWS), :]
            table_x[tx, pl.ds(32 + 4 * k, 4), :] = img[pl.ds(16 * ROWS + row, 4, stride=ROWS), :]
    for p in range(IMAGES):
        turned[pl.ds(p * LANES, LANES), :] = jnp.transpose(img[pl.ds(p * LANES, LANES), :])
    for ty in range(1, 15):
        for k, col in ((0, 8 * ty - 1), (1, 8 * ty + 8)):
            table_y[ty, pl.ds(8 * k, 8), :] = turned[pl.ds(col, 8, stride=LANES), :]
            table_y[ty, pl.ds(16 + 2 * k, 2), :] = turned[pl.ds(8 * LANES + col, 2, stride=LANES), :]


def wanted_tile(sources, tiles, o, me):
    tile = jnp.int32(0)
    for r in range(BOXES):
        tile = jnp.where(sources[r, o] == me, tiles[r, o], tile)
    return tile


def pack_rims(n, me, sources, tiles, table_x, table_y, by_tile, rims, wanted, box_of):
    group = iota((8, LANES), 1) // 8
    for tx in range(1, 7):
        for ty in range(1, 15):
            message = jnp.zeros((8, LANES), jnp.float32)
            for g in range(5):
                part = roll(table_x[tx, pl.ds(8 * g, 8), :], 8 * g - 8 * ty, 1)
                message = jnp.where(group == g, part, message)
            for u in range(3):
                columns = table_y[ty, pl.ds(8 * u, 8), :]
                for j in range(2):
                    part = roll(columns, 64 + 16 * u + 8 * j - 64 * j - 8 * tx, 1)
                    message = jnp.where(group == 8 + 2 * u + j, part, message)
            by_tile[16 * tx + ty] = message

    def one(o, carry):
        tile = wanted_tile(sources, tiles, o, me)
        wanted[o] = tile
        rims[o] = by_tile[jnp.maximum(tile, 17)]
        box = jnp.int32(0)
        for r in range(BOXES):
            box = jnp.where(sources[r, me] == o, r, box)
        box_of[o] = box
        return carry

    lax.fori_loop(0, n, one, 0)


def pack_halo(img, halo_rows, halo_cols):
    halo_rows[...] = jnp.zeros_like(halo_rows)
    halo_rows[pl.ds(0, 8), :] = img[pl.ds(0, 8, stride=ROWS), :]
    halo_rows[pl.ds(8, 2), :] = img[pl.ds(8 * ROWS, 2, stride=ROWS), :]
    halo_rows[pl.ds(16, 8), :] = img[pl.ds(ROWS - 1, 8, stride=ROWS), :]
    halo_rows[pl.ds(24, 2), :] = img[pl.ds(9 * ROWS - 1, 2, stride=ROWS), :]
    lane = iota((ROWS, LANES), 1)
    packed = jnp.ones((ROWS, LANES), jnp.float32)
    for image in range(IMAGES):
        cells = img[pl.ds(image * ROWS, ROWS), :]
        packed = jnp.where(lane == image, roll(cells, image, 1), packed)
        packed = jnp.where(lane == 16 + image, roll(cells, 17 + image, 1), packed)
    halo_cols[...] = packed


def finish_edges(img, halo_rows, halo_cols, from_rows, from_cols):
    def by_row(source, start):
        u = [source[pl.ds(start + 2 * f, 2), :] for f in range(5)]
        return scaled_state(u, *primitives(u), 1)

    own_low, own_high = by_row(halo_rows, 0), by_row(halo_rows, 16)
    low = face_flux(by_row(from_rows.at[0], 16), own_low, 1)
    high = face_flux(own_high, by_row(from_rows.at[1], 0), 1)
    for f in range(5):
        for z in range(2):
            base = (IMAGES + 2 * f + z) * ROWS
            first, last = pl.ds(base, 1), pl.ds(base + ROWS - 1, 1)
            img[first, :] = img[first, :] + low[f][z : z + 1]
            img[last, :] = img[last, :] - high[f][z : z + 1]

    lane = iota((ROWS, LANES), 1)
    own = halo_cols[...]
    left = jnp.where(lane < 16, roll(from_cols[0], -16, 1), own)
    right = jnp.where(lane < 16, own, roll(from_cols[1], 16, 1))

    def by_lane(packed):
        u = [roll(packed, -2 * f, 1) for f in range(5)]
        return scaled_state(u, *primitives(u), 2)

    faces = face_flux(by_lane(left), by_lane(right), 2)
    for f in range(5):
        for z in range(2):
            rows = pl.ds((IMAGES + 2 * f + z) * ROWS, ROWS)
            cells = img[rows, :]
            cells = jnp.where(lane == 0, cells + roll(faces[f], -z, 1), cells)
            cells = jnp.where(lane == LANES - 1, cells - roll(faces[f], 111 - z, 1), cells)
            img[rows, :] = cells


def spread_weights(weights):
    source, cell = iota((LANES, 256), 0), iota((LANES, 256), 1)
    a, b = cell // 16, cell % 16
    for side, (along, across) in enumerate(((b, a), (a, b))):
        chosen = (source < 16) & (source % 8 == along // 2) & (source // 8 == across // 8)
        weights[side] = jnp.where(chosen, 1.0, 0.0).astype(jnp.bfloat16)


def gather_weights(weights):
    source, target = iota((512, LANES), 0), iota((512, LANES), 1)
    cell, half = source % 256, source // 256
    a, b = cell // 16, cell % 16
    row, lane = target // 16 == a // 2, target % 16
    average = row & (lane == 8 * half + b // 2)
    low_col = row & (lane == 2 * half) & (b == 0)
    high_col = row & (lane == 2 * half + 1) & (b == 15)
    low_row = (target == 16 * half + b // 2) & (a == 0)
    high_row = (target == 16 * half + 8 + b // 2) & (a == 15)
    for i, (low, high) in enumerate(((None, average), (low_col, high_col), (low_row, high_row))):
        values = jnp.where(high, 0.125, 0.0)
        if low is not None:
            values = jnp.where(low, -0.125, values)
        weights[i] = values.astype(jnp.bfloat16)


def own_rims(me, sources, rims, held, weights):
    for r in range(BOXES):
        held[pl.ds(8 * r, 8), :] = rims[sources[r, me]]
    by_row = [held[pl.ds(s, BOXES, stride=8), :] for s in range(8)]
    lane = iota((BOXES, LANES), 1)

    def pair(low, low_lane, high, high_lane):
        first = roll(low, -low_lane, 1)
        second = roll(high, 8 - high_lane, 1)
        return jnp.where(lane < 8, first, jnp.where(lane < 16, second, 0.0))

    sides = [[], []]
    for image in range(2 * IMAGES):
        s, g = image % 8, image // 8
        if g < 2:
            sides[0].append(pair(by_row[s], 8 * g, by_row[s], 8 * (g + 2)))
        else:
            sides[0].append(pair(by_row[s], 32, by_row[s + 4], 32))
        p, j = image // 2, image % 2
        if p < 8:
            sides[1].append(pair(by_row[p], 64 + 8 * j, by_row[p], 80 + 8 * j))
        else:
            sides[1].append(pair(by_row[p - 8], 96 + 8 * j, by_row[p - 6], 96 + 8 * j))

    spread = []
    for side in range(2):
        old = sides[side][:IMAGES]
        mid = [0.5 * (x + y) for x, y in zip(old, sides[side][IMAGES:])]
        ghosts = select_dot(old + mid, weights[side])
        spread.append(
            [
                [ghosts[(IMAGES * t + i) * 8 : (IMAGES * t + i) * 8 + 8] for i in range(IMAGES)]
                for t in range(2)
            ]
        )
    return spread


def fine_step(u, ghosts_x, ghosts_y, edges):
    cell = iota((BOXES, 256), 1)
    a, b = cell // 16, cell % 16
    prims = [primitives([u[f][z] for f in range(5)]) for z in range(4)]
    states = [scaled_state([u[f][z] for f in range(5)], *prims[z], 0) for z in range(4)]
    deep = [face_flux(states[z], states[(z + 1) % 4], 0) for z in range(4)]
    new = [[u[f][z] - (deep[z][f] - deep[z - 1][f]) for z in range(4)] for f in range(5)]
    sides = (
        (1, ghosts_x, 16, a == 0, a == 15, a < 8),
        (2, ghosts_y, 1, b == 0, b == 15, b < 8),
    )
    for side, (k, ghosts, stride, first, last, lower) in enumerate(sides):
        for half in range(2):
            cells = [ghosts[2 * f + half] for f in range(5)]
            ghost = scaled_state(cells, *primitives(cells), k)
            for z in (2 * half, 2 * half + 1):
                state = scaled_state([u[f][z] for f in range(5)], *prims[z], k)
                before = [
                    jnp.where(first, ghost[i], roll(state[i], stride, 1)) for i in range(8)
                ]
                low = face_flux(before, state, k)
                outer = face_flux(state, ghost, k)
                for f in range(5):
                    high = jnp.where(last, outer[f], roll(low[f], -stride, 1))
                    new[f][z] = new[f][z] - (high - low[f])
                    edge = jnp.where(lower, low[f], high)
                    held = edges[side][2 * f + half]
                    edges[side][2 * f + half] = edge if held is None else held + edge
    return new


def pack_results(u, edges, weights, held, packed):
    thick = [u[i // 2][2 * (i % 2)] + u[i // 2][2 * (i % 2) + 1] for i in range(IMAGES)]

    def pairs(values, i):
        rows = [jnp.concatenate(values[2 * p : 2 * p + 2], axis=1) for p in range(5)]
        sums = select_dot(rows, weights[i])
        return [sums[8 * p : 8 * p + 8] for p in range(5)]

    inner, cols, rows = pairs(thick, 0), pairs(edges[1], 1), pairs(edges[0], 2)
    lane = iota((BOXES, LANES), 1)
    first_cols = cols[0]
    for p in range(1, 4):
        first_cols = jnp.where(lane % 16 // 4 == p, roll(cols[p], 4 * p, 1), first_cols)
    for i in range(8):
        message = roll(cols[4], 120 - 16 * i, 1)
        message = jnp.where(lane < 120, roll(first_cols, 104 - 16 * i, 1), message)
        if i < 4:
            start = 16 * (i % 2) + 8 * (i // 2)
            message = jnp.where(lane < 104, roll(rows[4], 96 - start, 1), message)
        message = jnp.where(lane < 96, roll(rows[i // 2], 80 - 16 * (i % 2), 1), message)
        for p in range(4, -1, -1):
            part = roll(inner[p], 16 * (p - i), 1)
            message = jnp.where(lane < 16 * p + 16, part, message)
        held[pl.ds(i, BOXES, stride=8), :] = message
    for r in range(BOXES):
        packed[r] = held[pl.ds(8 * r, 8), :]


def far_first(n):
    side = round(n**0.5)
    steps = [(a, b) for a in range(side) for b in range(side) if a or b]
    return side, sorted(steps, key=lambda s: -sum(min(x, side - x) for x in s))


def partners(n, me):
    side, steps = far_first(n)
    high, low = me // side, lax.rem(me, side)
    for a, b in steps:
        yield lax.rem(high + a, side) * side + lax.rem(low + b, side)


def send(me, other, source, target, sems):
    pltpu.make_async_remote_copy(
        src_ref=source.at[other],
        dst_ref=target.at[me],
        send_sem=sems.at[0],
        recv_sem=sems.at[1],
        device_id={"gx": other},
        device_id_type=MESH,
    ).start()


def all_slots(n, me, source, target, sems):
    return pltpu.make_async_remote_copy(
        src_ref=source.at[pl.ds(0, n - 1)],
        dst_ref=target.at[pl.ds(0, n - 1)],
        send_sem=sems.at[0],
        recv_sem=sems.at[1],
        device_id={"gx": me},
        device_id_type=MESH,
    )


def level_kernel(
    n,
    m,
    coarse,
    fine_in,
    sources_in,
    tiles_in,
    coarse_new,
    flux_x_out,
    flux_y_out,
    returned,
    fine_out,
    wanted_out,
    sources,
    tiles,
    wanted,
    box_of,
    img,
    flux_x,
    flux_y,
    fine,
    turned,
    table_x,
    table_y,
    by_tile,
    rims,
    rims_in,
    held,
    packed,
    results,
    cells,
    halo_rows,
    halo_cols,
    from_rows,
    from_cols,
    spread,
    gather,
    load_sems,
    store_sems,
    rim_sems,
    result_sems,
    halo_sems,
):
    me, column = lax.axis_index("gx"), lax.axis_index("gy")
    up, down = lax.rem(me + 1, n), lax.rem(me + n - 1, n)
    right, left = lax.rem(column + 1, m), lax.rem(column + m - 1, m)
    barrier = pltpu.get_barrier_semaphore()

    for other in partners(n, me):
        pl.semaphore_signal(barrier, 1, device_id={"gx": other}, device_id_type=MESH)
    pl.semaphore_signal(barrier, 1, device_id={"gy": right}, device_id_type=MESH)
    pl.semaphore_signal(barrier, 1, device_id={"gy": left}, device_id_type=MESH)

    old, new = pl.ds(0, IMAGES * ROWS), pl.ds(IMAGES * ROWS, IMAGES * ROWS)
    load = pltpu.make_async_copy(coarse, img.at[old], load_sems.at[0])
    load_fine = pltpu.make_async_copy(fine_in, fine, load_sems.at[1])
    load_sources = pltpu.make_async_copy(sources_in, sources, load_sems.at[2])
    load_tiles = pltpu.make_async_copy(tiles_in, tiles, load_sems.at[3])
    load.start()
    load_sources.start()
    load_tiles.start()
    load_fine.start()
    load.wait()
    coarse_step(img, flux_x, flux_y)
    stores = [
        pltpu.make_async_copy(flux_x, flux_x_out, store_sems.at[0]),
        pltpu.make_async_copy(flux_y, flux_y_out, store_sems.at[1]),
    ]
    stores[0].start()
    stores[1].start()
    table_x[...] = jnp.zeros_like(table_x)
    table_y[...] = jnp.zeros_like(table_y)
    build_tables(img, turned, table_x, table_y)
    load_sources.wait()
    load_tiles.wait()
    pack_rims(n, me, sources, tiles, table_x, table_y, by_tile, rims, wanted, box_of)
    rims_in[me] = rims[me]
    stores.append(pltpu.make_async_copy(wanted, wanted_out, store_sems.at[2]))
    stores[2].start()
    pack_halo(img, halo_rows, halo_cols)
    load_fine.wait()
    for r in range(BOXES):
        for f in range(5):
            for z in range(4):
                cells[4 * f + z, pl.ds(r, 1), :] = fine[r, f, pl.ds(z, 1), :]
    spread_weights(spread)
    gather_weights(gather)
    pl.semaphore_wait(barrier, n + 1)

    for other in partners(n, me):
        send(me, other, rims, rims_in, rim_sems)
    halos = []
    for i, (source, target, where) in enumerate(
        (
            (halo_rows, from_rows.at[0], {"gx": up}),
            (halo_rows, from_rows.at[1], {"gx": down}),
            (halo_cols, from_cols.at[0], {"gy": right}),
            (halo_cols, from_cols.at[1], {"gy": left}),
        )
    ):
        copy = pltpu.make_async_remote_copy(
            src_ref=source,
            dst_ref=target,
            send_sem=halo_sems.at[0, i],
            recv_sem=halo_sems.at[1, i],
            device_id=where,
            device_id_type=MESH,
        )
        copy.start()
        halos.append(copy)

    rim_copies = all_slots(n, me, rims, rims_in, rim_sems)
    rim_copies.wait_recv()
    ghosts = own_rims(me, sources, rims_in, held, spread)
    u = [[cells[4 * f + z] for z in range(4)] for f in range(5)]
    edges = [[None] * IMAGES, [None] * IMAGES]
    u = fine_step(u, ghosts[0][0], ghosts[1][0], edges)
    u = fine_step(u, ghosts[0][1], ghosts[1][1], edges)
    pack_results(u, edges, gather, held, packed)
    for other in partners(n, me):
        results[other] = packed[box_of[other]]
        send(me, other, results, returned, result_sems)
    results[me] = packed[box_of[me]]
    stores.append(pltpu.make_async_copy(results.at[me], returned.at[me], store_sems.at[3]))
    stores[3].start()
    for f in range(5):
        for z in range(4):
            for r in range(BOXES):
                fine[r, f, pl.ds(z, 1), :] = u[f][z][r : r + 1]
    stores.append(pltpu.make_async_copy(fine, fine_out, store_sems.at[4]))
    stores[4].start()
    for copy in halos:
        copy.wait_recv()
    finish_edges(img, halo_rows, halo_cols, from_rows, from_cols)
    stores.append(pltpu.make_async_copy(img.at[new], coarse_new, store_sems.at[5]))
    stores[5].start()
    rim_copies.wait_send()
    for copy in halos:
        copy.wait_send()
    for copy in stores:
        copy.wait()
    result_copies = all_slots(n, me, results, returned, result_sems)
    result_copies.wait_send()
    result_copies.wait_recv()


def merge_kernel(
    n,
    new_in,
    flux_x_in,
    flux_y_in,
    returned_in,
    wanted_in,
    fine_in,
    out_to,
    fine_out,
    new,
    flux_x,
    flux_y,
    returned,
    wanted,
    out,
    slots,
    covered_in,
    turned,
    fine,
    sems,
    out_sem,
    fine_sem,
):
    pairs = (
        (wanted_in, wanted),
        (returned_in, returned),
        (new_in, new),
        (flux_x_in, flux_x),
        (flux_y_in, flux_y),
        (fine_in, fine),
    )
    loads = [pltpu.make_async_copy(a, b, sems.at[i]) for i, (a, b) in enumerate(pairs)]
    for copy in loads:
        copy.start()
    lane, sub = iota((8, LANES), 1), iota((8, LANES), 0)

    def clear(t, carry):
        slots[t] = -1
        return carry

    def place(o, carry):
        slots[wanted[o]] = o
        return carry

    lax.fori_loop(0, 128, clear, 0, unroll=8)
    loads[0].wait()
    lax.fori_loop(0, n, place, 0, unroll=8)
    blank = jnp.zeros((8, LANES), jnp.float32)
    group = lane // 8
    for tx in (0, 7):
        covered_in[tx] = blank
        for i in range(16):
            turned[tx, i] = blank
    loads[5].wait()
    store_fine = pltpu.make_async_copy(fine, fine_out, fine_sem)
    store_fine.start()

    def row_of_tiles(tx, carry):
        covered = blank
        diagonals = [blank] * 16
        for ty in range(1, 15):
            slot = slots[16 * tx + ty]
            live = (slot >= 0).astype(jnp.int32)
            message = returned[jnp.maximum(slot, 0)]
            covered = jnp.where(lane // 8 == jnp.where(live > 0, ty, -1), 1.0, covered)
            for d in range(16):
                i = (ty - d) % 16
                diagonals[d] = jnp.where(group == i, message, diagonals[d])
        diagonals = [roll(diagonals[d], 8 * d, 1) for d in range(16)]
        covered_in[tx] = covered
        for i in range(16):
            part = blank
            for ty in range(1, 15):
                part = jnp.where(group == ty, diagonals[(ty - i) % 16], part)
            turned[tx, i] = part
        return carry

    loads[1].wait()
    lax.fori_loop(1, 7, row_of_tiles, 0)
    for copy in loads[2:5]:
        copy.wait()

    def finish(tx, carry):
        above, below = jnp.minimum(tx + 1, 7), jnp.maximum(tx - 1, 0)
        cover = covered_in[tx]
        covered = cover > 0.5
        last = lane % 8 == 7
        touched = last & (roll(cover, -1, 1) > 0.5) | (lane % 8 == 0) & (roll(cover, 1, 1) > 0.5)
        beside = (sub == 7) & (covered_in[above] > 0.5) | (sub == 0) & (covered_in[below] > 0.5)
        rows = pl.ds(pl.multiple_of(8 * tx, 8), 8)
        low, high = [turned[above, 10 + g] for g in range(3)], [turned[below, 10 + g] for g in range(3)]
        cols = [turned[tx, 13 + g] for g in range(3)]
        for image in range(IMAGES):
            if image < 8:
                lows, highs = low[0][image : image + 1], high[1][image : image + 1]
            else:
                lows, highs = low[2][image - 8 : image - 7], high[2][image - 6 : image - 5]
            place = 2 * (image % 4)
            value = cols[image // 4]
            value = jnp.where(last, roll(value, -1 - place, 1), roll(value, 7 - place, 1))
            cells = new[image, rows, :] + jnp.where(touched, value - flux_y[image, rows, :], 0.0)
            faces = jnp.where(sub == 7, lows, highs)
            cells = cells + jnp.where(beside, faces - flux_x[image, rows, :], 0.0)
            out[image, rows, :] = jnp.where(covered, turned[tx, image], cells)
        pltpu.make_async_copy(out.at[:, rows], out_to.at[:, rows], out_sem).start()
        return carry

    lax.fori_loop(0, 8, finish, 0)
    pltpu.make_async_copy(out, out_to, out_sem).wait()
    store_fine.wait()


def body(n, m, coarse_state, fine_state, source_rows, tile_ids):
    hbm = pl.BlockSpec(memory_space=pltpu.HBM)
    f32 = jnp.float32
    coarse = coarse_state.reshape(IMAGES * ROWS, LANES)
    fine = fine_state.reshape(BOXES, 5, 4, 256)
    sources = source_rows.reshape(n, BOXES).T
    tiles = tile_ids.reshape(n, BOXES).T
    shape = jax.ShapeDtypeStruct
    image = shape((IMAGES * ROWS, LANES), f32)
    boxes = shape((BOXES, 5, 4, 256), f32)
    new, flux_x, flux_y, returned, fine_out, wanted = pl.pallas_call(
        functools.partial(level_kernel, n, m),
        out_shape=(
            image,
            image,
            image,
            shape((n, 8, LANES), f32),
            boxes,
            shape((n,), jnp.int32),
        ),
        in_specs=[hbm] * 4,
        out_specs=(hbm,) * 6,
        scratch_shapes=[
            pltpu.SMEM((BOXES, n), jnp.int32),
            pltpu.SMEM((BOXES, n), jnp.int32),
            pltpu.SMEM((n,), jnp.int32),
            pltpu.SMEM((n,), jnp.int32),
            pltpu.VMEM((2 * IMAGES * ROWS, LANES), f32),
            pltpu.VMEM((IMAGES * ROWS, LANES), f32),
            pltpu.VMEM((IMAGES * ROWS, LANES), f32),
            pltpu.VMEM((BOXES, 5, 4, 256), f32),
            pltpu.VMEM((IMAGES * LANES, LANES), f32),
            pltpu.VMEM((8, 40, LANES), f32),
            pltpu.VMEM((16, 24, LANES), f32),
            pltpu.VMEM((128, 8, LANES), f32),
            pltpu.VMEM((n, 8, LANES), f32),
            pltpu.VMEM((n, 8, LANES), f32),
            pltpu.VMEM((8 * BOXES, LANES), f32),
            pltpu.VMEM((BOXES, 8, LANES), f32),
            pltpu.VMEM((n, 8, LANES), f32),
            pltpu.VMEM((20, BOXES, 256), f32),
            pltpu.VMEM((32, LANES), f32),
            pltpu.VMEM((ROWS, LANES), f32),
            pltpu.VMEM((2, 32, LANES), f32),
            pltpu.VMEM((2, ROWS, LANES), f32),
            pltpu.VMEM((2, LANES, 256), jnp.bfloat16),
            pltpu.VMEM((3, 512, LANES), jnp.bfloat16),
            pltpu.SemaphoreType.DMA((4,)),
            pltpu.SemaphoreType.DMA((6,)),
            pltpu.SemaphoreType.DMA((2,)),
            pltpu.SemaphoreType.DMA((2,)),
            pltpu.SemaphoreType.DMA((2, 4)),
        ],
        compiler_params=pltpu.CompilerParams(
            collective_id=0, has_side_effects=True, vmem_limit_bytes=VMEM_LIMIT
        ),
        name="levels",
    )(coarse, fine, sources, tiles)
    stack = shape((IMAGES, ROWS, LANES), f32)
    field = pltpu.VMEM((IMAGES, ROWS, LANES), f32)
    out, fine_out = pl.pallas_call(
        functools.partial(merge_kernel, n),
        out_shape=(stack, boxes),
        in_specs=[hbm] * 6,
        out_specs=(hbm,) * 2,
        scratch_shapes=[
            field,
            field,
            field,
            pltpu.VMEM((n, 8, LANES), f32),
            pltpu.SMEM((n,), jnp.int32),
            field,
            pltpu.SMEM((128,), jnp.int32),
            pltpu.VMEM((8, 8, LANES), f32),
            pltpu.VMEM((8, 16, 8, LANES), f32),
            pltpu.VMEM((BOXES, 5, 4, 256), f32),
            pltpu.SemaphoreType.DMA((6,)),
            pltpu.SemaphoreType.DMA,
            pltpu.SemaphoreType.DMA,
        ],
        compiler_params=pltpu.CompilerParams(vmem_limit_bytes=VMEM_LIMIT),
        name="merge",
    )(
        new.reshape(stack.shape),
        flux_x.reshape(stack.shape),
        flux_y.reshape(stack.shape),
        returned,
        wanted,
        fine_out,
    )
    return out.reshape(coarse_state.shape), fine_out.reshape(fine_state.shape)


def solution(mesh):
    return jax.shard_map(
        functools.partial(body, mesh.shape["gx"], mesh.shape["gy"]),
        mesh=mesh,
        in_specs=(
            P(None, None, "gx", "gy"),
            P("gx", "gy", None, None, None, None),
            P(None, "gy", None),
            P(None, "gy", None),
        ),
        out_specs=(P(None, None, "gx", "gy"), P("gx", "gy", None, None, None, None)),
        check_vma=False,
    )
```

```python
import functools

import jax
import jax.numpy as jnp
from jax import lax
from jax.experimental import pallas as pl
from jax.experimental.pallas import tpu as pltpu
from jax.sharding import PartitionSpec as P

MESH = pl.DeviceIdType.MESH
HEAT_RATIO = 1.4
HALF_STEP = 0.025
BOXES = 8
IMAGES = 10
ROWS = 64
LANES = 128
VMEM_LIMIT = 65280 * 1024


def iota(shape, dim):
    return lax.broadcasted_iota(jnp.int32, shape, dim)


def roll(x, shift, axis):
    if isinstance(shift, int):
        shift = shift % x.shape[axis]
        if shift == 0:
            return x
    return pltpu.roll(x, shift, axis)


def select_dot(values, weights):
    x = jnp.concatenate(values, axis=0)
    high = x.astype(jnp.bfloat16)
    x = x - high.astype(jnp.float32)
    middle = x.astype(jnp.bfloat16)
    low = (x - middle.astype(jnp.float32)).astype(jnp.bfloat16)
    parts = [
        jnp.dot(part, weights, preferred_element_type=jnp.float32) for part in (low, middle, high)
    ]
    return parts[0] + parts[1] + parts[2]


def primitives(u):
    inverse = 1.0 / u[0]
    velocity = [u[1] * inverse, u[2] * inverse, u[3] * inverse]
    kinetic = 0.5 * (u[1] * velocity[0] + u[2] * velocity[1] + u[3] * velocity[2])
    pressure = (HEAT_RATIO - 1.0) * (u[4] - kinetic)
    sound = jnp.sqrt(HEAT_RATIO * pressure * inverse)
    return velocity, pressure, sound


def scaled_state(u, velocity, pressure, sound, k):
    drift = HALF_STEP * velocity[k]
    speed = HALF_STEP * (jnp.abs(velocity[k]) + sound)
    return list(u) + [pressure, drift, speed]


def scaled_flux(state, k):
    u, pressure, drift = state[:5], state[5], state[6]
    flux = [u[f] * drift for f in range(5)]
    flux[1 + k] = flux[1 + k] + HALF_STEP * pressure
    flux[4] = (u[4] + pressure) * drift
    return flux


def face_flux(left, right, k):
    a, b = scaled_flux(left, k), scaled_flux(right, k)
    top = jnp.maximum(left[7], right[7])
    return [(a[f] + b[f]) - top * (right[f] - left[f]) for f in range(5)]


def coarse_step(img, flux_x, flux_y):
    row, col = iota((ROWS, LANES), 0), iota((ROWS, LANES), 1)
    cells, prims = [], []
    for z in range(2):
        u = [img[pl.ds((2 * f + z) * ROWS, ROWS), :] for f in range(5)]
        cells.append(u)
        prims.append(primitives(u))
    depth = [HALF_STEP * (jnp.abs(prims[z][0][0]) + prims[z][2]) for z in range(2)]
    depth = 2.0 * jnp.maximum(depth[0], depth[1])
    for z in range(2):
        u = cells[z]
        new = [u[f] - depth * (u[f] - cells[1 - z][f]) for f in range(5)]
        for k, axis, place, saved in ((1, 0, row, flux_x), (2, 1, col, flux_y)):
            state = scaled_state(u, *prims[z], k)
            before = [roll(s, 1, axis) for s in state]
            faces = face_flux(before, state, k)
            for f in range(5):
                face = jnp.where(place == 0, 0.0, faces[f])
                upper = roll(face, -1, axis)
                signed = jnp.where(place % 8 == 7, -upper, face)
                saved[pl.ds((2 * f + z) * ROWS, ROWS), :] = signed
                new[f] = new[f] - (upper - face)
        for f in range(5):
            img[pl.ds((IMAGES + 2 * f + z) * ROWS, ROWS), :] = new[f]


def build_tables(img, turned, table_x, table_y):
    for tx in range(1, 7):
        for k, row in ((0, 8 * tx - 1), (1, 8 * tx + 8)):
            for q in range(4):
                rows = img[pl.ds(5 * q * ROWS + row, 5, stride=ROWS), :]
                table_x[tx, 4 * k + q, pl.ds(0, 5), :] = rows
    for p in range(IMAGES):
        turned[pl.ds(p * LANES, LANES), :] = jnp.transpose(img[pl.ds(p * LANES, LANES), :])
    for ty in range(1, 15):
        for k, col in ((0, 8 * ty - 1), (1, 8 * ty + 8)):
            for h in range(2):
                rows = turned[pl.ds(5 * h * LANES + col, 5, stride=LANES), :]
                table_y[ty, 2 * k + h, pl.ds(0, 5), :] = rows


def wanted_tile(sources, tiles, o, me):
    tile = jnp.int32(0)
    for r in range(BOXES):
        tile = jnp.where(sources[r, o] == me, tiles[r, o], tile)
    return tile


def pack_rims(n, me, sources, tiles, table_x, table_y, by_tile, rims, wanted, box_of):
    group = iota((8, LANES), 1) // 8
    for tx in range(1, 7):
        for ty in range(1, 15):
            message = roll(table_x[tx, 0], -8 * ty, 1)
            for g in range(1, 8):
                part = roll(table_x[tx, g], 8 * g - 8 * ty, 1)
                message = jnp.where(group == g, part, message)
            for u in range(4):
                columns = table_y[ty, u]
                for j in range(2):
                    part = roll(columns, 64 + 16 * u + 8 * j - 64 * j - 8 * tx, 1)
                    message = jnp.where(group == 8 + 2 * u + j, part, message)
            by_tile[16 * tx + ty] = message[:5]

    def one(o, carry):
        tile = wanted_tile(sources, tiles, o, me)
        wanted[o] = tile
        rims[o] = by_tile[jnp.maximum(tile, 17)]
        box = jnp.int32(0)
        for r in range(BOXES):
            box = jnp.where(sources[r, me] == o, r, box)
        box_of[o] = box
        return carry

    lax.fori_loop(0, n, one, 0)


def pack_halo(img, halo_rows, halo_cols):
    halo_rows[...] = jnp.zeros_like(halo_rows)
    halo_rows[pl.ds(0, 8), :] = img[pl.ds(0, 8, stride=ROWS), :]
    halo_rows[pl.ds(8, 2), :] = img[pl.ds(8 * ROWS, 2, stride=ROWS), :]
    halo_rows[pl.ds(16, 8), :] = img[pl.ds(ROWS - 1, 8, stride=ROWS), :]
    halo_rows[pl.ds(24, 2), :] = img[pl.ds(9 * ROWS - 1, 2, stride=ROWS), :]
    lane = iota((ROWS, LANES), 1)
    packed = jnp.ones((ROWS, LANES), jnp.float32)
    for image in range(IMAGES):
        cells = img[pl.ds(image * ROWS, ROWS), :]
        packed = jnp.where(lane == image, roll(cells, image, 1), packed)
        packed = jnp.where(lane == 16 + image, roll(cells, 17 + image, 1), packed)
    halo_cols[...] = packed


def finish_edges(img, halo_rows, halo_cols, from_rows, from_cols):
    def by_row(source, start):
        u = [source[pl.ds(start + 2 * f, 2), :] for f in range(5)]
        return scaled_state(u, *primitives(u), 1)

    own_low, own_high = by_row(halo_rows, 0), by_row(halo_rows, 16)
    low = face_flux(by_row(from_rows.at[0], 16), own_low, 1)
    high = face_flux(own_high, by_row(from_rows.at[1], 0), 1)
    for f in range(5):
        for z in range(2):
            base = (IMAGES + 2 * f + z) * ROWS
            first, last = pl.ds(base, 1), pl.ds(base + ROWS - 1, 1)
            img[first, :] = img[first, :] + low[f][z : z + 1]
            img[last, :] = img[last, :] - high[f][z : z + 1]

    lane = iota((ROWS, LANES), 1)
    own = halo_cols[...]
    left = jnp.where(lane < 16, roll(from_cols[0], -16, 1), own)
    right = jnp.where(lane < 16, own, roll(from_cols[1], 16, 1))

    def by_lane(packed):
        u = [roll(packed, -2 * f, 1) for f in range(5)]
        return scaled_state(u, *primitives(u), 2)

    faces = face_flux(by_lane(left), by_lane(right), 2)
    for f in range(5):
        for z in range(2):
            rows = pl.ds((IMAGES + 2 * f + z) * ROWS, ROWS)
            cells = img[rows, :]
            cells = jnp.where(lane == 0, cells + roll(faces[f], -z, 1), cells)
            cells = jnp.where(lane == LANES - 1, cells - roll(faces[f], 111 - z, 1), cells)
            img[rows, :] = cells


def spread_weights(weights):
    source, cell = iota((LANES, 256), 0), iota((LANES, 256), 1)
    a, b = cell // 16, cell % 16
    for side, (along, across) in enumerate(((b, a), (a, b))):
        chosen = (source < 16) & (source % 8 == along // 2) & (source // 8 == across // 8)
        weights[side] = jnp.where(chosen, 1.0, 0.0).astype(jnp.bfloat16)


def gather_weights(weights):
    source, target = iota((512, LANES), 0), iota((512, LANES), 1)
    cell, half = source % 256, source // 256
    a, b = cell // 16, cell % 16
    row, lane = target // 16 == a // 2, target % 16
    average = row & (lane == 8 * half + b // 2)
    low_col = row & (lane == 2 * half) & (b == 0)
    high_col = row & (lane == 2 * half + 1) & (b == 15)
    low_row = (target == 16 * half + b // 2) & (a == 0)
    high_row = (target == 16 * half + 8 + b // 2) & (a == 15)
    for i, (low, high) in enumerate(((None, average), (low_col, high_col), (low_row, high_row))):
        values = jnp.where(high, 0.125, 0.0)
        if low is not None:
            values = jnp.where(low, -0.125, values)
        weights[i] = values.astype(jnp.bfloat16)


def own_rims(me, sources, rims, held, weights):
    for r in range(BOXES):
        held[pl.ds(8 * r, 5), :] = rims[sources[r, me]]
    by_row = [held[pl.ds(s, BOXES, stride=8), :] for s in range(5)]
    lane = iota((BOXES, LANES), 1)

    def pair(low, low_lane, high, high_lane):
        first = roll(low, -low_lane, 1)
        second = roll(high, 8 - high_lane, 1)
        return jnp.where(lane < 8, first, jnp.where(lane < 16, second, 0.0))

    sides = [[], []]
    for image in range(2 * IMAGES):
        row, q = by_row[image % 5], image // 5
        sides[0].append(pair(row, 8 * q, row, 32 + 8 * q))
        p, j = image // 2, image % 2
        row, lane_j = by_row[p % 5], 16 * (p // 5) + 8 * j
        sides[1].append(pair(row, 64 + lane_j, row, 96 + lane_j))

    spread = []
    for side in range(2):
        old = sides[side][:IMAGES]
        mid = [0.5 * (x + y) for x, y in zip(old, sides[side][IMAGES:])]
        ghosts = select_dot(old + mid, weights[side])
        spread.append(
            [
                [ghosts[(IMAGES * t + i) * 8 : (IMAGES * t + i) * 8 + 8] for i in range(IMAGES)]
                for t in range(2)
            ]
        )
    return spread


def fine_step(u, ghosts_x, ghosts_y, edges):
    cell = iota((BOXES, 256), 1)
    a, b = cell // 16, cell % 16
    prims = [primitives([u[f][z] for f in range(5)]) for z in range(4)]
    states = [scaled_state([u[f][z] for f in range(5)], *prims[z], 0) for z in range(4)]
    deep = [face_flux(states[z], states[(z + 1) % 4], 0) for z in range(4)]
    new = [[u[f][z] - (deep[z][f] - deep[z - 1][f]) for z in range(4)] for f in range(5)]
    sides = (
        (1, ghosts_x, 16, a == 0, a == 15, a < 8),
        (2, ghosts_y, 1, b == 0, b == 15, b < 8),
    )
    for side, (k, ghosts, stride, first, last, lower) in enumerate(sides):
        for half in range(2):
            cells = [ghosts[2 * f + half] for f in range(5)]
            ghost = scaled_state(cells, *primitives(cells), k)
            for z in (2 * half, 2 * half + 1):
                state = scaled_state([u[f][z] for f in range(5)], *prims[z], k)
                before = [
                    jnp.where(first, ghost[i], roll(state[i], stride, 1)) for i in range(8)
                ]
                low = face_flux(before, state, k)
                outer = face_flux(state, ghost, k)
                for f in range(5):
                    high = jnp.where(last, outer[f], roll(low[f], -stride, 1))
                    new[f][z] = new[f][z] - (high - low[f])
                    edge = jnp.where(lower, low[f], high)
                    held = edges[side][2 * f + half]
                    edges[side][2 * f + half] = edge if held is None else held + edge
    return new


def pack_results(u, edges, weights, held, packed):
    thick = [u[i // 2][2 * (i % 2)] + u[i // 2][2 * (i % 2) + 1] for i in range(IMAGES)]

    def pairs(values, i):
        rows = [jnp.concatenate(values[2 * p : 2 * p + 2], axis=1) for p in range(5)]
        sums = select_dot(rows, weights[i])
        return [sums[8 * p : 8 * p + 8] for p in range(5)]

    inner, cols, rows = pairs(thick, 0), pairs(edges[1], 1), pairs(edges[0], 2)
    lane = iota((BOXES, LANES), 1)
    first_cols = cols[0]
    for p in range(1, 4):
        first_cols = jnp.where(lane % 16 // 4 == p, roll(cols[p], 4 * p, 1), first_cols)
    for i in range(8):
        message = roll(cols[4], 120 - 16 * i, 1)
        message = jnp.where(lane < 120, roll(first_cols, 104 - 16 * i, 1), message)
        if i < 4:
            start = 16 * (i % 2) + 8 * (i // 2)
            message = jnp.where(lane < 104, roll(rows[4], 96 - start, 1), message)
        message = jnp.where(lane < 96, roll(rows[i // 2], 80 - 16 * (i % 2), 1), message)
        for p in range(4, -1, -1):
            part = roll(inner[p], 16 * (p - i), 1)
            message = jnp.where(lane < 16 * p + 16, part, message)
        held[pl.ds(i, BOXES, stride=8), :] = message
    for r in range(BOXES):
        packed[r] = held[pl.ds(8 * r, 8), :]


def far_first(n):
    side = round(n**0.5)
    steps = [(a, b) for a in range(side) for b in range(side) if a or b]
    return side, sorted(steps, key=lambda s: -sum(min(x, side - x) for x in s))


def partners(n, me):
    side, steps = far_first(n)
    high, low = me // side, lax.rem(me, side)
    for a, b in steps:
        yield lax.rem(high + a, side) * side + lax.rem(low + b, side)


def send(me, other, source, target, sems):
    pltpu.make_async_remote_copy(
        src_ref=source.at[other],
        dst_ref=target.at[me],
        send_sem=sems.at[0],
        recv_sem=sems.at[1],
        device_id={"gx": other},
        device_id_type=MESH,
    ).start()


def all_slots(n, me, source, target, sems):
    return pltpu.make_async_remote_copy(
        src_ref=source.at[pl.ds(0, n - 1)],
        dst_ref=target.at[pl.ds(0, n - 1)],
        send_sem=sems.at[0],
        recv_sem=sems.at[1],
        device_id={"gx": me},
        device_id_type=MESH,
    )


def level_kernel(
    n,
    m,
    coarse,
    fine_in,
    sources_in,
    tiles_in,
    coarse_new,
    rows_x_out,
    flux_y_out,
    returned,
    fine_out,
    wanted_out,
    sources,
    tiles,
    wanted,
    box_of,
    img,
    flux_x,
    flux_y,
    rows_x,
    fine,
    turned,
    table_x,
    table_y,
    by_tile,
    rims,
    rims_in,
    held,
    packed,
    results,
    cells,
    halo_rows,
    halo_cols,
    from_rows,
    from_cols,
    spread,
    gather,
    load_sems,
    store_sems,
    rim_sems,
    result_sems,
    halo_sems,
):
    me, column = lax.axis_index("gx"), lax.axis_index("gy")
    up, down = lax.rem(me + 1, n), lax.rem(me + n - 1, n)
    right, left = lax.rem(column + 1, m), lax.rem(column + m - 1, m)
    barrier = pltpu.get_barrier_semaphore()

    for other in partners(n, me):
        pl.semaphore_signal(barrier, 1, device_id={"gx": other}, device_id_type=MESH)
    pl.semaphore_signal(barrier, 1, device_id={"gy": right}, device_id_type=MESH)
    pl.semaphore_signal(barrier, 1, device_id={"gy": left}, device_id_type=MESH)

    old, new = pl.ds(0, IMAGES * ROWS), pl.ds(IMAGES * ROWS, IMAGES * ROWS)
    load = pltpu.make_async_copy(coarse, img.at[old], load_sems.at[0])
    load_fine = pltpu.make_async_copy(fine_in, fine, load_sems.at[1])
    load_sources = pltpu.make_async_copy(sources_in, sources, load_sems.at[2])
    load_tiles = pltpu.make_async_copy(tiles_in, tiles, load_sems.at[3])
    load.start()
    load_sources.start()
    load_tiles.start()
    load_fine.start()
    load.wait()
    coarse_step(img, flux_x, flux_y)
    for image in range(IMAGES):
        for i in range(2):
            rows = flux_x[pl.ds(image * ROWS + 7 * i, 8, stride=8), :]
            rows_x[image, pl.ds(8 * i, 8), :] = rows
    stores = [
        pltpu.make_async_copy(rows_x, rows_x_out, store_sems.at[0]),
        pltpu.make_async_copy(flux_y, flux_y_out, store_sems.at[1]),
    ]
    stores[0].start()
    stores[1].start()
    table_x[...] = jnp.zeros_like(table_x)
    table_y[...] = jnp.zeros_like(table_y)
    build_tables(img, turned, table_x, table_y)
    load_sources.wait()
    load_tiles.wait()
    pack_rims(n, me, sources, tiles, table_x, table_y, by_tile, rims, wanted, box_of)
    rims_in[me] = rims[me]
    stores.append(pltpu.make_async_copy(wanted, wanted_out, store_sems.at[2]))
    stores[2].start()
    pack_halo(img, halo_rows, halo_cols)
    load_fine.wait()
    for r in range(BOXES):
        for f in range(5):
            for z in range(4):
                cells[4 * f + z, pl.ds(r, 1), :] = fine[r, f, pl.ds(z, 1), :]
    spread_weights(spread)
    gather_weights(gather)
    pl.semaphore_wait(barrier, n + 1)

    for other in partners(n, me):
        send(me, other, rims, rims_in, rim_sems)
    halos = []
    for i, (source, target, where) in enumerate(
        (
            (halo_rows, from_rows.at[0], {"gx": up}),
            (halo_rows, from_rows.at[1], {"gx": down}),
            (halo_cols, from_cols.at[0], {"gy": right}),
            (halo_cols, from_cols.at[1], {"gy": left}),
        )
    ):
        copy = pltpu.make_async_remote_copy(
            src_ref=source,
            dst_ref=target,
            send_sem=halo_sems.at[0, i],
            recv_sem=halo_sems.at[1, i],
            device_id=where,
            device_id_type=MESH,
        )
        copy.start()
        halos.append(copy)

    rim_copies = all_slots(n, me, rims, rims_in, rim_sems)
    rim_copies.wait_recv()
    ghosts = own_rims(me, sources, rims_in, held, spread)
    u = [[cells[4 * f + z] for z in range(4)] for f in range(5)]
    edges = [[None] * IMAGES, [None] * IMAGES]
    u = fine_step(u, ghosts[0][0], ghosts[1][0], edges)
    u = fine_step(u, ghosts[0][1], ghosts[1][1], edges)
    pack_results(u, edges, gather, held, packed)
    for other in partners(n, me):
        results[other] = packed[box_of[other]]
        send(me, other, results, returned, result_sems)
    results[me] = packed[box_of[me]]
    stores.append(pltpu.make_async_copy(results.at[me], returned.at[me], store_sems.at[3]))
    stores[3].start()
    for f in range(5):
        for z in range(4):
            for r in range(BOXES):
                fine[r, f, pl.ds(z, 1), :] = u[f][z][r : r + 1]
    stores.append(pltpu.make_async_copy(fine, fine_out, store_sems.at[4]))
    stores[4].start()
    for copy in halos:
        copy.wait_recv()
    finish_edges(img, halo_rows, halo_cols, from_rows, from_cols)
    stores.append(pltpu.make_async_copy(img.at[new], coarse_new, store_sems.at[5]))
    stores[5].start()
    rim_copies.wait_send()
    for copy in halos:
        copy.wait_send()
    for copy in stores:
        copy.wait()
    result_copies = all_slots(n, me, results, returned, result_sems)
    result_copies.wait_send()
    result_copies.wait_recv()


def merge_kernel(
    n,
    new_in,
    rows_x_in,
    flux_y_in,
    returned_in,
    wanted_in,
    fine_in,
    out_to,
    fine_out,
    new,
    rows_x,
    flux_y,
    returned,
    wanted,
    out,
    slots,
    covered_in,
    turned,
    fine,
    sems,
    out_sem,
    fine_sem,
):
    pairs = (
        (wanted_in, wanted),
        (returned_in, returned),
        (new_in, new),
        (rows_x_in, rows_x),
        (flux_y_in, flux_y),
        (fine_in, fine),
    )
    loads = [pltpu.make_async_copy(a, b, sems.at[i]) for i, (a, b) in enumerate(pairs)]
    for copy in loads:
        copy.start()
    lane, sub = iota((8, LANES), 1), iota((8, LANES), 0)

    def clear(t, carry):
        slots[t] = -1
        return carry

    def place(o, carry):
        slots[wanted[o]] = o
        return carry

    lax.fori_loop(0, 128, clear, 0, unroll=8)
    loads[0].wait()
    lax.fori_loop(0, n, place, 0, unroll=8)
    blank = jnp.zeros((8, LANES), jnp.float32)
    group = lane // 8
    for tx in (0, 7):
        covered_in[tx] = blank
        for i in range(16):
            turned[tx, i] = blank
    loads[5].wait()
    store_fine = pltpu.make_async_copy(fine, fine_out, fine_sem)
    store_fine.start()

    def row_of_tiles(tx, carry):
        covered = blank
        diagonals = [blank] * 16
        for ty in range(1, 15):
            slot = slots[16 * tx + ty]
            live = (slot >= 0).astype(jnp.int32)
            message = returned[jnp.maximum(slot, 0)]
            covered = jnp.where(lane // 8 == jnp.where(live > 0, ty, -1), 1.0, covered)
            for d in range(16):
                i = (ty - d) % 16
                diagonals[d] = jnp.where(group == i, message, diagonals[d])
        diagonals = [roll(diagonals[d], 8 * d, 1) for d in range(16)]
        covered_in[tx] = covered
        for i in range(16):
            part = blank
            for ty in range(1, 15):
                part = jnp.where(group == ty, diagonals[(ty - i) % 16], part)
            turned[tx, i] = part
        return carry

    loads[1].wait()
    lax.fori_loop(1, 7, row_of_tiles, 0)
    for copy in loads[2:5]:
        copy.wait()

    def finish(tx, carry):
        above, below = jnp.minimum(tx + 1, 7), jnp.maximum(tx - 1, 0)
        cover = covered_in[tx]
        covered = cover > 0.5
        last = lane % 8 == 7
        touched = last & (roll(cover, -1, 1) > 0.5) | (lane % 8 == 0) & (roll(cover, 1, 1) > 0.5)
        beside = (sub == 7) & (covered_in[above] > 0.5) | (sub == 0) & (covered_in[below] > 0.5)
        rows = pl.ds(pl.multiple_of(8 * tx, 8), 8)
        low, high = [turned[above, 10 + g] for g in range(3)], [turned[below, 10 + g] for g in range(3)]
        cols = [turned[tx, 13 + g] for g in range(3)]
        for image in range(IMAGES):
            if image < 8:
                lows, highs = low[0][image : image + 1], high[1][image : image + 1]
            else:
                lows, highs = low[2][image - 8 : image - 7], high[2][image - 6 : image - 5]
            place = 2 * (image % 4)
            value = cols[image // 4]
            value = jnp.where(last, roll(value, -1 - place, 1), roll(value, 7 - place, 1))
            cells = new[image, rows, :] + jnp.where(touched, value - flux_y[image, rows, :], 0.0)
            lows = lows - rows_x[image, pl.ds(8 + tx, 1), :]
            highs = highs - rows_x[image, pl.ds(tx, 1), :]
            cells = cells + jnp.where(beside, jnp.where(sub == 7, lows, highs), 0.0)
            out[image, rows, :] = jnp.where(covered, turned[tx, image], cells)
        pltpu.make_async_copy(out.at[:, rows], out_to.at[:, rows], out_sem).start()
        return carry

    lax.fori_loop(0, 8, finish, 0)
    pltpu.make_async_copy(out, out_to, out_sem).wait()
    store_fine.wait()


def body(n, m, coarse_state, fine_state, source_rows, tile_ids):
    hbm = pl.BlockSpec(memory_space=pltpu.HBM)
    f32 = jnp.float32
    coarse = coarse_state.reshape(IMAGES * ROWS, LANES)
    fine = fine_state.reshape(BOXES, 5, 4, 256)
    sources = source_rows.reshape(n, BOXES).T
    tiles = tile_ids.reshape(n, BOXES).T
    shape = jax.ShapeDtypeStruct
    image = shape((IMAGES * ROWS, LANES), f32)
    boxes = shape((BOXES, 5, 4, 256), f32)
    new, rows_x, flux_y, returned, fine_out, wanted = pl.pallas_call(
        functools.partial(level_kernel, n, m),
        out_shape=(
            image,
            shape((IMAGES, 16, LANES), f32),
            image,
            shape((n, 8, LANES), f32),
            boxes,
            shape((n,), jnp.int32),
        ),
        in_specs=[hbm] * 4,
        out_specs=(hbm,) * 6,
        scratch_shapes=[
            pltpu.SMEM((BOXES, n), jnp.int32),
            pltpu.SMEM((BOXES, n), jnp.int32),
            pltpu.SMEM((n,), jnp.int32),
            pltpu.SMEM((n,), jnp.int32),
            pltpu.VMEM((2 * IMAGES * ROWS, LANES), f32),
            pltpu.VMEM((IMAGES * ROWS, LANES), f32),
            pltpu.VMEM((IMAGES * ROWS, LANES), f32),
            pltpu.VMEM((IMAGES, 16, LANES), f32),
            pltpu.VMEM((BOXES, 5, 4, 256), f32),
            pltpu.VMEM((IMAGES * LANES, LANES), f32),
            pltpu.VMEM((8, 8, 8, LANES), f32),
            pltpu.VMEM((16, 4, 8, LANES), f32),
            pltpu.VMEM((128, 5, LANES), f32),
            pltpu.VMEM((n, 5, LANES), f32),
            pltpu.VMEM((n, 5, LANES), f32),
            pltpu.VMEM((8 * BOXES, LANES), f32),
            pltpu.VMEM((BOXES, 8, LANES), f32),
            pltpu.VMEM((n, 8, LANES), f32),
            pltpu.VMEM((20, BOXES, 256), f32),
            pltpu.VMEM((32, LANES), f32),
            pltpu.VMEM((ROWS, LANES), f32),
            pltpu.VMEM((2, 32, LANES), f32),
            pltpu.VMEM((2, ROWS, LANES), f32),
            pltpu.VMEM((2, LANES, 256), jnp.bfloat16),
            pltpu.VMEM((3, 512, LANES), jnp.bfloat16),
            pltpu.SemaphoreType.DMA((4,)),
            pltpu.SemaphoreType.DMA((6,)),
            pltpu.SemaphoreType.DMA((2,)),
            pltpu.SemaphoreType.DMA((2,)),
            pltpu.SemaphoreType.DMA((2, 4)),
        ],
        compiler_params=pltpu.CompilerParams(
            collective_id=0, has_side_effects=True, vmem_limit_bytes=VMEM_LIMIT
        ),
        name="levels",
    )(coarse, fine, sources, tiles)
    stack = shape((IMAGES, ROWS, LANES), f32)
    field = pltpu.VMEM((IMAGES, ROWS, LANES), f32)
    out, fine_out = pl.pallas_call(
        functools.partial(merge_kernel, n),
        out_shape=(stack, boxes),
        in_specs=[hbm] * 6,
        out_specs=(hbm,) * 2,
        scratch_shapes=[
            field,
            pltpu.VMEM((IMAGES, 16, LANES), f32),
            field,
            pltpu.VMEM((n, 8, LANES), f32),
            pltpu.SMEM((n,), jnp.int32),
            field,
            pltpu.SMEM((128,), jnp.int32),
            pltpu.VMEM((8, 8, LANES), f32),
            pltpu.VMEM((8, 16, 8, LANES), f32),
            pltpu.VMEM((BOXES, 5, 4, 256), f32),
            pltpu.SemaphoreType.DMA((6,)),
            pltpu.SemaphoreType.DMA,
            pltpu.SemaphoreType.DMA,
        ],
        compiler_params=pltpu.CompilerParams(vmem_limit_bytes=VMEM_LIMIT),
        name="merge",
    )(
        new.reshape(stack.shape),
        rows_x,
        flux_y.reshape(stack.shape),
        returned,
        wanted,
        fine_out,
    )
    return out.reshape(coarse_state.shape), fine_out.reshape(fine_state.shape)


def solution(mesh):
    return jax.shard_map(
        functools.partial(body, mesh.shape["gx"], mesh.shape["gy"]),
        mesh=mesh,
        in_specs=(
            P(None, None, "gx", "gy"),
            P("gx", "gy", None, None, None, None),
            P(None, "gy", None),
            P(None, "gy", None),
        ),
        out_specs=(P(None, None, "gx", "gy"), P("gx", "gy", None, None, None, None)),
        check_vma=False,
    )
```

```python
import functools

import jax
import jax.numpy as jnp
from jax import lax
from jax.experimental import pallas as pl
from jax.experimental.pallas import tpu as pltpu
from jax.sharding import PartitionSpec as P

MESH = pl.DeviceIdType.MESH
HEAT_RATIO = 1.4
HALF_STEP = 0.025
BOXES = 8
IMAGES = 10
ROWS = 64
LANES = 128
VMEM_LIMIT = 65280 * 1024


def iota(shape, dim):
    return lax.broadcasted_iota(jnp.int32, shape, dim)


def roll(x, shift, axis):
    if isinstance(shift, int):
        shift = shift % x.shape[axis]
        if shift == 0:
            return x
    return pltpu.roll(x, shift, axis)


def select_dot(values, weights):
    x = jnp.concatenate(values, axis=0)
    high = x.astype(jnp.bfloat16)
    x = x - high.astype(jnp.float32)
    middle = x.astype(jnp.bfloat16)
    low = (x - middle.astype(jnp.float32)).astype(jnp.bfloat16)
    parts = [
        jnp.dot(part, weights, preferred_element_type=jnp.float32) for part in (low, middle, high)
    ]
    return parts[0] + parts[1] + parts[2]


def primitives(u):
    inverse = 1.0 / u[0]
    velocity = [u[1] * inverse, u[2] * inverse, u[3] * inverse]
    kinetic = 0.5 * (u[1] * velocity[0] + u[2] * velocity[1] + u[3] * velocity[2])
    pressure = (HEAT_RATIO - 1.0) * (u[4] - kinetic)
    sound = jnp.sqrt(HEAT_RATIO * pressure * inverse)
    return velocity, pressure, sound


def scaled_state(u, velocity, pressure, sound, k):
    drift = HALF_STEP * velocity[k]
    speed = HALF_STEP * (jnp.abs(velocity[k]) + sound)
    return list(u) + [pressure, drift, speed]


def scaled_flux(state, k):
    u, pressure, drift = state[:5], state[5], state[6]
    flux = [u[f] * drift for f in range(5)]
    flux[1 + k] = flux[1 + k] + HALF_STEP * pressure
    flux[4] = (u[4] + pressure) * drift
    return flux


def face_flux(left, right, k):
    a, b = scaled_flux(left, k), scaled_flux(right, k)
    top = jnp.maximum(left[7], right[7])
    return [(a[f] + b[f]) - top * (right[f] - left[f]) for f in range(5)]


def coarse_step(img, flux_x, flux_y):
    row, col = iota((ROWS, LANES), 0), iota((ROWS, LANES), 1)
    cells, prims = [], []
    for z in range(2):
        u = [img[pl.ds((2 * f + z) * ROWS, ROWS), :] for f in range(5)]
        cells.append(u)
        prims.append(primitives(u))
    depth = [HALF_STEP * (jnp.abs(prims[z][0][0]) + prims[z][2]) for z in range(2)]
    depth = 2.0 * jnp.maximum(depth[0], depth[1])
    for z in range(2):
        u = cells[z]
        new = [u[f] - depth * (u[f] - cells[1 - z][f]) for f in range(5)]
        for k, axis, place, saved in ((1, 0, row, flux_x), (2, 1, col, flux_y)):
            state = scaled_state(u, *prims[z], k)
            before = [roll(s, 1, axis) for s in state]
            faces = face_flux(before, state, k)
            for f in range(5):
                face = jnp.where(place == 0, 0.0, faces[f])
                upper = roll(face, -1, axis)
                signed = jnp.where(place % 8 == 7, -upper, face)
                saved[pl.ds((2 * f + z) * ROWS, ROWS), :] = signed
                new[f] = new[f] - (upper - face)
        for f in range(5):
            img[pl.ds((IMAGES + 2 * f + z) * ROWS, ROWS), :] = new[f]


def build_tables(img, turned, table_x, table_y):
    for tx in range(1, 7):
        for k, row in ((0, 8 * tx - 1), (1, 8 * tx + 8)):
            for q in range(4):
                rows = img[pl.ds(5 * q * ROWS + row, 5, stride=ROWS), :]
                table_x[tx, 4 * k + q, pl.ds(0, 5), :] = rows
    for p in range(IMAGES):
        turned[pl.ds(p * LANES, LANES), :] = jnp.transpose(img[pl.ds(p * LANES, LANES), :])
    for ty in range(1, 15):
        for k, col in ((0, 8 * ty - 1), (1, 8 * ty + 8)):
            for h in range(2):
                rows = turned[pl.ds(5 * h * LANES + col, 5, stride=LANES), :]
                table_y[ty, 2 * k + h, pl.ds(0, 5), :] = rows


def wanted_tile(sources, tiles, o, me):
    tile = jnp.int32(0)
    for r in range(BOXES):
        tile = jnp.where(sources[r, o] == me, tiles[r, o], tile)
    return tile


def pack_rims(n, me, sources, tiles, table_x, table_y, by_tile, rims, wanted, box_of):
    group = iota((8, LANES), 1) // 8
    for tx in range(1, 7):
        for ty in range(1, 15):
            message = roll(table_x[tx, 0], -8 * ty, 1)
            for g in range(1, 8):
                part = roll(table_x[tx, g], 8 * g - 8 * ty, 1)
                message = jnp.where(group == g, part, message)
            for u in range(4):
                columns = table_y[ty, u]
                for j in range(2):
                    part = roll(columns, 64 + 16 * u + 8 * j - 64 * j - 8 * tx, 1)
                    message = jnp.where(group == 8 + 2 * u + j, part, message)
            by_tile[16 * tx + ty] = message[:5]

    def one(o, carry):
        tile = wanted_tile(sources, tiles, o, me)
        wanted[o] = tile
        rims[o] = by_tile[jnp.maximum(tile, 17)]
        box = jnp.int32(0)
        for r in range(BOXES):
            box = jnp.where(sources[r, me] == o, r, box)
        box_of[o] = box
        return carry

    lax.fori_loop(0, n, one, 0)


def pack_halo(img, halo_rows, halo_cols):
    halo_rows[...] = jnp.zeros_like(halo_rows)
    halo_rows[pl.ds(0, 8), :] = img[pl.ds(0, 8, stride=ROWS), :]
    halo_rows[pl.ds(8, 2), :] = img[pl.ds(8 * ROWS, 2, stride=ROWS), :]
    halo_rows[pl.ds(16, 8), :] = img[pl.ds(ROWS - 1, 8, stride=ROWS), :]
    halo_rows[pl.ds(24, 2), :] = img[pl.ds(9 * ROWS - 1, 2, stride=ROWS), :]
    lane = iota((ROWS, LANES), 1)
    packed = jnp.ones((ROWS, LANES), jnp.float32)
    for image in range(IMAGES):
        cells = img[pl.ds(image * ROWS, ROWS), :]
        packed = jnp.where(lane == image, roll(cells, image, 1), packed)
        packed = jnp.where(lane == 16 + image, roll(cells, 17 + image, 1), packed)
    halo_cols[...] = packed


def finish_edges(img, halo_rows, halo_cols, from_rows, from_cols):
    def by_row(source, start):
        u = [source[pl.ds(start + 2 * f, 2), :] for f in range(5)]
        return scaled_state(u, *primitives(u), 1)

    own_low, own_high = by_row(halo_rows, 0), by_row(halo_rows, 16)
    low = face_flux(by_row(from_rows.at[0], 16), own_low, 1)
    high = face_flux(own_high, by_row(from_rows.at[1], 0), 1)
    for f in range(5):
        for z in range(2):
            base = (IMAGES + 2 * f + z) * ROWS
            first, last = pl.ds(base, 1), pl.ds(base + ROWS - 1, 1)
            img[first, :] = img[first, :] + low[f][z : z + 1]
            img[last, :] = img[last, :] - high[f][z : z + 1]

    lane = iota((ROWS, LANES), 1)
    own = halo_cols[...]
    left = jnp.where(lane < 16, roll(from_cols[0], -16, 1), own)
    right = jnp.where(lane < 16, own, roll(from_cols[1], 16, 1))

    def by_lane(packed):
        u = [roll(packed, -2 * f, 1) for f in range(5)]
        return scaled_state(u, *primitives(u), 2)

    faces = face_flux(by_lane(left), by_lane(right), 2)
    for f in range(5):
        for z in range(2):
            rows = pl.ds((IMAGES + 2 * f + z) * ROWS, ROWS)
            cells = img[rows, :]
            cells = jnp.where(lane == 0, cells + roll(faces[f], -z, 1), cells)
            cells = jnp.where(lane == LANES - 1, cells - roll(faces[f], 111 - z, 1), cells)
            img[rows, :] = cells


def spread_weights(weights):
    source, cell = iota((LANES, 256), 0), iota((LANES, 256), 1)
    a, b = cell // 16, cell % 16
    for side, (along, across) in enumerate(((b, a), (a, b))):
        chosen = (source < 16) & (source % 8 == along // 2) & (source // 8 == across // 8)
        weights[side] = jnp.where(chosen, 1.0, 0.0).astype(jnp.bfloat16)


def gather_weights(weights):
    source, target = iota((512, LANES), 0), iota((512, LANES), 1)
    cell, half = source % 256, source // 256
    a, b = cell // 16, cell % 16
    row, lane = target // 16 == a // 2, target % 16
    average = row & (lane == 8 * half + b // 2)
    low_col = row & (lane == 2 * half) & (b == 0)
    high_col = row & (lane == 2 * half + 1) & (b == 15)
    low_row = (target == 16 * half + b // 2) & (a == 0)
    high_row = (target == 16 * half + 8 + b // 2) & (a == 15)
    for i, (low, high) in enumerate(((None, average), (low_col, high_col), (low_row, high_row))):
        values = jnp.where(high, 0.125, 0.0)
        if low is not None:
            values = jnp.where(low, -0.125, values)
        weights[i] = values.astype(jnp.bfloat16)


def own_rims(me, sources, rims, held, weights):
    for r in range(BOXES):
        held[pl.ds(8 * r, 5), :] = rims[sources[r, me]]
    by_row = [held[pl.ds(s, BOXES, stride=8), :] for s in range(5)]
    lane = iota((BOXES, LANES), 1)

    def pair(low, low_lane, high, high_lane):
        first = roll(low, -low_lane, 1)
        second = roll(high, 8 - high_lane, 1)
        return jnp.where(lane < 8, first, jnp.where(lane < 16, second, 0.0))

    sides = [[], []]
    for image in range(2 * IMAGES):
        row, q = by_row[image % 5], image // 5
        sides[0].append(pair(row, 8 * q, row, 32 + 8 * q))
        p, j = image // 2, image % 2
        row, lane_j = by_row[p % 5], 16 * (p // 5) + 8 * j
        sides[1].append(pair(row, 64 + lane_j, row, 96 + lane_j))

    spread = []
    for side in range(2):
        old = sides[side][:IMAGES]
        mid = [0.5 * (x + y) for x, y in zip(old, sides[side][IMAGES:])]
        ghosts = select_dot(old + mid, weights[side])
        spread.append(
            [
                [ghosts[(IMAGES * t + i) * 8 : (IMAGES * t + i) * 8 + 8] for i in range(IMAGES)]
                for t in range(2)
            ]
        )
    return spread


def fine_step(u, ghosts_x, ghosts_y, edges):
    cell = iota((BOXES, 256), 1)
    a, b = cell // 16, cell % 16
    prims = [primitives([u[f][z] for f in range(5)]) for z in range(4)]
    states = [scaled_state([u[f][z] for f in range(5)], *prims[z], 0) for z in range(4)]
    deep = [face_flux(states[z], states[(z + 1) % 4], 0) for z in range(4)]
    new = [[u[f][z] - (deep[z][f] - deep[z - 1][f]) for z in range(4)] for f in range(5)]
    sides = (
        (1, ghosts_x, 16, a == 0, a == 15, a < 8),
        (2, ghosts_y, 1, b == 0, b == 15, b < 8),
    )
    for side, (k, ghosts, stride, first, last, lower) in enumerate(sides):
        for half in range(2):
            cells = [ghosts[2 * f + half] for f in range(5)]
            ghost = scaled_state(cells, *primitives(cells), k)
            for z in (2 * half, 2 * half + 1):
                state = scaled_state([u[f][z] for f in range(5)], *prims[z], k)
                before = [
                    jnp.where(first, ghost[i], roll(state[i], stride, 1)) for i in range(8)
                ]
                low = face_flux(before, state, k)
                outer = face_flux(state, ghost, k)
                for f in range(5):
                    high = jnp.where(last, outer[f], roll(low[f], -stride, 1))
                    new[f][z] = new[f][z] - (high - low[f])
                    edge = jnp.where(lower, low[f], high)
                    held = edges[side][2 * f + half]
                    edges[side][2 * f + half] = edge if held is None else held + edge
    return new


def pack_results(u, edges, weights, held, packed):
    thick = [u[i // 2][2 * (i % 2)] + u[i // 2][2 * (i % 2) + 1] for i in range(IMAGES)]

    def pairs(values, i):
        rows = [jnp.concatenate(values[2 * p : 2 * p + 2], axis=1) for p in range(5)]
        sums = select_dot(rows, weights[i])
        return [sums[8 * p : 8 * p + 8] for p in range(5)]

    inner, cols, rows = pairs(thick, 0), pairs(edges[1], 1), pairs(edges[0], 2)
    lane = iota((BOXES, LANES), 1)
    first_cols = cols[0]
    for p in range(1, 4):
        first_cols = jnp.where(lane % 16 // 4 == p, roll(cols[p], 4 * p, 1), first_cols)
    for i in range(8):
        message = roll(cols[4], 120 - 16 * i, 1)
        message = jnp.where(lane < 120, roll(first_cols, 104 - 16 * i, 1), message)
        if i < 4:
            start = 16 * (i % 2) + 8 * (i // 2)
            message = jnp.where(lane < 104, roll(rows[4], 96 - start, 1), message)
        message = jnp.where(lane < 96, roll(rows[i // 2], 80 - 16 * (i % 2), 1), message)
        for p in range(4, -1, -1):
            part = roll(inner[p], 16 * (p - i), 1)
            message = jnp.where(lane < 16 * p + 16, part, message)
        held[pl.ds(i, BOXES, stride=8), :] = message
    for r in range(BOXES):
        packed[r] = held[pl.ds(8 * r, 8), :]


def far_first(n):
    side = round(n**0.5)
    steps = [(a, b) for a in range(side) for b in range(side) if a or b]
    return side, sorted(steps, key=lambda s: -sum(min(x, side - x) for x in s))


def partners(n, me):
    side, steps = far_first(n)
    high, low = me // side, lax.rem(me, side)
    for a, b in steps:
        yield lax.rem(high + a, side) * side + lax.rem(low + b, side)


def send(me, other, source, target, sems):
    pltpu.make_async_remote_copy(
        src_ref=source.at[other],
        dst_ref=target.at[me],
        send_sem=sems.at[0],
        recv_sem=sems.at[1],
        device_id={"gx": other},
        device_id_type=MESH,
    ).start()


def all_slots(n, me, source, target, sems):
    return pltpu.make_async_remote_copy(
        src_ref=source.at[pl.ds(0, n - 1)],
        dst_ref=target.at[pl.ds(0, n - 1)],
        send_sem=sems.at[0],
        recv_sem=sems.at[1],
        device_id={"gx": me},
        device_id_type=MESH,
    )


def level_kernel(
    n,
    m,
    coarse,
    fine_in,
    sources_in,
    tiles_in,
    coarse_new,
    rows_x_out,
    flux_y_out,
    returned,
    fine_out,
    wanted_out,
    sources,
    tiles,
    wanted,
    box_of,
    img,
    flux_x,
    flux_y,
    rows_x,
    fine,
    turned,
    table_x,
    table_y,
    by_tile,
    rims,
    rims_in,
    held,
    packed,
    results,
    cells,
    halo_rows,
    halo_cols,
    from_rows,
    from_cols,
    spread,
    gather,
    load_sems,
    store_sems,
    rim_sems,
    result_sems,
    halo_sems,
):
    me, column = lax.axis_index("gx"), lax.axis_index("gy")
    up, down = lax.rem(me + 1, n), lax.rem(me + n - 1, n)
    right, left = lax.rem(column + 1, m), lax.rem(column + m - 1, m)
    barrier = pltpu.get_barrier_semaphore()

    for other in partners(n, me):
        pl.semaphore_signal(barrier, 1, device_id={"gx": other}, device_id_type=MESH)
    pl.semaphore_signal(barrier, 1, device_id={"gy": right}, device_id_type=MESH)
    pl.semaphore_signal(barrier, 1, device_id={"gy": left}, device_id_type=MESH)

    old, new = pl.ds(0, IMAGES * ROWS), pl.ds(IMAGES * ROWS, IMAGES * ROWS)
    load = pltpu.make_async_copy(coarse, img.at[old], load_sems.at[0])
    load_fine = pltpu.make_async_copy(fine_in, fine, load_sems.at[1])
    load_sources = pltpu.make_async_copy(sources_in, sources, load_sems.at[2])
    load_tiles = pltpu.make_async_copy(tiles_in, tiles, load_sems.at[3])
    load.start()
    load_sources.start()
    load_tiles.start()
    load_fine.start()
    load.wait()
    coarse_step(img, flux_x, flux_y)
    for image in range(IMAGES):
        for i in range(2):
            rows = flux_x[pl.ds(image * ROWS + 7 * i, 8, stride=8), :]
            rows_x[image, pl.ds(8 * i, 8), :] = rows
    stores = [
        pltpu.make_async_copy(rows_x, rows_x_out, store_sems.at[0]),
        pltpu.make_async_copy(flux_y, flux_y_out, store_sems.at[1]),
    ]
    stores[0].start()
    stores[1].start()
    table_x[...] = jnp.zeros_like(table_x)
    table_y[...] = jnp.zeros_like(table_y)
    build_tables(img, turned, table_x, table_y)
    load_sources.wait()
    load_tiles.wait()
    pack_rims(n, me, sources, tiles, table_x, table_y, by_tile, rims, wanted, box_of)
    rims_in[me] = rims[me]
    stores.append(pltpu.make_async_copy(wanted, wanted_out, store_sems.at[2]))
    stores[2].start()
    pack_halo(img, halo_rows, halo_cols)
    load_fine.wait()
    for r in range(BOXES):
        for f in range(5):
            for z in range(4):
                cells[4 * f + z, pl.ds(r, 1), :] = fine[r, f, pl.ds(z, 1), :]
    spread_weights(spread)
    gather_weights(gather)
    pl.semaphore_wait(barrier, n + 1)

    for other in partners(n, me):
        send(me, other, rims, rims_in, rim_sems)
    halos = []
    for i, (source, target, where) in enumerate(
        (
            (halo_rows, from_rows.at[0], {"gx": up}),
            (halo_rows, from_rows.at[1], {"gx": down}),
            (halo_cols, from_cols.at[0], {"gy": right}),
            (halo_cols, from_cols.at[1], {"gy": left}),
        )
    ):
        copy = pltpu.make_async_remote_copy(
            src_ref=source,
            dst_ref=target,
            send_sem=halo_sems.at[0, i],
            recv_sem=halo_sems.at[1, i],
            device_id=where,
            device_id_type=MESH,
        )
        copy.start()
        halos.append(copy)

    rim_copies = all_slots(n, me, rims, rims_in, rim_sems)
    rim_copies.wait_recv()
    ghosts = own_rims(me, sources, rims_in, held, spread)
    u = [[cells[4 * f + z] for z in range(4)] for f in range(5)]
    edges = [[None] * IMAGES, [None] * IMAGES]
    u = fine_step(u, ghosts[0][0], ghosts[1][0], edges)
    u = fine_step(u, ghosts[0][1], ghosts[1][1], edges)
    pack_results(u, edges, gather, held, packed)
    for other in partners(n, me):
        results[other] = packed[box_of[other]]
        send(me, other, results, returned, result_sems)
    results[me] = packed[box_of[me]]
    stores.append(pltpu.make_async_copy(results.at[me], returned.at[me], store_sems.at[3]))
    stores[3].start()
    for f in range(5):
        for z in range(4):
            for r in range(BOXES):
                fine[r, f, pl.ds(z, 1), :] = u[f][z][r : r + 1]
    stores.append(pltpu.make_async_copy(fine, fine_out, store_sems.at[4]))
    stores[4].start()
    for copy in halos:
        copy.wait_recv()
    finish_edges(img, halo_rows, halo_cols, from_rows, from_cols)
    stores.append(pltpu.make_async_copy(img.at[new], coarse_new, store_sems.at[5]))
    stores[5].start()
    rim_copies.wait_send()
    for copy in halos:
        copy.wait_send()
    for copy in stores:
        copy.wait()
    result_copies = all_slots(n, me, results, returned, result_sems)
    result_copies.wait_send()
    result_copies.wait_recv()


def merge_kernel(
    n,
    new_in,
    rows_x_in,
    flux_y_in,
    returned_in,
    wanted_in,
    fine_in,
    out_to,
    fine_out,
    new,
    rows_x,
    flux_y,
    returned,
    wanted,
    out,
    slots,
    covered_in,
    turned,
    fine,
    sems,
    out_sem,
    fine_sem,
):
    pairs = (
        (wanted_in, wanted),
        (returned_in, returned),
        (new_in, new),
        (rows_x_in, rows_x),
        (flux_y_in, flux_y),
        (fine_in, fine),
    )
    loads = [pltpu.make_async_copy(a, b, sems.at[i]) for i, (a, b) in enumerate(pairs)]
    for copy in loads:
        copy.start()
    lane, sub = iota((8, LANES), 1), iota((8, LANES), 0)

    def clear(t, carry):
        slots[t] = -1
        return carry

    def place(o, carry):
        slots[wanted[o]] = o
        return carry

    lax.fori_loop(0, 128, clear, 0, unroll=8)
    loads[0].wait()
    lax.fori_loop(0, n, place, 0, unroll=8)
    blank = jnp.zeros((8, LANES), jnp.float32)
    group = lane // 8
    for tx in (0, 7):
        covered_in[tx] = blank
        for i in range(16):
            turned[tx, i] = blank

    def row_of_tiles(tx, carry):
        covered = blank
        parts = [blank] * 16
        for ty in range(1, 15):
            slot = slots[16 * tx + ty]
            live = (slot >= 0).astype(jnp.int32)
            parts[ty] = returned[jnp.maximum(slot, 0)]
            covered = jnp.where(group == jnp.where(live > 0, ty, -1), 1.0, covered)
        for step in (8, 4, 2, 1):
            kept = group // step % 2 == 0
            for i in range(16):
                if i // step % 2 == 0:
                    low, high = parts[i], parts[i + step]
                    parts[i] = jnp.where(kept, low, roll(high, 8 * step, 1))
                    parts[i + step] = jnp.where(kept, roll(low, -8 * step, 1), high)
        covered_in[tx] = covered
        for i in range(16):
            turned[tx, i] = parts[i]
        return carry

    loads[1].wait()
    lax.fori_loop(1, 7, row_of_tiles, 0)
    loads[5].wait()
    store_fine = pltpu.make_async_copy(fine, fine_out, fine_sem)
    store_fine.start()
    for copy in loads[2:5]:
        copy.wait()

    def finish(tx, carry):
        above, below = jnp.minimum(tx + 1, 7), jnp.maximum(tx - 1, 0)
        cover = covered_in[tx]
        covered = cover > 0.5
        last = lane % 8 == 7
        touched = last & (roll(cover, -1, 1) > 0.5) | (lane % 8 == 0) & (roll(cover, 1, 1) > 0.5)
        beside = (sub == 7) & (covered_in[above] > 0.5) | (sub == 0) & (covered_in[below] > 0.5)
        rows = pl.ds(pl.multiple_of(8 * tx, 8), 8)
        low, high = [turned[above, 10 + g] for g in range(3)], [turned[below, 10 + g] for g in range(3)]
        cols = [turned[tx, 13 + g] for g in range(3)]
        for image in range(IMAGES):
            if image < 8:
                lows, highs = low[0][image : image + 1], high[1][image : image + 1]
            else:
                lows, highs = low[2][image - 8 : image - 7], high[2][image - 6 : image - 5]
            place = 2 * (image % 4)
            value = cols[image // 4]
            value = jnp.where(last, roll(value, -1 - place, 1), roll(value, 7 - place, 1))
            cells = new[image, rows, :] + jnp.where(touched, value - flux_y[image, rows, :], 0.0)
            lows = lows - rows_x[image, pl.ds(8 + tx, 1), :]
            highs = highs - rows_x[image, pl.ds(tx, 1), :]
            cells = cells + jnp.where(beside, jnp.where(sub == 7, lows, highs), 0.0)
            out[image, rows, :] = jnp.where(covered, turned[tx, image], cells)
        pltpu.make_async_copy(out.at[:, rows], out_to.at[:, rows], out_sem).start()
        return carry

    lax.fori_loop(0, 8, finish, 0)
    pltpu.make_async_copy(out, out_to, out_sem).wait()
    store_fine.wait()


def body(n, m, coarse_state, fine_state, source_rows, tile_ids):
    hbm = pl.BlockSpec(memory_space=pltpu.HBM)
    f32 = jnp.float32
    coarse = coarse_state.reshape(IMAGES * ROWS, LANES)
    fine = fine_state.reshape(BOXES, 5, 4, 256)
    sources = source_rows.reshape(n, BOXES).T
    tiles = tile_ids.reshape(n, BOXES).T
    shape = jax.ShapeDtypeStruct
    image = shape((IMAGES * ROWS, LANES), f32)
    boxes = shape((BOXES, 5, 4, 256), f32)
    new, rows_x, flux_y, returned, fine_out, wanted = pl.pallas_call(
        functools.partial(level_kernel, n, m),
        out_shape=(
            image,
            shape((IMAGES, 16, LANES), f32),
            image,
            shape((n, 8, LANES), f32),
            boxes,
            shape((n,), jnp.int32),
        ),
        in_specs=[hbm] * 4,
        out_specs=(hbm,) * 6,
        scratch_shapes=[
            pltpu.SMEM((BOXES, n), jnp.int32),
            pltpu.SMEM((BOXES, n), jnp.int32),
            pltpu.SMEM((n,), jnp.int32),
            pltpu.SMEM((n,), jnp.int32),
            pltpu.VMEM((2 * IMAGES * ROWS, LANES), f32),
            pltpu.VMEM((IMAGES * ROWS, LANES), f32),
            pltpu.VMEM((IMAGES * ROWS, LANES), f32),
            pltpu.VMEM((IMAGES, 16, LANES), f32),
            pltpu.VMEM((BOXES, 5, 4, 256), f32),
            pltpu.VMEM((IMAGES * LANES, LANES), f32),
            pltpu.VMEM((8, 8, 8, LANES), f32),
            pltpu.VMEM((16, 4, 8, LANES), f32),
            pltpu.VMEM((128, 5, LANES), f32),
            pltpu.VMEM((n, 5, LANES), f32),
            pltpu.VMEM((n, 5, LANES), f32),
            pltpu.VMEM((8 * BOXES, LANES), f32),
            pltpu.VMEM((BOXES, 8, LANES), f32),
            pltpu.VMEM((n, 8, LANES), f32),
            pltpu.VMEM((20, BOXES, 256), f32),
            pltpu.VMEM((32, LANES), f32),
            pltpu.VMEM((ROWS, LANES), f32),
            pltpu.VMEM((2, 32, LANES), f32),
            pltpu.VMEM((2, ROWS, LANES), f32),
            pltpu.VMEM((2, LANES, 256), jnp.bfloat16),
            pltpu.VMEM((3, 512, LANES), jnp.bfloat16),
            pltpu.SemaphoreType.DMA((4,)),
            pltpu.SemaphoreType.DMA((6,)),
            pltpu.SemaphoreType.DMA((2,)),
            pltpu.SemaphoreType.DMA((2,)),
            pltpu.SemaphoreType.DMA((2, 4)),
        ],
        compiler_params=pltpu.CompilerParams(
            collective_id=0, has_side_effects=True, vmem_limit_bytes=VMEM_LIMIT
        ),
        name="levels",
    )(coarse, fine, sources, tiles)
    stack = shape((IMAGES, ROWS, LANES), f32)
    field = pltpu.VMEM((IMAGES, ROWS, LANES), f32)
    out, fine_out = pl.pallas_call(
        functools.partial(merge_kernel, n),
        out_shape=(stack, boxes),
        in_specs=[hbm] * 6,
        out_specs=(hbm,) * 2,
        scratch_shapes=[
            field,
            pltpu.VMEM((IMAGES, 16, LANES), f32),
            field,
            pltpu.VMEM((n, 8, LANES), f32),
            pltpu.SMEM((n,), jnp.int32),
            field,
            pltpu.SMEM((128,), jnp.int32),
            pltpu.VMEM((8, 8, LANES), f32),
            pltpu.VMEM((8, 16, 8, LANES), f32),
            pltpu.VMEM((BOXES, 5, 4, 256), f32),
            pltpu.SemaphoreType.DMA((6,)),
            pltpu.SemaphoreType.DMA,
            pltpu.SemaphoreType.DMA,
        ],
        compiler_params=pltpu.CompilerParams(vmem_limit_bytes=VMEM_LIMIT),
        name="merge",
    )(
        new.reshape(stack.shape),
        rows_x,
        flux_y.reshape(stack.shape),
        returned,
        wanted,
        fine_out,
    )
    return out.reshape(coarse_state.shape), fine_out.reshape(fine_state.shape)


def solution(mesh):
    return jax.shard_map(
        functools.partial(body, mesh.shape["gx"], mesh.shape["gy"]),
        mesh=mesh,
        in_specs=(
            P(None, None, "gx", "gy"),
            P("gx", "gy", None, None, None, None),
            P(None, "gy", None),
            P(None, "gy", None),
        ),
        out_specs=(P(None, None, "gx", "gy"), P("gx", "gy", None, None, None, None)),
        check_vma=False,
    )
```

```python
import functools

import jax
import jax.numpy as jnp
from jax import lax
from jax.experimental import pallas as pl
from jax.experimental.pallas import tpu as pltpu
from jax.sharding import PartitionSpec as P

MESH = pl.DeviceIdType.MESH
HEAT_RATIO = 1.4
HALF_STEP = 0.025
BOXES = 8
IMAGES = 10
ROWS = 64
LANES = 128
VMEM_LIMIT = 65280 * 1024


def iota(shape, dim):
    return lax.broadcasted_iota(jnp.int32, shape, dim)


def roll(x, shift, axis):
    if isinstance(shift, int):
        shift = shift % x.shape[axis]
        if shift == 0:
            return x
    return pltpu.roll(x, shift, axis)


def select_dot(values, weights):
    x = jnp.concatenate(values, axis=0)
    high = x.astype(jnp.bfloat16)
    x = x - high.astype(jnp.float32)
    middle = x.astype(jnp.bfloat16)
    low = (x - middle.astype(jnp.float32)).astype(jnp.bfloat16)
    parts = [
        jnp.dot(part, weights, preferred_element_type=jnp.float32) for part in (low, middle, high)
    ]
    return parts[0] + parts[1] + parts[2]


def primitives(u):
    inverse = 1.0 / u[0]
    velocity = [u[1] * inverse, u[2] * inverse, u[3] * inverse]
    kinetic = 0.5 * (u[1] * velocity[0] + u[2] * velocity[1] + u[3] * velocity[2])
    pressure = (HEAT_RATIO - 1.0) * (u[4] - kinetic)
    sound = jnp.sqrt(HEAT_RATIO * pressure * inverse)
    return velocity, pressure, sound


def scaled_state(u, velocity, pressure, sound, k):
    drift = HALF_STEP * velocity[k]
    speed = HALF_STEP * (jnp.abs(velocity[k]) + sound)
    return list(u) + [pressure, drift, speed]


def scaled_flux(state, k):
    u, pressure, drift = state[:5], state[5], state[6]
    flux = [u[f] * drift for f in range(5)]
    flux[1 + k] = flux[1 + k] + HALF_STEP * pressure
    flux[4] = (u[4] + pressure) * drift
    return flux


def face_flux(left, right, k):
    a, b = scaled_flux(left, k), scaled_flux(right, k)
    top = jnp.maximum(left[7], right[7])
    return [(a[f] + b[f]) - top * (right[f] - left[f]) for f in range(5)]


def coarse_step(img, flux_x, flux_y):
    row, col = iota((ROWS, LANES), 0), iota((ROWS, LANES), 1)
    cells, prims = [], []
    for z in range(2):
        u = [img[pl.ds((2 * f + z) * ROWS, ROWS), :] for f in range(5)]
        cells.append(u)
        prims.append(primitives(u))
    depth = [HALF_STEP * (jnp.abs(prims[z][0][0]) + prims[z][2]) for z in range(2)]
    depth = 2.0 * jnp.maximum(depth[0], depth[1])
    for z in range(2):
        u = cells[z]
        new = [u[f] - depth * (u[f] - cells[1 - z][f]) for f in range(5)]
        for k, axis, place, saved in ((1, 0, row, flux_x), (2, 1, col, flux_y)):
            state = scaled_state(u, *prims[z], k)
            before = [roll(s, 1, axis) for s in state]
            faces = face_flux(before, state, k)
            for f in range(5):
                face = jnp.where(place == 0, 0.0, faces[f])
                upper = roll(face, -1, axis)
                signed = jnp.where(place % 8 == 7, -upper, face)
                saved[pl.ds((2 * f + z) * ROWS, ROWS), :] = signed
                new[f] = new[f] - (upper - face)
        for f in range(5):
            img[pl.ds((IMAGES + 2 * f + z) * ROWS, ROWS), :] = new[f]


def build_tables(img, turned, table_x, table_y):
    for tx in range(1, 7):
        for k, row in ((0, 8 * tx - 1), (1, 8 * tx + 8)):
            for q in range(4):
                rows = img[pl.ds(5 * q * ROWS + row, 5, stride=ROWS), :]
                table_x[tx, 4 * k + q, pl.ds(0, 5), :] = rows
    for p in range(IMAGES):
        turned[pl.ds(p * LANES, LANES), :] = jnp.transpose(img[pl.ds(p * LANES, LANES), :])
    for ty in range(1, 15):
        for k, col in ((0, 8 * ty - 1), (1, 8 * ty + 8)):
            for h in range(2):
                rows = turned[pl.ds(5 * h * LANES + col, 5, stride=LANES), :]
                table_y[ty, 2 * k + h, pl.ds(0, 5), :] = rows


def wanted_tile(sources, tiles, o, me):
    tile = jnp.int32(0)
    for r in range(BOXES):
        tile = jnp.where(sources[r, o] == me, tiles[r, o], tile)
    return tile


def pack_rims(n, me, sources, tiles, table_x, table_y, by_tile, rims, wanted, box_of):
    group = iota((8, LANES), 1) // 8
    for tx in range(1, 7):
        for ty in range(1, 15):
            message = roll(table_x[tx, 0], -8 * ty, 1)
            for g in range(1, 8):
                part = roll(table_x[tx, g], 8 * g - 8 * ty, 1)
                message = jnp.where(group == g, part, message)
            for u in range(4):
                columns = table_y[ty, u]
                for j in range(2):
                    part = roll(columns, 64 + 16 * u + 8 * j - 64 * j - 8 * tx, 1)
                    message = jnp.where(group == 8 + 2 * u + j, part, message)
            by_tile[16 * tx + ty] = message[:5]

    def one(o, carry):
        tile = wanted_tile(sources, tiles, o, me)
        wanted[o] = tile
        rims[o] = by_tile[jnp.maximum(tile, 17)]
        box = jnp.int32(0)
        for r in range(BOXES):
            box = jnp.where(sources[r, me] == o, r, box)
        box_of[o] = box
        return carry

    lax.fori_loop(0, n, one, 0)


def pack_halo(img, halo_rows, halo_cols):
    halo_rows[...] = jnp.zeros_like(halo_rows)
    halo_rows[pl.ds(0, 8), :] = img[pl.ds(0, 8, stride=ROWS), :]
    halo_rows[pl.ds(8, 2), :] = img[pl.ds(8 * ROWS, 2, stride=ROWS), :]
    halo_rows[pl.ds(16, 8), :] = img[pl.ds(ROWS - 1, 8, stride=ROWS), :]
    halo_rows[pl.ds(24, 2), :] = img[pl.ds(9 * ROWS - 1, 2, stride=ROWS), :]
    lane = iota((ROWS, LANES), 1)
    packed = jnp.ones((ROWS, LANES), jnp.float32)
    for image in range(IMAGES):
        cells = img[pl.ds(image * ROWS, ROWS), :]
        packed = jnp.where(lane == image, roll(cells, image, 1), packed)
        packed = jnp.where(lane == 16 + image, roll(cells, 17 + image, 1), packed)
    halo_cols[...] = packed


def finish_edges(img, halo_rows, halo_cols, from_rows, from_cols):
    def by_row(source, start):
        u = [source[pl.ds(start + 2 * f, 2), :] for f in range(5)]
        return scaled_state(u, *primitives(u), 1)

    own_low, own_high = by_row(halo_rows, 0), by_row(halo_rows, 16)
    low = face_flux(by_row(from_rows.at[0], 16), own_low, 1)
    high = face_flux(own_high, by_row(from_rows.at[1], 0), 1)
    for f in range(5):
        for z in range(2):
            base = (IMAGES + 2 * f + z) * ROWS
            first, last = pl.ds(base, 1), pl.ds(base + ROWS - 1, 1)
            img[first, :] = img[first, :] + low[f][z : z + 1]
            img[last, :] = img[last, :] - high[f][z : z + 1]

    lane = iota((ROWS, LANES), 1)
    own = halo_cols[...]
    left = jnp.where(lane < 16, roll(from_cols[0], -16, 1), own)
    right = jnp.where(lane < 16, own, roll(from_cols[1], 16, 1))

    def by_lane(packed):
        u = [roll(packed, -2 * f, 1) for f in range(5)]
        return scaled_state(u, *primitives(u), 2)

    faces = face_flux(by_lane(left), by_lane(right), 2)
    for f in range(5):
        for z in range(2):
            rows = pl.ds((IMAGES + 2 * f + z) * ROWS, ROWS)
            cells = img[rows, :]
            cells = jnp.where(lane == 0, cells + roll(faces[f], -z, 1), cells)
            cells = jnp.where(lane == LANES - 1, cells - roll(faces[f], 111 - z, 1), cells)
            img[rows, :] = cells


def spread_weights(weights):
    source, cell = iota((LANES, 256), 0), iota((LANES, 256), 1)
    a, b = cell // 16, cell % 16
    for side, (along, across) in enumerate(((b, a), (a, b))):
        chosen = (source < 16) & (source % 8 == along // 2) & (source // 8 == across // 8)
        weights[side] = jnp.where(chosen, 1.0, 0.0).astype(jnp.bfloat16)


def gather_weights(weights):
    source, target = iota((512, LANES), 0), iota((512, LANES), 1)
    cell, half = source % 256, source // 256
    a, b = cell // 16, cell % 16
    row, lane = target // 16 == a // 2, target % 16
    average = row & (lane == 8 * half + b // 2)
    low_col = row & (lane == 2 * half) & (b == 0)
    high_col = row & (lane == 2 * half + 1) & (b == 15)
    low_row = (target == 16 * half + b // 2) & (a == 0)
    high_row = (target == 16 * half + 8 + b // 2) & (a == 15)
    for i, (low, high) in enumerate(((None, average), (low_col, high_col), (low_row, high_row))):
        values = jnp.where(high, 0.125, 0.0)
        if low is not None:
            values = jnp.where(low, -0.125, values)
        weights[i] = values.astype(jnp.bfloat16)


def own_rims(me, sources, rims, held, weights):
    for r in range(BOXES):
        held[pl.ds(8 * r, 5), :] = rims[sources[r, me]]
    by_row = [held[pl.ds(s, BOXES, stride=8), :] for s in range(5)]
    lane = iota((BOXES, LANES), 1)

    def pair(low, low_lane, high, high_lane):
        first = roll(low, -low_lane, 1)
        second = roll(high, 8 - high_lane, 1)
        return jnp.where(lane < 8, first, jnp.where(lane < 16, second, 0.0))

    sides = [[], []]
    for image in range(2 * IMAGES):
        row, q = by_row[image % 5], image // 5
        sides[0].append(pair(row, 8 * q, row, 32 + 8 * q))
        p, j = image // 2, image % 2
        row, lane_j = by_row[p % 5], 16 * (p // 5) + 8 * j
        sides[1].append(pair(row, 64 + lane_j, row, 96 + lane_j))

    spread = []
    for side in range(2):
        old = sides[side][:IMAGES]
        mid = [0.5 * (x + y) for x, y in zip(old, sides[side][IMAGES:])]
        ghosts = select_dot(old + mid, weights[side])
        spread.append(
            [
                [ghosts[(IMAGES * t + i) * 8 : (IMAGES * t + i) * 8 + 8] for i in range(IMAGES)]
                for t in range(2)
            ]
        )
    return spread


def fine_step(u, ghosts_x, ghosts_y, edges):
    cell = iota((BOXES, 256), 1)
    a, b = cell // 16, cell % 16
    prims = [primitives([u[f][z] for f in range(5)]) for z in range(4)]
    states = [scaled_state([u[f][z] for f in range(5)], *prims[z], 0) for z in range(4)]
    deep = [face_flux(states[z], states[(z + 1) % 4], 0) for z in range(4)]
    new = [[u[f][z] - (deep[z][f] - deep[z - 1][f]) for z in range(4)] for f in range(5)]
    sides = (
        (1, ghosts_x, 16, a == 0, a == 15, a < 8),
        (2, ghosts_y, 1, b == 0, b == 15, b < 8),
    )
    for side, (k, ghosts, stride, first, last, lower) in enumerate(sides):
        for half in range(2):
            cells = [ghosts[2 * f + half] for f in range(5)]
            ghost = scaled_state(cells, *primitives(cells), k)
            for z in (2 * half, 2 * half + 1):
                state = scaled_state([u[f][z] for f in range(5)], *prims[z], k)
                before = [
                    jnp.where(first, ghost[i], roll(state[i], stride, 1)) for i in range(8)
                ]
                low = face_flux(before, state, k)
                outer = face_flux(state, ghost, k)
                for f in range(5):
                    high = jnp.where(last, outer[f], roll(low[f], -stride, 1))
                    new[f][z] = new[f][z] - (high - low[f])
                    edge = jnp.where(lower, low[f], high)
                    held = edges[side][2 * f + half]
                    edges[side][2 * f + half] = edge if held is None else held + edge
    return new


def pack_results(u, edges, weights, held, packed):
    thick = [u[i // 2][2 * (i % 2)] + u[i // 2][2 * (i % 2) + 1] for i in range(IMAGES)]

    def pairs(values, i):
        rows = [jnp.concatenate(values[2 * p : 2 * p + 2], axis=1) for p in range(5)]
        sums = select_dot(rows, weights[i])
        return [sums[8 * p : 8 * p + 8] for p in range(5)]

    inner, cols, rows = pairs(thick, 0), pairs(edges[1], 1), pairs(edges[0], 2)
    lane = iota((BOXES, LANES), 1)
    first_cols = cols[0]
    for p in range(1, 4):
        first_cols = jnp.where(lane % 16 // 4 == p, roll(cols[p], 4 * p, 1), first_cols)
    for i in range(8):
        message = roll(cols[4], 120 - 16 * i, 1)
        message = jnp.where(lane < 120, roll(first_cols, 104 - 16 * i, 1), message)
        if i < 4:
            start = 16 * (i % 2) + 8 * (i // 2)
            message = jnp.where(lane < 104, roll(rows[4], 96 - start, 1), message)
        message = jnp.where(lane < 96, roll(rows[i // 2], 80 - 16 * (i % 2), 1), message)
        for p in range(4, -1, -1):
            part = roll(inner[p], 16 * (p - i), 1)
            message = jnp.where(lane < 16 * p + 16, part, message)
        held[pl.ds(i, BOXES, stride=8), :] = message
    for r in range(BOXES):
        packed[r] = held[pl.ds(8 * r, 8), :]


def far_first(n):
    side = round(n**0.5)
    steps = [(a, b) for a in range(side) for b in range(side) if a or b]
    return side, sorted(steps, key=lambda s: -sum(min(x, side - x) for x in s))


def partners(n, me):
    side, steps = far_first(n)
    high, low = me // side, lax.rem(me, side)
    for a, b in steps:
        yield lax.rem(high + a, side) * side + lax.rem(low + b, side)


def send(me, other, source, target, sems):
    pltpu.make_async_remote_copy(
        src_ref=source.at[other],
        dst_ref=target.at[me],
        send_sem=sems.at[0],
        recv_sem=sems.at[1],
        device_id={"gx": other},
        device_id_type=MESH,
    ).start()


def all_slots(n, me, source, target, sems):
    return pltpu.make_async_remote_copy(
        src_ref=source.at[pl.ds(0, n - 1)],
        dst_ref=target.at[pl.ds(0, n - 1)],
        send_sem=sems.at[0],
        recv_sem=sems.at[1],
        device_id={"gx": me},
        device_id_type=MESH,
    )


def level_kernel(
    n,
    m,
    coarse,
    fine_in,
    sources_in,
    tiles_in,
    coarse_new,
    rows_x_out,
    flux_y_out,
    returned,
    fine_out,
    wanted_out,
    sources,
    tiles,
    wanted,
    box_of,
    img,
    flux_x,
    flux_y,
    rows_x,
    fine,
    turned,
    table_x,
    table_y,
    by_tile,
    rims,
    rims_in,
    held,
    packed,
    results,
    cells,
    halo_rows,
    halo_cols,
    from_rows,
    from_cols,
    spread,
    gather,
    load_sems,
    store_sems,
    rim_sems,
    result_sems,
    halo_sems,
):
    me, column = lax.axis_index("gx"), lax.axis_index("gy")
    up, down = lax.rem(me + 1, n), lax.rem(me + n - 1, n)
    right, left = lax.rem(column + 1, m), lax.rem(column + m - 1, m)
    barrier = pltpu.get_barrier_semaphore()

    for other in partners(n, me):
        pl.semaphore_signal(barrier, 1, device_id={"gx": other}, device_id_type=MESH)
    pl.semaphore_signal(barrier, 1, device_id={"gy": right}, device_id_type=MESH)
    pl.semaphore_signal(barrier, 1, device_id={"gy": left}, device_id_type=MESH)

    old, new = pl.ds(0, IMAGES * ROWS), pl.ds(IMAGES * ROWS, IMAGES * ROWS)
    load = pltpu.make_async_copy(coarse, img.at[old], load_sems.at[0])
    load_fine = pltpu.make_async_copy(fine_in, fine, load_sems.at[1])
    load_sources = pltpu.make_async_copy(sources_in, sources, load_sems.at[2])
    load_tiles = pltpu.make_async_copy(tiles_in, tiles, load_sems.at[3])
    load.start()
    load_sources.start()
    load_tiles.start()
    load_fine.start()
    load.wait()
    coarse_step(img, flux_x, flux_y)
    for image in range(IMAGES):
        for i in range(2):
            rows = flux_x[pl.ds(image * ROWS + 7 * i, 8, stride=8), :]
            rows_x[image, pl.ds(8 * i, 8), :] = rows
    stores = [
        pltpu.make_async_copy(rows_x, rows_x_out, store_sems.at[0]),
        pltpu.make_async_copy(flux_y, flux_y_out, store_sems.at[1]),
    ]
    stores[0].start()
    stores[1].start()
    table_x[...] = jnp.zeros_like(table_x)
    table_y[...] = jnp.zeros_like(table_y)
    build_tables(img, turned, table_x, table_y)
    load_sources.wait()
    load_tiles.wait()
    pack_rims(n, me, sources, tiles, table_x, table_y, by_tile, rims, wanted, box_of)
    rims_in[me] = rims[me]
    stores.append(pltpu.make_async_copy(wanted, wanted_out, store_sems.at[2]))
    stores[2].start()
    pack_halo(img, halo_rows, halo_cols)
    load_fine.wait()
    for r in range(BOXES):
        for f in range(5):
            for z in range(4):
                cells[4 * f + z, pl.ds(r, 1), :] = fine[r, f, pl.ds(z, 1), :]
    spread_weights(spread)
    gather_weights(gather)
    pl.semaphore_wait(barrier, n + 1)

    for other in partners(n, me):
        send(me, other, rims, rims_in, rim_sems)
    halos = []
    for i, (source, target, where) in enumerate(
        (
            (halo_rows, from_rows.at[0], {"gx": up}),
            (halo_rows, from_rows.at[1], {"gx": down}),
            (halo_cols, from_cols.at[0], {"gy": right}),
            (halo_cols, from_cols.at[1], {"gy": left}),
        )
    ):
        copy = pltpu.make_async_remote_copy(
            src_ref=source,
            dst_ref=target,
            send_sem=halo_sems.at[0, i],
            recv_sem=halo_sems.at[1, i],
            device_id=where,
            device_id_type=MESH,
        )
        copy.start()
        halos.append(copy)

    rim_copies = all_slots(n, me, rims, rims_in, rim_sems)
    rim_copies.wait_recv()
    ghosts = own_rims(me, sources, rims_in, held, spread)
    u = [[cells[4 * f + z] for z in range(4)] for f in range(5)]
    edges = [[None] * IMAGES, [None] * IMAGES]
    u = fine_step(u, ghosts[0][0], ghosts[1][0], edges)
    u = fine_step(u, ghosts[0][1], ghosts[1][1], edges)
    pack_results(u, edges, gather, held, packed)
    for other in partners(n, me):
        results[other] = packed[box_of[other]]
        send(me, other, results, returned, result_sems)
    results[me] = packed[box_of[me]]
    stores.append(pltpu.make_async_copy(results.at[me], returned.at[me], store_sems.at[3]))
    stores[3].start()
    for f in range(5):
        for z in range(4):
            for r in range(BOXES):
                fine[r, f, pl.ds(z, 1), :] = u[f][z][r : r + 1]
    stores.append(pltpu.make_async_copy(fine, fine_out, store_sems.at[4]))
    stores[4].start()
    for copy in halos:
        copy.wait_recv()
    finish_edges(img, halo_rows, halo_cols, from_rows, from_cols)
    stores.append(pltpu.make_async_copy(img.at[new], coarse_new, store_sems.at[5]))
    stores[5].start()
    rim_copies.wait_send()
    for copy in halos:
        copy.wait_send()
    for copy in stores:
        copy.wait()
    result_copies = all_slots(n, me, results, returned, result_sems)
    result_copies.wait_send()
    result_copies.wait_recv()


def merge_kernel(
    n,
    new_in,
    rows_x_in,
    flux_y_in,
    returned_in,
    wanted_in,
    fine_in,
    out_to,
    fine_out,
    new,
    rows_x,
    flux_y,
    returned,
    wanted,
    out,
    slots,
    covered_in,
    turned,
    fine,
    sems,
    out_sem,
    fine_sem,
):
    pairs = (
        (wanted_in, wanted),
        (returned_in, returned),
        (new_in, new),
        (rows_x_in, rows_x),
        (flux_y_in, flux_y),
        (fine_in, fine),
    )
    loads = [pltpu.make_async_copy(a, b, sems.at[i]) for i, (a, b) in enumerate(pairs)]
    for copy in loads:
        copy.start()
    lane, sub = iota((8, LANES), 1), iota((8, LANES), 0)

    def clear(t, carry):
        slots[t] = -1
        return carry

    def place(o, carry):
        slots[wanted[o]] = o
        return carry

    lax.fori_loop(0, 128, clear, 0, unroll=8)
    loads[0].wait()
    lax.fori_loop(0, n, place, 0, unroll=8)
    blank = jnp.zeros((8, LANES), jnp.float32)
    group = lane // 8
    for tx in (0, 7):
        covered_in[tx] = blank
        for i in range(16):
            turned[tx, i] = blank

    def row_of_tiles(tx, carry):
        covered = blank
        diagonals = [blank] * 16
        for ty in range(1, 15):
            slot = slots[16 * tx + ty]
            live = (slot >= 0).astype(jnp.int32)
            message = returned[jnp.maximum(slot, 0)]
            covered = jnp.where(lane // 8 == jnp.where(live > 0, ty, -1), 1.0, covered)
            for d in range(16):
                i = (ty - d) % 16
                diagonals[d] = jnp.where(group == i, message, diagonals[d])
        diagonals = [roll(diagonals[d], 8 * d, 1) for d in range(16)]
        covered_in[tx] = covered
        for i in range(16):
            part = diagonals[(1 - i) % 16]
            for ty in range(2, 15):
                part = jnp.where(group == ty, diagonals[(ty - i) % 16], part)
            turned[tx, i] = part
        return carry

    loads[1].wait()
    lax.fori_loop(1, 7, row_of_tiles, 0, unroll=6)
    loads[5].wait()
    store_fine = pltpu.make_async_copy(fine, fine_out, fine_sem)
    store_fine.start()
    for copy in loads[2:5]:
        copy.wait()

    def finish(tx, carry):
        above, below = jnp.minimum(tx + 1, 7), jnp.maximum(tx - 1, 0)
        cover = covered_in[tx]
        covered = cover > 0.5
        last = lane % 8 == 7
        touched = last & (roll(cover, -1, 1) > 0.5) | (lane % 8 == 0) & (roll(cover, 1, 1) > 0.5)
        beside = (sub == 7) & (covered_in[above] > 0.5) | (sub == 0) & (covered_in[below] > 0.5)
        rows = pl.ds(pl.multiple_of(8 * tx, 8), 8)
        low, high = [turned[above, 10 + g] for g in range(3)], [turned[below, 10 + g] for g in range(3)]
        cols = [turned[tx, 13 + g] for g in range(3)]
        for image in range(IMAGES):
            if image < 8:
                lows, highs = low[0][image : image + 1], high[1][image : image + 1]
            else:
                lows, highs = low[2][image - 8 : image - 7], high[2][image - 6 : image - 5]
            place = 2 * (image % 4)
            value = cols[image // 4]
            value = jnp.where(last, roll(value, -1 - place, 1), roll(value, 7 - place, 1))
            cells = new[image, rows, :] + jnp.where(touched, value - flux_y[image, rows, :], 0.0)
            lows = lows - rows_x[image, pl.ds(8 + tx, 1), :]
            highs = highs - rows_x[image, pl.ds(tx, 1), :]
            cells = cells + jnp.where(beside, jnp.where(sub == 7, lows, highs), 0.0)
            out[image, rows, :] = jnp.where(covered, turned[tx, image], cells)
        pltpu.make_async_copy(out.at[:, rows], out_to.at[:, rows], out_sem).start()
        return carry

    lax.fori_loop(0, 8, finish, 0, unroll=8)
    pltpu.make_async_copy(out, out_to, out_sem).wait()
    store_fine.wait()


def body(n, m, coarse_state, fine_state, source_rows, tile_ids):
    hbm = pl.BlockSpec(memory_space=pltpu.HBM)
    f32 = jnp.float32
    coarse = coarse_state.reshape(IMAGES * ROWS, LANES)
    fine = fine_state.reshape(BOXES, 5, 4, 256)
    sources = source_rows.reshape(n, BOXES).T
    tiles = tile_ids.reshape(n, BOXES).T
    shape = jax.ShapeDtypeStruct
    image = shape((IMAGES * ROWS, LANES), f32)
    boxes = shape((BOXES, 5, 4, 256), f32)
    new, rows_x, flux_y, returned, fine_out, wanted = pl.pallas_call(
        functools.partial(level_kernel, n, m),
        out_shape=(
            image,
            shape((IMAGES, 16, LANES), f32),
            image,
            shape((n, 8, LANES), f32),
            boxes,
            shape((n,), jnp.int32),
        ),
        in_specs=[hbm] * 4,
        out_specs=(hbm,) * 6,
        scratch_shapes=[
            pltpu.SMEM((BOXES, n), jnp.int32),
            pltpu.SMEM((BOXES, n), jnp.int32),
            pltpu.SMEM((n,), jnp.int32),
            pltpu.SMEM((n,), jnp.int32),
            pltpu.VMEM((2 * IMAGES * ROWS, LANES), f32),
            pltpu.VMEM((IMAGES * ROWS, LANES), f32),
            pltpu.VMEM((IMAGES * ROWS, LANES), f32),
            pltpu.VMEM((IMAGES, 16, LANES), f32),
            pltpu.VMEM((BOXES, 5, 4, 256), f32),
            pltpu.VMEM((IMAGES * LANES, LANES), f32),
            pltpu.VMEM((8, 8, 8, LANES), f32),
            pltpu.VMEM((16, 4, 8, LANES), f32),
            pltpu.VMEM((128, 5, LANES), f32),
            pltpu.VMEM((n, 5, LANES), f32),
            pltpu.VMEM((n, 5, LANES), f32),
            pltpu.VMEM((8 * BOXES, LANES), f32),
            pltpu.VMEM((BOXES, 8, LANES), f32),
            pltpu.VMEM((n, 8, LANES), f32),
            pltpu.VMEM((20, BOXES, 256), f32),
            pltpu.VMEM((32, LANES), f32),
            pltpu.VMEM((ROWS, LANES), f32),
            pltpu.VMEM((2, 32, LANES), f32),
            pltpu.VMEM((2, ROWS, LANES), f32),
            pltpu.VMEM((2, LANES, 256), jnp.bfloat16),
            pltpu.VMEM((3, 512, LANES), jnp.bfloat16),
            pltpu.SemaphoreType.DMA((4,)),
            pltpu.SemaphoreType.DMA((6,)),
            pltpu.SemaphoreType.DMA((2,)),
            pltpu.SemaphoreType.DMA((2,)),
            pltpu.SemaphoreType.DMA((2, 4)),
        ],
        compiler_params=pltpu.CompilerParams(
            collective_id=0, has_side_effects=True, vmem_limit_bytes=VMEM_LIMIT
        ),
        name="levels",
    )(coarse, fine, sources, tiles)
    stack = shape((IMAGES, ROWS, LANES), f32)
    field = pltpu.VMEM((IMAGES, ROWS, LANES), f32)
    out, fine_out = pl.pallas_call(
        functools.partial(merge_kernel, n),
        out_shape=(stack, boxes),
        in_specs=[hbm] * 6,
        out_specs=(hbm,) * 2,
        scratch_shapes=[
            field,
            pltpu.VMEM((IMAGES, 16, LANES), f32),
            field,
            pltpu.VMEM((n, 8, LANES), f32),
            pltpu.SMEM((n,), jnp.int32),
            field,
            pltpu.SMEM((128,), jnp.int32),
            pltpu.VMEM((8, 8, LANES), f32),
            pltpu.VMEM((8, 16, 8, LANES), f32),
            pltpu.VMEM((BOXES, 5, 4, 256), f32),
            pltpu.SemaphoreType.DMA((6,)),
            pltpu.SemaphoreType.DMA,
            pltpu.SemaphoreType.DMA,
        ],
        compiler_params=pltpu.CompilerParams(vmem_limit_bytes=VMEM_LIMIT),
        name="merge",
    )(
        new.reshape(stack.shape),
        rows_x,
        flux_y.reshape(stack.shape),
        returned,
        wanted,
        fine_out,
    )
    return out.reshape(coarse_state.shape), fine_out.reshape(fine_state.shape)


def solution(mesh):
    return jax.shard_map(
        functools.partial(body, mesh.shape["gx"], mesh.shape["gy"]),
        mesh=mesh,
        in_specs=(
            P(None, None, "gx", "gy"),
            P("gx", "gy", None, None, None, None),
            P(None, "gy", None),
            P(None, "gy", None),
        ),
        out_specs=(P(None, None, "gx", "gy"), P("gx", "gy", None, None, None, None)),
        check_vma=False,
    )
```

```python
import functools

import jax
import jax.numpy as jnp
from jax import lax
from jax.experimental import pallas as pl
from jax.experimental.pallas import tpu as pltpu
from jax.sharding import PartitionSpec as P

MESH = pl.DeviceIdType.MESH
HEAT_RATIO = 1.4
HALF_STEP = 0.025
BOXES = 8
IMAGES = 10
ROWS = 64
LANES = 128
VMEM_LIMIT = 65280 * 1024


def iota(shape, dim):
    return lax.broadcasted_iota(jnp.int32, shape, dim)


def roll(x, shift, axis):
    if isinstance(shift, int):
        shift = shift % x.shape[axis]
        if shift == 0:
            return x
    return pltpu.roll(x, shift, axis)


def select_dot(values, weights):
    x = jnp.concatenate(values, axis=0)
    high = x.astype(jnp.bfloat16)
    x = x - high.astype(jnp.float32)
    middle = x.astype(jnp.bfloat16)
    low = (x - middle.astype(jnp.float32)).astype(jnp.bfloat16)
    parts = [
        jnp.dot(part, weights, preferred_element_type=jnp.float32) for part in (low, middle, high)
    ]
    return parts[0] + parts[1] + parts[2]


def primitives(u):
    inverse = 1.0 / u[0]
    velocity = [u[1] * inverse, u[2] * inverse, u[3] * inverse]
    kinetic = 0.5 * (u[1] * velocity[0] + u[2] * velocity[1] + u[3] * velocity[2])
    pressure = (HEAT_RATIO - 1.0) * (u[4] - kinetic)
    sound = jnp.sqrt(HEAT_RATIO * pressure * inverse)
    return velocity, pressure, sound


def scaled_state(u, velocity, pressure, sound, k):
    drift = HALF_STEP * velocity[k]
    speed = HALF_STEP * (jnp.abs(velocity[k]) + sound)
    return list(u) + [pressure, drift, speed]


def scaled_flux(state, k):
    u, pressure, drift = state[:5], state[5], state[6]
    flux = [u[f] * drift for f in range(5)]
    flux[1 + k] = flux[1 + k] + HALF_STEP * pressure
    flux[4] = (u[4] + pressure) * drift
    return flux


def face_flux(left, right, k):
    a, b = scaled_flux(left, k), scaled_flux(right, k)
    top = jnp.maximum(left[7], right[7])
    return [(a[f] + b[f]) - top * (right[f] - left[f]) for f in range(5)]


def coarse_step(img, flux_x, flux_y):
    row, col = iota((ROWS, LANES), 0), iota((ROWS, LANES), 1)
    cells, prims = [], []
    for z in range(2):
        u = [img[pl.ds((2 * f + z) * ROWS, ROWS), :] for f in range(5)]
        cells.append(u)
        prims.append(primitives(u))
    depth = [HALF_STEP * (jnp.abs(prims[z][0][0]) + prims[z][2]) for z in range(2)]
    depth = 2.0 * jnp.maximum(depth[0], depth[1])
    for z in range(2):
        u = cells[z]
        new = [u[f] - depth * (u[f] - cells[1 - z][f]) for f in range(5)]
        for k, axis, place, saved in ((1, 0, row, flux_x), (2, 1, col, flux_y)):
            state = scaled_state(u, *prims[z], k)
            before = [roll(s, 1, axis) for s in state]
            faces = face_flux(before, state, k)
            for f in range(5):
                face = jnp.where(place == 0, 0.0, faces[f])
                upper = roll(face, -1, axis)
                signed = jnp.where(place % 8 == 7, -upper, face)
                saved[pl.ds((2 * f + z) * ROWS, ROWS), :] = signed
                new[f] = new[f] - (upper - face)
        for f in range(5):
            img[pl.ds((IMAGES + 2 * f + z) * ROWS, ROWS), :] = new[f]


def build_tables(img, turned, table_x, table_y):
    for tx in range(1, 7):
        for k, row in ((0, 8 * tx - 1), (1, 8 * tx + 8)):
            for q in range(4):
                rows = img[pl.ds(5 * q * ROWS + row, 5, stride=ROWS), :]
                table_x[tx, 4 * k + q, pl.ds(0, 5), :] = rows
    for p in range(IMAGES):
        turned[pl.ds(p * LANES, LANES), :] = jnp.transpose(img[pl.ds(p * LANES, LANES), :])
    for ty in range(1, 15):
        for k, col in ((0, 8 * ty - 1), (1, 8 * ty + 8)):
            for h in range(2):
                rows = turned[pl.ds(5 * h * LANES + col, 5, stride=LANES), :]
                table_y[ty, 2 * k + h, pl.ds(0, 5), :] = rows


def wanted_tile(sources, tiles, o, me):
    tile = jnp.int32(0)
    for r in range(BOXES):
        tile = jnp.where(sources[r, o] == me, tiles[r, o], tile)
    return tile


def pack_rims(n, me, sources, tiles, table_x, table_y, by_tile, rims, wanted, box_of):
    group = iota((8, LANES), 1) // 8
    for tx in range(1, 7):
        for ty in range(1, 15):
            message = roll(table_x[tx, 0], -8 * ty, 1)
            for g in range(1, 8):
                part = roll(table_x[tx, g], 8 * g - 8 * ty, 1)
                message = jnp.where(group == g, part, message)
            for u in range(4):
                columns = table_y[ty, u]
                for j in range(2):
                    part = roll(columns, 64 + 16 * u + 8 * j - 64 * j - 8 * tx, 1)
                    message = jnp.where(group == 8 + 2 * u + j, part, message)
            by_tile[16 * tx + ty] = message[:5]

    def one(o, carry):
        tile = wanted_tile(sources, tiles, o, me)
        wanted[o] = tile
        rims[o] = by_tile[jnp.maximum(tile, 17)]
        box = jnp.int32(0)
        for r in range(BOXES):
            box = jnp.where(sources[r, me] == o, r, box)
        box_of[o] = box
        return carry

    lax.fori_loop(0, n, one, 0, unroll=8)


def pack_halo(img, halo_rows, halo_cols):
    halo_rows[...] = jnp.zeros_like(halo_rows)
    halo_rows[pl.ds(0, 8), :] = img[pl.ds(0, 8, stride=ROWS), :]
    halo_rows[pl.ds(8, 2), :] = img[pl.ds(8 * ROWS, 2, stride=ROWS), :]
    halo_rows[pl.ds(16, 8), :] = img[pl.ds(ROWS - 1, 8, stride=ROWS), :]
    halo_rows[pl.ds(24, 2), :] = img[pl.ds(9 * ROWS - 1, 2, stride=ROWS), :]
    lane = iota((ROWS, LANES), 1)
    packed = jnp.ones((ROWS, LANES), jnp.float32)
    for image in range(IMAGES):
        cells = img[pl.ds(image * ROWS, ROWS), :]
        packed = jnp.where(lane == image, roll(cells, image, 1), packed)
        packed = jnp.where(lane == 16 + image, roll(cells, 17 + image, 1), packed)
    halo_cols[...] = packed


def finish_edges(img, halo_rows, halo_cols, from_rows, from_cols):
    def by_row(source, start):
        u = [source[pl.ds(start + 2 * f, 2), :] for f in range(5)]
        return scaled_state(u, *primitives(u), 1)

    own_low, own_high = by_row(halo_rows, 0), by_row(halo_rows, 16)
    low = face_flux(by_row(from_rows.at[0], 16), own_low, 1)
    high = face_flux(own_high, by_row(from_rows.at[1], 0), 1)
    for f in range(5):
        for z in range(2):
            base = (IMAGES + 2 * f + z) * ROWS
            first, last = pl.ds(base, 1), pl.ds(base + ROWS - 1, 1)
            img[first, :] = img[first, :] + low[f][z : z + 1]
            img[last, :] = img[last, :] - high[f][z : z + 1]

    lane = iota((ROWS, LANES), 1)
    own = halo_cols[...]
    left = jnp.where(lane < 16, roll(from_cols[0], -16, 1), own)
    right = jnp.where(lane < 16, own, roll(from_cols[1], 16, 1))

    def by_lane(packed):
        u = [roll(packed, -2 * f, 1) for f in range(5)]
        return scaled_state(u, *primitives(u), 2)

    faces = face_flux(by_lane(left), by_lane(right), 2)
    for f in range(5):
        for z in range(2):
            rows = pl.ds((IMAGES + 2 * f + z) * ROWS, ROWS)
            cells = img[rows, :]
            cells = jnp.where(lane == 0, cells + roll(faces[f], -z, 1), cells)
            cells = jnp.where(lane == LANES - 1, cells - roll(faces[f], 111 - z, 1), cells)
            img[rows, :] = cells


def spread_weights(weights):
    source, cell = iota((LANES, 256), 0), iota((LANES, 256), 1)
    a, b = cell // 16, cell % 16
    for side, (along, across) in enumerate(((b, a), (a, b))):
        chosen = (source < 16) & (source % 8 == along // 2) & (source // 8 == across // 8)
        weights[side] = jnp.where(chosen, 1.0, 0.0).astype(jnp.bfloat16)


def gather_weights(weights):
    source, target = iota((512, LANES), 0), iota((512, LANES), 1)
    cell, half = source % 256, source // 256
    a, b = cell // 16, cell % 16
    row, lane = target // 16 == a // 2, target % 16
    average = row & (lane == 8 * half + b // 2)
    low_col = row & (lane == 2 * half) & (b == 0)
    high_col = row & (lane == 2 * half + 1) & (b == 15)
    low_row = (target == 16 * half + b // 2) & (a == 0)
    high_row = (target == 16 * half + 8 + b // 2) & (a == 15)
    for i, (low, high) in enumerate(((None, average), (low_col, high_col), (low_row, high_row))):
        values = jnp.where(high, 0.125, 0.0)
        if low is not None:
            values = jnp.where(low, -0.125, values)
        weights[i] = values.astype(jnp.bfloat16)


def own_rims(me, sources, rims, held, weights):
    for r in range(BOXES):
        held[pl.ds(8 * r, 5), :] = rims[sources[r, me]]
    by_row = [held[pl.ds(s, BOXES, stride=8), :] for s in range(5)]
    lane = iota((BOXES, LANES), 1)

    def pair(low, low_lane, high, high_lane):
        first = roll(low, -low_lane, 1)
        second = roll(high, 8 - high_lane, 1)
        return jnp.where(lane < 8, first, jnp.where(lane < 16, second, 0.0))

    sides = [[], []]
    for image in range(2 * IMAGES):
        row, q = by_row[image % 5], image // 5
        sides[0].append(pair(row, 8 * q, row, 32 + 8 * q))
        p, j = image // 2, image % 2
        row, lane_j = by_row[p % 5], 16 * (p // 5) + 8 * j
        sides[1].append(pair(row, 64 + lane_j, row, 96 + lane_j))

    spread = []
    for side in range(2):
        old = sides[side][:IMAGES]
        mid = [0.5 * (x + y) for x, y in zip(old, sides[side][IMAGES:])]
        ghosts = select_dot(old + mid, weights[side])
        spread.append(
            [
                [ghosts[(IMAGES * t + i) * 8 : (IMAGES * t + i) * 8 + 8] for i in range(IMAGES)]
                for t in range(2)
            ]
        )
    return spread


def fine_step(u, ghosts_x, ghosts_y, edges):
    cell = iota((BOXES, 256), 1)
    a, b = cell // 16, cell % 16
    prims = [primitives([u[f][z] for f in range(5)]) for z in range(4)]
    states = [scaled_state([u[f][z] for f in range(5)], *prims[z], 0) for z in range(4)]
    deep = [face_flux(states[z], states[(z + 1) % 4], 0) for z in range(4)]
    new = [[u[f][z] - (deep[z][f] - deep[z - 1][f]) for z in range(4)] for f in range(5)]
    sides = (
        (1, ghosts_x, 16, a == 0, a == 15, a < 8),
        (2, ghosts_y, 1, b == 0, b == 15, b < 8),
    )
    for side, (k, ghosts, stride, first, last, lower) in enumerate(sides):
        for half in range(2):
            cells = [ghosts[2 * f + half] for f in range(5)]
            ghost = scaled_state(cells, *primitives(cells), k)
            for z in (2 * half, 2 * half + 1):
                state = scaled_state([u[f][z] for f in range(5)], *prims[z], k)
                before = [
                    jnp.where(first, ghost[i], roll(state[i], stride, 1)) for i in range(8)
                ]
                low = face_flux(before, state, k)
                outer = face_flux(state, ghost, k)
                for f in range(5):
                    high = jnp.where(last, outer[f], roll(low[f], -stride, 1))
                    new[f][z] = new[f][z] - (high - low[f])
                    edge = jnp.where(lower, low[f], high)
                    held = edges[side][2 * f + half]
                    edges[side][2 * f + half] = edge if held is None else held + edge
    return new


def pack_results(u, edges, weights, held, packed):
    thick = [u[i // 2][2 * (i % 2)] + u[i // 2][2 * (i % 2) + 1] for i in range(IMAGES)]

    def pairs(values, i):
        rows = [jnp.concatenate(values[2 * p : 2 * p + 2], axis=1) for p in range(5)]
        sums = select_dot(rows, weights[i])
        return [sums[8 * p : 8 * p + 8] for p in range(5)]

    inner, cols, rows = pairs(thick, 0), pairs(edges[1], 1), pairs(edges[0], 2)
    lane = iota((BOXES, LANES), 1)
    first_cols = cols[0]
    for p in range(1, 4):
        first_cols = jnp.where(lane % 16 // 4 == p, roll(cols[p], 4 * p, 1), first_cols)
    for i in range(8):
        message = roll(cols[4], 120 - 16 * i, 1)
        message = jnp.where(lane < 120, roll(first_cols, 104 - 16 * i, 1), message)
        if i < 4:
            start = 16 * (i % 2) + 8 * (i // 2)
            message = jnp.where(lane < 104, roll(rows[4], 96 - start, 1), message)
        message = jnp.where(lane < 96, roll(rows[i // 2], 80 - 16 * (i % 2), 1), message)
        for p in range(4, -1, -1):
            part = roll(inner[p], 16 * (p - i), 1)
            message = jnp.where(lane < 16 * p + 16, part, message)
        held[pl.ds(i, BOXES, stride=8), :] = message
    for r in range(BOXES):
        packed[r] = held[pl.ds(8 * r, 8), :]


def far_first(n):
    side = round(n**0.5)
    steps = [(a, b) for a in range(side) for b in range(side) if a or b]
    return side, sorted(steps, key=lambda s: -sum(min(x, side - x) for x in s))


def partners(n, me):
    side, steps = far_first(n)
    high, low = me // side, lax.rem(me, side)
    for a, b in steps:
        yield lax.rem(high + a, side) * side + lax.rem(low + b, side)


def send(me, other, source, target, sems):
    pltpu.make_async_remote_copy(
        src_ref=source.at[other],
        dst_ref=target.at[me],
        send_sem=sems.at[0],
        recv_sem=sems.at[1],
        device_id={"gx": other},
        device_id_type=MESH,
    ).start()


def all_slots(n, me, source, target, sems):
    return pltpu.make_async_remote_copy(
        src_ref=source.at[pl.ds(0, n - 1)],
        dst_ref=target.at[pl.ds(0, n - 1)],
        send_sem=sems.at[0],
        recv_sem=sems.at[1],
        device_id={"gx": me},
        device_id_type=MESH,
    )


def level_kernel(
    n,
    m,
    coarse,
    fine_in,
    sources_in,
    tiles_in,
    coarse_new,
    rows_x_out,
    flux_y_out,
    returned,
    fine_out,
    wanted_out,
    sources,
    tiles,
    wanted,
    box_of,
    img,
    flux_x,
    flux_y,
    rows_x,
    fine,
    turned,
    table_x,
    table_y,
    by_tile,
    rims,
    rims_in,
    held,
    packed,
    results,
    cells,
    halo_rows,
    halo_cols,
    from_rows,
    from_cols,
    spread,
    gather,
    load_sems,
    store_sems,
    rim_sems,
    result_sems,
    halo_sems,
):
    me, column = lax.axis_index("gx"), lax.axis_index("gy")
    up, down = lax.rem(me + 1, n), lax.rem(me + n - 1, n)
    right, left = lax.rem(column + 1, m), lax.rem(column + m - 1, m)
    barrier = pltpu.get_barrier_semaphore()

    for other in partners(n, me):
        pl.semaphore_signal(barrier, 1, device_id={"gx": other}, device_id_type=MESH)
    pl.semaphore_signal(barrier, 1, device_id={"gy": right}, device_id_type=MESH)
    pl.semaphore_signal(barrier, 1, device_id={"gy": left}, device_id_type=MESH)

    old, new = pl.ds(0, IMAGES * ROWS), pl.ds(IMAGES * ROWS, IMAGES * ROWS)
    load = pltpu.make_async_copy(coarse, img.at[old], load_sems.at[0])
    load_fine = pltpu.make_async_copy(fine_in, fine, load_sems.at[1])
    load_sources = pltpu.make_async_copy(sources_in, sources, load_sems.at[2])
    load_tiles = pltpu.make_async_copy(tiles_in, tiles, load_sems.at[3])
    load.start()
    load_sources.start()
    load_tiles.start()
    load_fine.start()
    load.wait()
    coarse_step(img, flux_x, flux_y)
    for image in range(IMAGES):
        for i in range(2):
            rows = flux_x[pl.ds(image * ROWS + 7 * i, 8, stride=8), :]
            rows_x[image, pl.ds(8 * i, 8), :] = rows
    stores = [
        pltpu.make_async_copy(rows_x, rows_x_out, store_sems.at[0]),
        pltpu.make_async_copy(flux_y, flux_y_out, store_sems.at[1]),
    ]
    stores[0].start()
    stores[1].start()
    table_x[...] = jnp.zeros_like(table_x)
    table_y[...] = jnp.zeros_like(table_y)
    build_tables(img, turned, table_x, table_y)
    load_sources.wait()
    load_tiles.wait()
    pack_rims(n, me, sources, tiles, table_x, table_y, by_tile, rims, wanted, box_of)
    rims_in[me] = rims[me]
    stores.append(pltpu.make_async_copy(wanted, wanted_out, store_sems.at[2]))
    stores[2].start()
    pl.semaphore_wait(barrier, n + 1)

    for other in partners(n, me):
        send(me, other, rims, rims_in, rim_sems)
    pack_halo(img, halo_rows, halo_cols)
    halos = []
    for i, (source, target, where) in enumerate(
        (
            (halo_rows, from_rows.at[0], {"gx": up}),
            (halo_rows, from_rows.at[1], {"gx": down}),
            (halo_cols, from_cols.at[0], {"gy": right}),
            (halo_cols, from_cols.at[1], {"gy": left}),
        )
    ):
        copy = pltpu.make_async_remote_copy(
            src_ref=source,
            dst_ref=target,
            send_sem=halo_sems.at[0, i],
            recv_sem=halo_sems.at[1, i],
            device_id=where,
            device_id_type=MESH,
        )
        copy.start()
        halos.append(copy)
    load_fine.wait()
    for r in range(BOXES):
        for f in range(5):
            for z in range(4):
                cells[4 * f + z, pl.ds(r, 1), :] = fine[r, f, pl.ds(z, 1), :]
    spread_weights(spread)
    gather_weights(gather)

    rim_copies = all_slots(n, me, rims, rims_in, rim_sems)
    rim_copies.wait_recv()
    ghosts = own_rims(me, sources, rims_in, held, spread)
    u = [[cells[4 * f + z] for z in range(4)] for f in range(5)]
    edges = [[None] * IMAGES, [None] * IMAGES]
    u = fine_step(u, ghosts[0][0], ghosts[1][0], edges)
    u = fine_step(u, ghosts[0][1], ghosts[1][1], edges)
    pack_results(u, edges, gather, held, packed)
    for other in partners(n, me):
        results[other] = packed[box_of[other]]
        send(me, other, results, returned, result_sems)
    results[me] = packed[box_of[me]]
    stores.append(pltpu.make_async_copy(results.at[me], returned.at[me], store_sems.at[3]))
    stores[3].start()
    for f in range(5):
        for z in range(4):
            for r in range(BOXES):
                fine[r, f, pl.ds(z, 1), :] = u[f][z][r : r + 1]
    stores.append(pltpu.make_async_copy(fine, fine_out, store_sems.at[4]))
    stores[4].start()
    for copy in halos:
        copy.wait_recv()
    finish_edges(img, halo_rows, halo_cols, from_rows, from_cols)
    stores.append(pltpu.make_async_copy(img.at[new], coarse_new, store_sems.at[5]))
    stores[5].start()
    rim_copies.wait_send()
    for copy in halos:
        copy.wait_send()
    for copy in stores:
        copy.wait()
    result_copies = all_slots(n, me, results, returned, result_sems)
    result_copies.wait_send()
    result_copies.wait_recv()


def merge_kernel(
    n,
    new_in,
    rows_x_in,
    flux_y_in,
    returned_in,
    wanted_in,
    fine_in,
    out_to,
    fine_out,
    new,
    rows_x,
    flux_y,
    returned,
    wanted,
    out,
    slots,
    covered_in,
    turned,
    fine,
    sems,
    out_sem,
    fine_sem,
):
    pairs = (
        (wanted_in, wanted),
        (returned_in, returned),
        (new_in, new),
        (rows_x_in, rows_x),
        (flux_y_in, flux_y),
        (fine_in, fine),
    )
    loads = [pltpu.make_async_copy(a, b, sems.at[i]) for i, (a, b) in enumerate(pairs)]
    for copy in loads:
        copy.start()
    lane, sub = iota((8, LANES), 1), iota((8, LANES), 0)

    def clear(t, carry):
        slots[t] = -1
        return carry

    def place(o, carry):
        slots[wanted[o]] = o
        return carry

    lax.fori_loop(0, 128, clear, 0, unroll=8)
    loads[0].wait()
    lax.fori_loop(0, n, place, 0, unroll=8)
    blank = jnp.zeros((8, LANES), jnp.float32)
    group = lane // 8
    for tx in (0, 7):
        covered_in[tx] = blank
        for i in range(16):
            turned[tx, i] = blank

    def row_of_tiles(tx, carry):
        covered = blank
        diagonals = [blank] * 16
        for ty in range(1, 15):
            slot = slots[16 * tx + ty]
            live = (slot >= 0).astype(jnp.int32)
            message = returned[jnp.maximum(slot, 0)]
            covered = jnp.where(lane // 8 == jnp.where(live > 0, ty, -1), 1.0, covered)
            for d in range(16):
                i = (ty - d) % 16
                diagonals[d] = jnp.where(group == i, message, diagonals[d])
        diagonals = [roll(diagonals[d], 8 * d, 1) for d in range(16)]
        covered_in[tx] = covered
        for i in range(16):
            part = diagonals[(1 - i) % 16]
            for ty in range(2, 15):
                part = jnp.where(group == ty, diagonals[(ty - i) % 16], part)
            turned[tx, i] = part
        return carry

    loads[1].wait()
    lax.fori_loop(1, 7, row_of_tiles, 0, unroll=6)
    loads[5].wait()
    store_fine = pltpu.make_async_copy(fine, fine_out, fine_sem)
    store_fine.start()
    for copy in loads[2:5]:
        copy.wait()

    def finish(tx, carry):
        above, below = jnp.minimum(tx + 1, 7), jnp.maximum(tx - 1, 0)
        cover = covered_in[tx]
        covered = cover > 0.5
        last = lane % 8 == 7
        touched = last & (roll(cover, -1, 1) > 0.5) | (lane % 8 == 0) & (roll(cover, 1, 1) > 0.5)
        beside = (sub == 7) & (covered_in[above] > 0.5) | (sub == 0) & (covered_in[below] > 0.5)
        rows = pl.ds(pl.multiple_of(8 * tx, 8), 8)
        low, high = [turned[above, 10 + g] for g in range(3)], [turned[below, 10 + g] for g in range(3)]
        cols = [turned[tx, 13 + g] for g in range(3)]
        for image in range(IMAGES):
            if image < 8:
                lows, highs = low[0][image : image + 1], high[1][image : image + 1]
            else:
                lows, highs = low[2][image - 8 : image - 7], high[2][image - 6 : image - 5]
            place = 2 * (image % 4)
            value = cols[image // 4]
            value = jnp.where(last, roll(value, -1 - place, 1), roll(value, 7 - place, 1))
            cells = new[image, rows, :] + jnp.where(touched, value - flux_y[image, rows, :], 0.0)
            lows = lows - rows_x[image, pl.ds(8 + tx, 1), :]
            highs = highs - rows_x[image, pl.ds(tx, 1), :]
            cells = cells + jnp.where(beside, jnp.where(sub == 7, lows, highs), 0.0)
            out[image, rows, :] = jnp.where(covered, turned[tx, image], cells)
        pltpu.make_async_copy(out.at[:, rows], out_to.at[:, rows], out_sem).start()
        return carry

    lax.fori_loop(0, 8, finish, 0, unroll=8)
    pltpu.make_async_copy(out, out_to, out_sem).wait()
    store_fine.wait()


def body(n, m, coarse_state, fine_state, source_rows, tile_ids):
    hbm = pl.BlockSpec(memory_space=pltpu.HBM)
    f32 = jnp.float32
    coarse = coarse_state.reshape(IMAGES * ROWS, LANES)
    fine = fine_state.reshape(BOXES, 5, 4, 256)
    sources = source_rows.reshape(n, BOXES).T
    tiles = tile_ids.reshape(n, BOXES).T
    shape = jax.ShapeDtypeStruct
    image = shape((IMAGES * ROWS, LANES), f32)
    boxes = shape((BOXES, 5, 4, 256), f32)
    new, rows_x, flux_y, returned, fine_out, wanted = pl.pallas_call(
        functools.partial(level_kernel, n, m),
        out_shape=(
            image,
            shape((IMAGES, 16, LANES), f32),
            image,
            shape((n, 8, LANES), f32),
            boxes,
            shape((n,), jnp.int32),
        ),
        in_specs=[hbm] * 4,
        out_specs=(hbm,) * 6,
        scratch_shapes=[
            pltpu.SMEM((BOXES, n), jnp.int32),
            pltpu.SMEM((BOXES, n), jnp.int32),
            pltpu.SMEM((n,), jnp.int32),
            pltpu.SMEM((n,), jnp.int32),
            pltpu.VMEM((2 * IMAGES * ROWS, LANES), f32),
            pltpu.VMEM((IMAGES * ROWS, LANES), f32),
            pltpu.VMEM((IMAGES * ROWS, LANES), f32),
            pltpu.VMEM((IMAGES, 16, LANES), f32),
            pltpu.VMEM((BOXES, 5, 4, 256), f32),
            pltpu.VMEM((IMAGES * LANES, LANES), f32),
            pltpu.VMEM((8, 8, 8, LANES), f32),
            pltpu.VMEM((16, 4, 8, LANES), f32),
            pltpu.VMEM((128, 5, LANES), f32),
            pltpu.VMEM((n, 5, LANES), f32),
            pltpu.VMEM((n, 5, LANES), f32),
            pltpu.VMEM((8 * BOXES, LANES), f32),
            pltpu.VMEM((BOXES, 8, LANES), f32),
            pltpu.VMEM((n, 8, LANES), f32),
            pltpu.VMEM((20, BOXES, 256), f32),
            pltpu.VMEM((32, LANES), f32),
            pltpu.VMEM((ROWS, LANES), f32),
            pltpu.VMEM((2, 32, LANES), f32),
            pltpu.VMEM((2, ROWS, LANES), f32),
            pltpu.VMEM((2, LANES, 256), jnp.bfloat16),
            pltpu.VMEM((3, 512, LANES), jnp.bfloat16),
            pltpu.SemaphoreType.DMA((4,)),
            pltpu.SemaphoreType.DMA((6,)),
            pltpu.SemaphoreType.DMA((2,)),
            pltpu.SemaphoreType.DMA((2,)),
            pltpu.SemaphoreType.DMA((2, 4)),
        ],
        compiler_params=pltpu.CompilerParams(
            collective_id=0, has_side_effects=True, vmem_limit_bytes=VMEM_LIMIT
        ),
        name="levels",
    )(coarse, fine, sources, tiles)
    stack = shape((IMAGES, ROWS, LANES), f32)
    field = pltpu.VMEM((IMAGES, ROWS, LANES), f32)
    out, fine_out = pl.pallas_call(
        functools.partial(merge_kernel, n),
        out_shape=(stack, boxes),
        in_specs=[hbm] * 6,
        out_specs=(hbm,) * 2,
        scratch_shapes=[
            field,
            pltpu.VMEM((IMAGES, 16, LANES), f32),
            field,
            pltpu.VMEM((n, 8, LANES), f32),
            pltpu.SMEM((n,), jnp.int32),
            field,
            pltpu.SMEM((128,), jnp.int32),
            pltpu.VMEM((8, 8, LANES), f32),
            pltpu.VMEM((8, 16, 8, LANES), f32),
            pltpu.VMEM((BOXES, 5, 4, 256), f32),
            pltpu.SemaphoreType.DMA((6,)),
            pltpu.SemaphoreType.DMA,
            pltpu.SemaphoreType.DMA,
        ],
        compiler_params=pltpu.CompilerParams(vmem_limit_bytes=VMEM_LIMIT),
        name="merge",
    )(
        new.reshape(stack.shape),
        rows_x,
        flux_y.reshape(stack.shape),
        returned,
        wanted,
        fine_out,
    )
    return out.reshape(coarse_state.shape), fine_out.reshape(fine_state.shape)


def solution(mesh):
    return jax.shard_map(
        functools.partial(body, mesh.shape["gx"], mesh.shape["gy"]),
        mesh=mesh,
        in_specs=(
            P(None, None, "gx", "gy"),
            P("gx", "gy", None, None, None, None),
            P(None, "gy", None),
            P(None, "gy", None),
        ),
        out_specs=(P(None, None, "gx", "gy"), P("gx", "gy", None, None, None, None)),
        check_vma=False,
    )
```
